32 devices in a mesh: dp: 8 (over y, x, core), tensor: 4 (over z).
Axes of the slice: x: 2, y: 2, z: 4, core: 2. Of those that a mesh axis runs over, the one named last changes fastest.
Arguments:
- tokens: bfloat16 [8, 1024, 2048], P('dp', 'tensor'), may hold values from -6 to 6
- cotangent: bfloat16 [8, 1024, 2048], P('dp', 'tensor'), may hold values from -6 to 6
- adapter_ids: int32 [8, 1], P('dp'), may hold values from 0 to 7
- segments: int32 [8, 1024], P('dp'), may hold values from 0 to 5, never falling along the last dimension, each value on 1 to 800 neighbouring positions
- norm_attn: float32 [2048], replicated, may hold values from 0.1 to 1.9
- norm_mlp: float32 [2048], replicated, may hold values from 0.1 to 1.9
- weight_query: bfloat16 [2048, 2048], P('dp', 'tensor'), may hold values from -0.125 to 0.125
- weight_key: bfloat16 [2048, 2048], P('dp', 'tensor'), may hold values from -0.125 to 0.125
- weight_value: bfloat16 [2048, 4096], P('dp', 'tensor'), may hold values from -0.125 to 0.125
- weight_gate: bfloat16 [2048, 4096], P('dp', 'tensor'), may hold values from -0.125 to 0.125
- weight_out: bfloat16 [4096, 2048], P('tensor', 'dp'), may hold values from -0.1875 to 0.1875
- weight_mlp_gate: bfloat16 [2048, 4096], P('dp', 'tensor'), may hold values from -0.125 to 0.125
- weight_mlp_up: bfloat16 [2048, 4096], P('dp', 'tensor'), may hold values from -0.125 to 0.125
- weight_mlp_down: bfloat16 [4096, 2048], P('tensor', 'dp'), may hold values from -0.1875 to 0.1875
- adapt_attn_in: bfloat16 [8, 2048, 64], replicated, may hold values from -0.125 to 0.125
- adapt_query_key: bfloat16 [8, 2, 16, 2048], P(None, None, None, 'tensor'), may hold values from -1.5 to 1.5
- adapt_value_gate: bfloat16 [8, 2, 16, 4096], P(None, None, None, 'tensor'), may hold values from -1.5 to 1.5
- adapt_out_in: bfloat16 [8, 4096, 16], P(None, 'tensor'), may hold values from -0.09375 to 0.09375
- adapt_out_back: bfloat16 [8, 16, 2048], replicated, may hold values from -1.5 to 1.5
- adapt_mlp_in: bfloat16 [8, 2048, 32], replicated, may hold values from -0.125 to 0.125
- adapt_mlp_hidden: bfloat16 [8, 2, 16, 4096], P(None, None, None, 'tensor'), may hold values from -1.5 to 1.5
- adapt_down_in: bfloat16 [8, 4096, 16], P(None, 'tensor'), may hold values from -0.09375 to 0.09375
- adapt_down_back: bfloat16 [8, 16, 2048], replicated, may hold values from -1.5 to 1.5
Outputs:
- output: bfloat16 [8, 1024, 2048], P('dp', 'tensor')
- input_grad: float32 [8, 1024, 2048], P('dp', 'tensor')
- grad_attn_in: float32 [8, 2048, 64], replicated
- grad_query_key: float32 [8, 2, 16, 2048], P(None, None, None, 'tensor')
- grad_value_gate: float32 [8, 2, 16, 4096], P(None, None, None, 'tensor')
- grad_out_in: float32 [8, 4096, 16], P(None, 'tensor')
- grad_out_back: float32 [8, 16, 2048], replicated
- grad_mlp_in: float32 [8, 2048, 32], replicated
- grad_mlp_hidden: float32 [8, 2, 16, 4096], P(None, None, None, 'tensor')
- grad_down_in: float32 [8, 4096, 16], P(None, 'tensor')
- grad_down_back: float32 [8, 16, 2048], replicated
The draws below stay inside these ranges and needn't reach their ends.
Inputs may be any that keep to these rules, and one draw needn't show every extreme that they name: `adapter_ids`: every one of the 8 adapters is chosen by at least one sequence. `segments`: along a sequence the document numbers never fall; a document has at most 800 tokens, and some document has exactly 800.
All inputs are finite; a program needn't handle non-finite values.
Results may differ from the reference program's by a relative error of at most 0.023.
Values may be sent and summed in bfloat16 or wider, within the bound.
No kernel may reach another device: no remote copies, remote signals or barrier semaphores. Data moves between devices by JAX's collectives and lax.ppermute only.
A program may use at most 192 MiB of HBM per device.

```python
import math
import jax
import jax.numpy as jnp
import numpy as np
from jax import lax

D = 2048
HEADS = 8
KEY_DIM = 256
VALUE_DIM = 512
FF = 4096
RANK = 16
ADAPTERS = 8
SEQ_LEN = 1024
ROW_BLOCK = 512
DOCS = 6
DOC_MOST = 800
SEQS = 8
HK = 2048
HV = 4096


def block_levels(key, dims, shards, low, top_value):
    gain, own = 1.0, jax.random.fold_in(key, 6)
    for axis_at, shards_of in shards:
        heights = jnp.exp(jax.random.uniform(jax.random.fold_in(own, axis_at), (shards_of,), jnp.float32, low / len(shards), top_value / len(shards)))
        gain = gain * jnp.repeat(heights, dims[axis_at] // shards_of).reshape([-1 if axis == axis_at else 1 for axis in range(len(dims))])
    return gain


def different_ones(own_key, rows, count, top, lift):
    sequence = jax.random.permutation(jax.random.fold_in(own_key, 1), count)
    pull = sequence
    for power in range(3):
        pull = pull * pull // count
    pull = pull * lift // count
    lots = jax.random.randint(jax.random.fold_in(own_key, 2), (rows, count), 0, 4096) + pull
    holders = jax.random.permutation(jax.random.fold_in(own_key, 3), rows)[jnp.arange(count) % rows]
    lots = jnp.where(jnp.arange(rows)[:, None] == holders[None, :], 1 << 14, lots)
    priority = lots * count + jnp.arange(count)
    return lax.top_k(priority.astype(jnp.int32), top)[1].astype(jnp.int32)


def length_profile(count, total, bound, lean):
    loads = [(1 << 20) // math.isqrt(grade ** lean) + 1 for grade in range(2, count + 1)]
    rest, given = total - bound - (count - 1), [1] * (count - 1)
    while rest > 0:
        free = [i for i in range(count - 1) if given[i] < bound]
        pool, left = sum([loads[i] for i in free]), rest
        for i in free:
            extra = min(bound - given[i], max(1, left * loads[i] // pool), rest)
            given[i] = given[i] + extra
            rest = rest - extra
    return np.array([bound] + given)


def uneven_parts(rng, amount, total, bound, slope):
    if amount == 2:
        one = jax.random.randint(rng, (), max(1, total - bound), min(bound, total - 1) + 1)
        return jnp.stack([one, total - one])
    sizes = jnp.asarray(length_profile(amount, total, bound, slope), jnp.int32)
    pairs = (amount - 1) // 2
    source_of, sink = sizes[1:1 + 2 * pairs:2], sizes[2:2 + 2 * pairs:2]
    room = jnp.minimum(source_of - 1, bound - sink)
    shifted = jax.random.randint(jax.random.fold_in(rng, 1), (pairs,), 0, 1 << 20) % (room + 1)
    sizes = sizes.at[1:1 + 2 * pairs:2].set(source_of - shifted).at[2:2 + 2 * pairs:2].set(sink + shifted)
    return sizes[jax.random.permutation(jax.random.fold_in(rng, 2), amount)]


def centred(own_key, dims, spread, most, pieces=(), kind=jnp.bfloat16):
    drawn = jax.random.normal(own_key, dims, jnp.float32) * spread
    if len(pieces) > 0:
        drawn = block_levels(own_key, dims, pieces, -0.22, 0.18) * drawn
    return jnp.clip(drawn, min=-most, max=most).astype(kind)


def setup_inputs(seed: int = 0) -> dict:
    streams_of = jax.random.split(jax.random.key(seed), 24)
    tokens = centred(streams_of[0], (SEQS, SEQ_LEN, D), 1.0, 6.0, ((0, 8), (1, 4)))
    cotangent = centred(streams_of[1], (SEQS, SEQ_LEN, D), 1.0, 6.0, ((0, 8), (1, 4)))
    adapter_ids = different_ones(streams_of[2], SEQS, ADAPTERS, 1, 0)
    segments = jax.vmap(lambda own: jnp.searchsorted(jnp.cumsum(uneven_parts(own, DOCS, SEQ_LEN, DOC_MOST, 0)), jnp.arange(SEQ_LEN), side="right"))(jax.random.split(streams_of[3], SEQS)).reshape((SEQS, SEQ_LEN)).astype(jnp.int32)
    norm_attn = jnp.clip(1.0 + 0.18 * jax.random.normal(streams_of[4], (D,), jnp.float32), 0.1, 1.9)
    norm_mlp = jnp.clip(1.0 + 0.18 * jax.random.normal(streams_of[5], (D,), jnp.float32), 0.1, 1.9)
    weight_query = centred(streams_of[6], (D, HK), D ** -0.5, 0.125, ((0, 8), (1, 4)))
    weight_key = centred(streams_of[7], (D, HK), D ** -0.5, 0.125, ((0, 8), (1, 4)))
    weight_value = centred(streams_of[8], (D, HV), D ** -0.5, 0.125, ((0, 8), (1, 4)))
    weight_gate = centred(streams_of[9], (D, HV), D ** -0.5, 0.125, ((0, 8), (1, 4)))
    weight_out = centred(streams_of[10], (HV, D), (HV // 4) ** -0.5, 0.1875, ((0, 4), (1, 8)))
    weight_mlp_gate = centred(streams_of[11], (D, FF), D ** -0.5, 0.125, ((0, 8), (1, 4)))
    weight_mlp_up = centred(streams_of[12], (D, FF), D ** -0.5, 0.125, ((0, 8), (1, 4)))
    weight_mlp_down = centred(streams_of[13], (FF, D), (FF // 4) ** -0.5, 0.1875, ((0, 4), (1, 8)))
    adapt_attn_in = centred(streams_of[14], (ADAPTERS, D, 4 * RANK), D ** -0.5, 0.125)
    adapt_query_key = centred(streams_of[15], (ADAPTERS, 2, RANK, HK), RANK ** -0.5, 1.5, ((3, 4),))
    adapt_value_gate = centred(streams_of[16], (ADAPTERS, 2, RANK, HV), RANK ** -0.5, 1.5, ((3, 4),))
    adapt_out_in = centred(streams_of[17], (ADAPTERS, HV, RANK), HV ** -0.5, 0.09375, ((1, 4),))
    adapt_out_back = centred(streams_of[18], (ADAPTERS, RANK, D), RANK ** -0.5, 1.5)
    adapt_mlp_in = centred(streams_of[19], (ADAPTERS, D, 2 * RANK), D ** -0.5, 0.125)
    adapt_mlp_hidden = centred(streams_of[20], (ADAPTERS, 2, RANK, FF), RANK ** -0.5, 1.5, ((3, 4),))
    adapt_down_in = centred(streams_of[21], (ADAPTERS, FF, RANK), FF ** -0.5, 0.09375, ((1, 4),))
    adapt_down_back = centred(streams_of[22], (ADAPTERS, RANK, D), RANK ** -0.5, 1.5)
    return {"tokens": tokens, "cotangent": cotangent, "adapter_ids": adapter_ids, "segments": segments, "norm_attn": norm_attn, "norm_mlp": norm_mlp, "weight_query": weight_query, "weight_key": weight_key, "weight_value": weight_value, "weight_gate": weight_gate, "weight_out": weight_out, "weight_mlp_gate": weight_mlp_gate, "weight_mlp_up": weight_mlp_up, "weight_mlp_down": weight_mlp_down, "adapt_attn_in": adapt_attn_in, "adapt_query_key": adapt_query_key, "adapt_value_gate": adapt_value_gate, "adapt_out_in": adapt_out_in, "adapt_out_back": adapt_out_back, "adapt_mlp_in": adapt_mlp_in, "adapt_mlp_hidden": adapt_mlp_hidden, "adapt_down_in": adapt_down_in, "adapt_down_back": adapt_down_back}


highest = lax.Precision.HIGHEST
rms_epsilon = 1e-06
group_floor = 1.0

@jax.custom_vjp
def low(v):
    return lax.optimization_barrier(v.astype(jnp.bfloat16)).astype(jnp.float32)

@jax.custom_vjp
def low_back(v):
    return v

def low_keep(v):
    return (low(v), None)

def low_pass(kept, grad):
    return (grad,)

def back_keep(v):
    return (v, None)

def back_low(kept, grad):
    return (low(grad),)
low.defvjp(low_keep, low_pass)
low_back.defvjp(back_keep, back_low)

def matmul(left_side, right_side):
    return jnp.dot(left_side, right_side, precision=highest, preferred_element_type=jnp.float32)

def rms_scale(rows_in, gain_row):
    return rows_in * lax.rsqrt(lax.optimization_barrier(jnp.mean(rows_in * rows_in, axis=-1, keepdims=True)) + rms_epsilon) * gain_row

def rotation_tables(seq_length, half_dim):
    positions = jnp.arange(seq_length, dtype=jnp.float32)
    frequency = jnp.exp(-jnp.log(10000.0) * jnp.arange(half_dim, dtype=jnp.float32) / half_dim)
    angles = positions[:, None] * frequency[None, :]
    return (jnp.cos(angles)[:, None, :], jnp.sin(angles)[:, None, :])

def rotate(values, cosine, sine_table):
    middle = values.shape[-1] // 2
    first_half = values[..., :middle]
    second = values[..., middle:]
    return jnp.concatenate([first_half * cosine - second * sine_table, second * cosine + first_half * sine_table], axis=-1)

def decay_block(head_ids, first_row, block_rows, seg_all):
    key_pos = jnp.arange(seg_all.shape[0], dtype=jnp.int32)
    query_pos = first_row.astype(jnp.int32) + jnp.arange(block_rows, dtype=jnp.int32)
    distance = query_pos[:, None] - key_pos[None, :]
    seg_query = lax.dynamic_slice_in_dim(seg_all, first_row.astype(jnp.int32), block_rows, 0)
    alive_mask = (distance >= 0) & (seg_query[:, None] == seg_all[None, :])
    decay_rate = jnp.log(1.0 - jnp.exp2(-5.0 - head_ids))
    weight_table = jnp.exp(jnp.maximum(distance, 0).astype(head_ids.dtype)[None, :, :] * decay_rate[:, None, None])
    return jnp.where(alive_mask[None, :, :], weight_table, jnp.zeros_like(weight_table))

def retention(queries, keys_all, values_all, seg_all):
    seq_length = queries.shape[0]
    head_ids = jnp.arange(queries.shape[1], dtype=jnp.float32)
    starts = jnp.arange(seq_length // ROW_BLOCK, dtype=jnp.int32) * ROW_BLOCK

    def one_block(first_row):
        query_block = lax.dynamic_slice_in_dim(queries, first_row, ROW_BLOCK, 0)
        scores = low_back(jnp.einsum('qhd,khd->hqk', query_block, keys_all, precision=highest))
        mixed_low = low(scores * decay_block(head_ids, first_row, ROW_BLOCK, seg_all))
        return jnp.einsum('hqk,khd->qhd', mixed_low, values_all, precision=highest)
    blocks = lax.map(jax.checkpoint(one_block), starts)
    return blocks.reshape(seq_length, queries.shape[1], values_all.shape[2])

def group_norm(mixed_rows):
    centered = mixed_rows - lax.optimization_barrier(jnp.mean(mixed_rows, axis=-1, keepdims=True))
    return centered * lax.rsqrt(lax.optimization_barrier(jnp.mean(centered * centered, axis=-1, keepdims=True)) + group_floor)

def reference(tokens, cotangent, adapter_ids, segments, norm_attn, norm_mlp, weight_query, weight_key, weight_value, weight_gate, weight_out, weight_mlp_gate, weight_mlp_up, weight_mlp_down, adapt_attn_in, adapt_query_key, adapt_value_gate, adapt_out_in, adapt_out_back, adapt_mlp_in, adapt_mlp_hidden, adapt_down_in, adapt_down_back):
    frozen = tuple((matrix.astype(jnp.float32) for matrix in (weight_query, weight_key, weight_value, weight_gate, weight_out, weight_mlp_gate, weight_mlp_up, weight_mlp_down)))
    tables = tuple((matrix.astype(jnp.float32) for matrix in (adapt_attn_in, adapt_query_key, adapt_value_gate, adapt_out_in, adapt_out_back, adapt_mlp_in, adapt_mlp_hidden, adapt_down_in, adapt_down_back)))
    cosine, sine_table = rotation_tables(SEQ_LEN, KEY_DIM // 2)
    key_scale = 1.0 / KEY_DIM ** 0.5

    def one_sequence(totals, inputs):
        tokens_seq, cotangent_seq, chosen, seg_all = inputs
        selector = (jnp.arange(ADAPTERS, dtype=jnp.int32) == chosen[0]).astype(jnp.float32)

        def forward(rows_in, adapters):
            attn_in, query_key, value_gate, out_in, out_back, mlp_in, mlp_hidden, down_in, down_back = [jnp.tensordot(selector, adapter_table, axes=1, precision=highest) for adapter_table in adapters]
            attn_rows = low(rms_scale(rows_in, norm_attn))
            attn_low = low(matmul(attn_rows, attn_in))
            proj_query = matmul(attn_rows, frozen[0]) + matmul(attn_low[:, :RANK], query_key[0])
            proj_key = matmul(attn_rows, frozen[1]) + matmul(attn_low[:, RANK:2 * RANK], query_key[1])
            proj_value = matmul(attn_rows, frozen[2]) + matmul(attn_low[:, 2 * RANK:3 * RANK], value_gate[0])
            proj_gate = low_back(matmul(attn_rows, frozen[3]) + matmul(attn_low[:, 3 * RANK:], value_gate[1]))
            queries = low(rotate(low_back(proj_query).reshape(SEQ_LEN, HEADS, KEY_DIM), cosine, sine_table))
            keys_all = low(key_scale * rotate(low_back(proj_key).reshape(SEQ_LEN, HEADS, KEY_DIM), cosine, sine_table))
            values_all = low(low_back(proj_value)).reshape(SEQ_LEN, HEADS, VALUE_DIM)
            retained = low_back(retention(queries, keys_all, values_all, seg_all))
            gated_low = low(jax.nn.silu(proj_gate) * group_norm(retained).reshape(SEQ_LEN, HEADS * VALUE_DIM))
            out_low = low_back(matmul(gated_low, out_in))
            attn_branch = low_back(matmul(gated_low, frozen[4]) + matmul(out_low, out_back))
            middle_rows = rows_in + attn_branch
            mlp_rows = low(rms_scale(middle_rows, norm_mlp))
            mlp_low = low(matmul(mlp_rows, mlp_in))
            proj_mlp_gate = low_back(matmul(mlp_rows, frozen[5]) + matmul(mlp_low[:, :RANK], mlp_hidden[0]))
            proj_mlp_up = low_back(matmul(mlp_rows, frozen[6]) + matmul(mlp_low[:, RANK:], mlp_hidden[1]))
            hidden = low(jax.nn.gelu(proj_mlp_gate, approximate=False) * proj_mlp_up)
            down_low = low_back(matmul(hidden, down_in))
            mlp_branch = low_back(matmul(hidden, frozen[7]) + matmul(down_low, down_back))
            return middle_rows + mlp_branch
        result, pullback = jax.vjp(forward, tokens_seq.astype(jnp.float32), tables)
        input_grad, table_grads = pullback(cotangent_seq.astype(jnp.float32))
        totals = jax.tree.map(jnp.add, totals, tuple(table_grads))
        return (totals, (result.astype(jnp.bfloat16), input_grad))
    zeros = tuple((jnp.zeros(adapter_table.shape, jnp.float32) for adapter_table in tables))
    totals, (output, input_grad) = lax.scan(one_sequence, zeros, (tokens, cotangent, adapter_ids, segments))
    return (output, input_grad, totals[0], totals[1], totals[2], totals[3], totals[4], totals[5], totals[6], totals[7], totals[8])
```

```python
from functools import partial

import jax
import jax.numpy as jnp
from jax import lax
from jax.experimental import pallas as pl
from jax.experimental.pallas import tpu as pltpu
from jax.sharding import PartitionSpec as P

KEY_DIM = 256
VALUE_DIM = 512
RANK = 16
HALF = KEY_DIM // 2

rms_epsilon = 1e-06
group_floor = 1.0
BF = jnp.bfloat16
F32 = jnp.float32


def dot(a, b):
    return jnp.dot(a, b, preferred_element_type=F32)


def dot_nt(a, b):
    return lax.dot_general(a, b, (((1,), (1,)), ((), ())), preferred_element_type=F32)


def dot_tn(a, b):
    return lax.dot_general(a, b, (((0,), (0,)), ((), ())), preferred_element_type=F32)


def aligned(start, size):
    return pl.ds(pl.multiple_of(start, size), size)


def params(mib):
    return pltpu.CompilerParams(
        vmem_limit_bytes=mib << 20, dimension_semantics=("arbitrary",)
    )


def estimate(flops, moved):
    return pl.CostEstimate(flops=1, bytes_accessed=1, transcendentals=0)


def full(shape):
    return pl.BlockSpec(shape, lambda *_: (0,) * len(shape))


def in_hbm(*arrays):
    return [pltpu.with_memory_space_constraint(array, pltpu.HBM) for array in arrays]


def smem():
    return pl.BlockSpec(memory_space=pltpu.SMEM)


def columns(refs, ids):
    count = ids.shape[0]
    width = refs[0].shape[1] // count
    if count == 1:
        return all_rows(refs)
    return jnp.concatenate(
        [
            jnp.concatenate([ref[:, aligned(ids[i] * width, width)] for i in range(count)], axis=1)
            for ref in refs
        ],
        axis=0,
    )


def all_rows(refs):
    return refs[0][...] if len(refs) == 1 else jnp.concatenate([ref[...] for ref in refs], axis=0)


def low_rows(low_in, refs):
    return jnp.concatenate([dot_nt(low_in, ref[...]) for ref in refs], axis=1)


def whole(arrays):
    return [full(array.shape) for array in arrays]


def row_count(arrays):
    return sum(array.shape[0] for array in arrays)


def stacked(refs):
    return jnp.concatenate([w[s] for w in refs for s in range(w.shape[0])], axis=0)


def rotated(values, cosine, sine_table):
    first = values[:, :HALF]
    second = values[:, HALF:]
    return jnp.concatenate(
        [first * cosine - second * sine_table, second * cosine + first * sine_table], axis=1
    )


def unrotated(values, cosine, sine_table):
    first = values[:, :HALF]
    second = values[:, HALF:]
    return jnp.concatenate(
        [first * cosine + second * sine_table, second * cosine - first * sine_table], axis=1
    )


def norm_kernel(x, gain, out):
    rows = x[...].astype(F32)
    inverse = lax.rsqrt(jnp.mean(rows * rows, axis=1, keepdims=True) + rms_epsilon)
    out[...] = (rows * inverse * gain[...]).astype(BF)


def norm_rows(x, gain):
    return pl.pallas_call(
        norm_kernel,
        out_shape=jax.ShapeDtypeStruct(x.shape, BF),
        compiler_params=pltpu.CompilerParams(vmem_limit_bytes=24 << 20),
        name="norm_rows",
    )(x, gain)


def query_key_kernel(parts, ids, chunks, low_in, low_out, cosine, sine_table, *refs):
    act, pieces, (out, low) = refs[:parts], refs[parts:-2], refs[-2:]
    n = pl.program_id(0)

    @pl.when(n == 0)
    def _():
        low[...] = low_rows(low_in[...], act).astype(BF)

    product = dot(columns(act, ids), stacked(pieces)) + dot_tn(low[...], low_out[...])
    scale = jnp.where(n >= pl.num_programs(0) // 2, 1.0 / KEY_DIM**0.5, 1.0)
    size = out.shape[0] // chunks.shape[0]
    for j in range(chunks.shape[0]):
        at = aligned(chunks[j] * size, size)
        rows = slice(j * size, (j + 1) * size)
        out[rows, :] = (scale * rotated(product[rows], cosine[at, :], sine_table[at, :])).astype(BF)


def piece_specs(pieces, width):
    return [
        pl.BlockSpec((w.shape[0], w.shape[1], width), lambda n: (0, 0, n)) for w in pieces
    ]


def project_query_key(ids, chunks, act, low_in, low_out, cosine, sine_table, pieces):
    rows, depth = row_count(act), act[0].shape[1]
    width = pieces[0].shape[2]
    block = KEY_DIM
    return pl.pallas_call(
        partial(query_key_kernel, len(act)),
        grid=(width // block,),
        in_specs=[smem(), smem(), full(low_in.shape),
                  pl.BlockSpec((low_out.shape[0], block), lambda n: (0, n)),
                  full(cosine.shape), full(cosine.shape)] + whole(act)
        + piece_specs(pieces, block),
        out_specs=[pl.BlockSpec((rows, block), lambda n: (0, n)),
                   full((low_in.shape[0], rows))],
        out_shape=[jax.ShapeDtypeStruct((rows, width), BF),
                   jax.ShapeDtypeStruct((low_in.shape[0], rows), BF)],
        compiler_params=params(40),
        cost_estimate=estimate(2 * rows * depth * width, 2 * depth * width + 8 * rows * depth),
        name="project_query_key",
    )(ids, chunks, low_in, low_out, cosine, sine_table, *act, *pieces)


def project_kernel(parts, ids, low, low_out, *refs):
    act, pieces, out = refs[:parts], refs[parts:-1], refs[-1]
    product = dot(columns(act, ids), stacked(pieces)) + dot_tn(low[...], low_out[...])
    out[...] = product.astype(out.dtype)


def project(ids, act, low, low_out, pieces, kind):
    rows, depth = row_count(act), act[0].shape[1]
    width = pieces[0].shape[2]
    block = 256
    return pl.pallas_call(
        partial(project_kernel, len(act)),
        grid=(width // block,),
        in_specs=[smem(), full(low.shape),
                  pl.BlockSpec((low_out.shape[0], block), lambda n: (0, n))]
        + whole(act) + piece_specs(pieces, block),
        out_specs=pl.BlockSpec((rows, block), lambda n: (0, n)),
        out_shape=jax.ShapeDtypeStruct((rows, width), kind),
        compiler_params=params(40),
        cost_estimate=estimate(2 * rows * depth * width, 2 * depth * width + 8 * rows * depth),
        name="project",
    )(ids, low, low_out, *act, *pieces)


def decay_factors(rate, size):
    down = lax.broadcasted_iota(jnp.int32, (size, 1), 0).astype(F32)
    across = lax.broadcasted_iota(jnp.int32, (1, size), 1).astype(F32)
    return down, across


def retention_kernel(spots, rates, seg_col, seg_row, q, k, v, gate, out, nrm, inverse):
    rate = rates[pl.program_id(0)]
    count = spots.shape[0]
    size = q.shape[0] // count
    down, across = decay_factors(rate, size)
    row_factor = jnp.exp(rate * down)
    for i in range(count):
        here = aligned(spots[i] * size, size)
        query = q[here, :]
        seg_here = seg_col[i * size:(i + 1) * size, :]
        total = jnp.zeros((size, v.shape[1]), F32)
        for j in range(i + 1):
            there = aligned(spots[j] * size, size)
            column_factor = jnp.exp(rate * ((i - j) * size - across))
            alive = seg_here == seg_row[:, j * size:(j + 1) * size]
            if i == j:
                alive = alive & (down >= across)
            scores = dot_nt(query, k[there, :])
            mixed = jnp.where(alive, scores * row_factor * column_factor, 0.0).astype(BF)
            total = total + dot(mixed, v[there, :])
        centered = total - jnp.mean(total, axis=1, keepdims=True)
        scale = lax.rsqrt(jnp.mean(centered * centered, axis=1, keepdims=True) + group_floor)
        normed = centered * scale
        level = gate[here, :]
        out[here, :] = (level / (1.0 + jnp.exp(-level)) * normed).astype(BF)
        nrm[here, :] = normed.astype(nrm.dtype)
        inverse[0, here, :] = jnp.broadcast_to(scale, (size, 128))


def retention(spots, rates, seg_col, seg_row, qk, v, gate):
    rows = qk.shape[0]
    heads = v.shape[1] // VALUE_DIM
    return pl.pallas_call(
        retention_kernel,
        grid=(heads,),
        in_specs=[smem(), smem(), full(seg_col.shape), full(seg_row.shape),
                  pl.BlockSpec((rows, KEY_DIM), lambda h: (0, h)),
                  pl.BlockSpec((rows, KEY_DIM), lambda h: (0, h + heads)),
                  pl.BlockSpec((rows, VALUE_DIM), lambda h: (0, h)),
                  pl.BlockSpec((rows, VALUE_DIM), lambda h: (0, h))],
        out_specs=[pl.BlockSpec((rows, VALUE_DIM), lambda h: (0, h)),
                   pl.BlockSpec((rows, VALUE_DIM), lambda h: (0, h)),
                   pl.BlockSpec((1, rows, 128), lambda h: (h, 0, 0))],
        out_shape=[jax.ShapeDtypeStruct(v.shape, BF), jax.ShapeDtypeStruct(v.shape, F32),
                   jax.ShapeDtypeStruct((heads, rows, 128), F32)],
        compiler_params=params(40),
        cost_estimate=estimate(2 * rows * rows * 768 * heads, 30 << 20),
        name="retention",
    )(spots, rates, seg_col, seg_row, qk, qk, v, gate)


def fold_kernel(ids, act, low_in, low_out, *refs):
    pieces, (outs, low) = refs[:-5], (refs[-5:-1], refs[-1])
    step = pl.program_id(0)
    subs = pl.num_programs(0)
    width = pieces[0].shape[2]
    size = outs[0].shape[0]

    @pl.when(step == 0)
    def _():
        low[...] = dot_nt(low_in[...], act[...])

    extra = low[...].astype(BF)
    rows = act[...]
    for i, piece in enumerate(pieces):
        at = aligned(ids[i * subs + step] * width, width)
        product = (dot(rows, piece[0]) + dot_tn(extra, low_out[:, at])).astype(BF)
        for j, out in enumerate(outs):
            out[:, at] = product[j * size:(j + 1) * size]


def fold(ids, act, low_in, low_out, pieces):
    rows, depth = act.shape
    subs = pieces[0].shape[0]
    width = low_out.shape[1]
    return pl.pallas_call(
        fold_kernel,
        grid=(subs,),
        in_specs=[smem(), full(act.shape), full(low_in.shape), full(low_out.shape)]
        + [pl.BlockSpec((1,) + w.shape[1:], lambda s: (s, 0, 0)) for w in pieces],
        out_specs=[full((rows // 4, width))] * 4 + [full((low_in.shape[0], rows))],
        out_shape=[jax.ShapeDtypeStruct((rows // 4, width), BF)] * 4
        + [jax.ShapeDtypeStruct((low_in.shape[0], rows), F32)],
        compiler_params=params(48),
        cost_estimate=estimate(2 * rows * depth * width, 2 * depth * width + 4 * rows * depth),
        name="fold",
    )(ids, act, low_in, low_out, *pieces)


def join_kernel(x, part0, part1, part2, gain, middle, normed):
    rows = x[...].astype(F32) + (
        part0[...].astype(F32) + part1[...].astype(F32) + part2[...].astype(F32)
    )
    inverse = lax.rsqrt(jnp.mean(rows * rows, axis=1, keepdims=True) + rms_epsilon)
    middle[...] = rows
    normed[...] = (rows * inverse * gain[...]).astype(BF)


def join_rows(x, parts, gain):
    return pl.pallas_call(
        join_kernel,
        out_shape=[jax.ShapeDtypeStruct(x.shape, F32), jax.ShapeDtypeStruct(x.shape, BF)],
        compiler_params=pltpu.CompilerParams(vmem_limit_bytes=24 << 20),
        name="join_rows",
    )(x, *parts, gain)


def rms_back_kernel(rows_in, grad_in, part0, part1, part2, gain, out, out_low):
    rows = rows_in[...].astype(F32)
    inverse = lax.rsqrt(jnp.mean(rows * rows, axis=1, keepdims=True) + rms_epsilon)
    normed = rows * inverse
    scaled = gain[...] * (
        part0[...].astype(F32) + part1[...].astype(F32) + part2[...].astype(F32)
    )
    result = grad_in[...].astype(F32) + inverse * (
        scaled - normed * jnp.mean(scaled * normed, axis=1, keepdims=True)
    )
    out[...] = result
    out_low[...] = result.astype(BF)


def rms_back(rows_in, grad_in, parts, gain, begin, count):
    width = rows_in.shape[1]
    size = 128
    block = lambda skip: pl.BlockSpec((size, width), lambda i: (i + skip // size, 0))
    skips = (begin,) * 4 + (0,)
    return pl.pallas_call(
        rms_back_kernel,
        grid=(count // size,),
        in_specs=[block(skip) for skip in skips] + [full(gain.shape)],
        out_specs=[block(0)] * 2,
        out_shape=[jax.ShapeDtypeStruct((count, width), F32),
                   jax.ShapeDtypeStruct((count, width), BF)],
        compiler_params=params(24),
        name="rms_back",
    )(rows_in, grad_in, *parts, gain)


def hidden_grad_kernel(parts, ids, low_back, low_in, *refs):
    act, pieces, (out, low) = refs[:parts], refs[parts:-2], refs[-2:]

    @pl.when(pl.program_id(0) == 0)
    def _():
        low[...] = low_rows(low_back[...], act).astype(BF)

    weights = jnp.concatenate([w[s] for w in pieces for s in range(w.shape[0])], axis=1)
    out[...] = dot_nt(columns(act, ids), weights) + dot_tn(low[...], low_in[...])


def hidden_grad(ids, act, low_back, low_in, pieces):
    rows, depth = row_count(act), act[0].shape[1]
    width = pieces[0].shape[1]
    block = 256
    return pl.pallas_call(
        partial(hidden_grad_kernel, len(act)),
        grid=(width // block,),
        in_specs=[smem(), full(low_back.shape),
                  pl.BlockSpec((low_in.shape[0], block), lambda n: (0, n))]
        + whole(act) + [pl.BlockSpec((w.shape[0], block, w.shape[2]), lambda n: (0, n, 0)) for w in pieces],
        out_specs=[pl.BlockSpec((rows, block), lambda n: (0, n)),
                   full((low_back.shape[0], rows))],
        out_shape=[jax.ShapeDtypeStruct((rows, width), F32),
                   jax.ShapeDtypeStruct((low_back.shape[0], rows), BF)],
        compiler_params=params(40),
        cost_estimate=estimate(2 * rows * depth * width, 2 * depth * width + 8 * rows * depth),
        name="hidden_grad",
    )(ids, low_back, low_in, *act, *pieces)


def mlp_kernel(parts, count, ids, low_in, gate_out, up_out, down_in, grad, grad_low, *refs):
    act, refs = refs[:parts], refs[parts:]
    gate_pieces, up_pieces = refs[:count], refs[count:2 * count]
    hid, dgate, dup, low, lows, grad_hidden, grad_down = refs[2 * count:]

    @pl.when(pl.program_id(0) == 0)
    def _():
        low[...] = low_rows(low_in[...], act).astype(BF)
        lows[...] = jnp.zeros(lows.shape, F32)

    rows = columns(act, ids)
    extra = low[...]
    gate = dot(rows, stacked(gate_pieces)) + dot_tn(extra, gate_out[...])
    up = dot(rows, stacked(up_pieces)) + dot_tn(extra, up_out[...])
    chance = 0.5 * (1.0 + lax.erf(gate * (0.5**0.5)))
    active = gate * chance
    slope = chance + gate * (jnp.exp(-0.5 * gate * gate) * 0.3989422804014327)
    hidden = (active * up).astype(BF)
    back = grad[...]
    back_gate = (back * up * slope).astype(BF)
    back_up = (back * active).astype(BF)
    hid[...] = hidden
    dgate[...] = back_gate
    dup[...] = back_up
    lows[:RANK, :] += dot_nt(down_in[...], hidden)
    lows[RANK:, :] += dot_nt(gate_out[...], back_gate) + dot_nt(up_out[...], back_up)
    grad_hidden[:RANK, :] = dot(extra[:RANK], back_gate).astype(BF)
    grad_hidden[RANK:, :] = dot(extra[RANK:], back_up).astype(BF)
    grad_down[...] = dot(grad_low[...], hidden).astype(BF)


def mlp(ids, act, low_in, gate_out, up_out, down_in, grad, grad_low, gate_pieces, up_pieces):
    rows, depth = row_count(act), act[0].shape[1]
    width = gate_pieces[0].shape[2]
    block = 256
    ranks = low_in.shape[0]
    column = lambda height: pl.BlockSpec((height, block), lambda n: (0, n))
    return pl.pallas_call(
        partial(mlp_kernel, len(act), len(gate_pieces)),
        grid=(width // block,),
        in_specs=[smem(), full(low_in.shape), column(ranks), column(ranks),
                  column(down_in.shape[0]), column(rows), full(grad_low.shape)]
        + whole(act) + piece_specs(gate_pieces, block) + piece_specs(up_pieces, block),
        out_specs=[column(rows), column(rows), column(rows), full((ranks, rows)),
                   full((ranks + RANK, rows)), column(ranks), column(grad_low.shape[0])],
        out_shape=[jax.ShapeDtypeStruct((rows, width), BF)] * 3
        + [jax.ShapeDtypeStruct((ranks, rows), BF),
           jax.ShapeDtypeStruct((ranks + RANK, rows), F32),
           jax.ShapeDtypeStruct((ranks, width), BF),
           jax.ShapeDtypeStruct((grad_low.shape[0], width), BF)],
        compiler_params=params(48),
        cost_estimate=estimate(4 * rows * depth * width, 4 * depth * width + 8 * rows * depth),
        name="mlp",
    )(ids, low_in, gate_out, up_out, down_in, grad, grad_low, *act, *gate_pieces, *up_pieces)


def unfold_kernel(layout, ids, low_in, *refs):
    blocks, count, weights = layout
    lows, refs = refs[:blocks], refs[blocks:]
    acts, pieces, outs = refs[:blocks * count], refs[blocks * count:-blocks], refs[-blocks:]
    size = outs[0].shape[0]
    step = pl.program_id(0)
    subs = pl.num_programs(0)
    width = pieces[0].shape[1]
    extra = jnp.concatenate([low[...] for low in lows], axis=1).astype(BF)
    per = len(pieces) // weights
    rows = jnp.concatenate(
        [jnp.concatenate([act[...] for act in acts[i * count:(i + 1) * count]], axis=1)
         for i in range(blocks)], axis=0
    )
    for i in range(per):
        at = aligned(ids[i * subs + step] * width, width)
        weight = jnp.concatenate([pieces[k * per + i][0] for k in range(weights)], axis=1)
        product = (dot_nt(rows, weight) + dot_tn(extra, low_in[:, at])).astype(BF)
        for j, out in enumerate(outs):
            out[:, at] = product[j * size:(j + 1) * size]


def unfold(ids, acts, low, low_in, weights, size, blocks):
    subs = weights[0][0].shape[0]
    width = low_in.shape[1]
    pieces = [piece for weight in weights for piece in weight]
    depth = sum(act.shape[1] for act in acts)
    count = len(blocks)
    return pl.pallas_call(
        partial(unfold_kernel, (count, len(acts), len(weights))),
        grid=(subs,),
        in_specs=[smem(), full(low_in.shape)]
        + [pl.BlockSpec((low.shape[0], size), lambda s, at=at: (0, at)) for at in blocks]
        + [pl.BlockSpec((size, act.shape[1]), lambda s, at=at: (at, 0))
           for at in blocks for act in acts]
        + [pl.BlockSpec((1,) + w.shape[1:], lambda s: (s, 0, 0)) for w in pieces],
        out_specs=[full((size, width))] * count,
        out_shape=[jax.ShapeDtypeStruct((size, width), BF)] * count,
        compiler_params=params(48),
        cost_estimate=estimate(
            2 * count * size * depth * width, 2 * depth * width + 4 * count * size * depth
        ),
        name="unfold",
    )(ids, low_in, *[low] * count, *list(acts) * count, *pieces)


def gate_back_kernel(parts, ids, low_back, low_in, gate, nrm, inverse, hold, low_gate, low_out,
                     *refs):
    act, pieces = refs[:parts], refs[parts:-6]
    dgate, dret, low, dlow, grad_in, grad_gate = refs[-6:]

    @pl.when(pl.program_id(0) == 0)
    def _():
        low[...] = low_rows(low_back[...], act).astype(BF)
        dlow[...] = jnp.zeros(dlow.shape, F32)

    weights = jnp.concatenate([w[s] for w in pieces for s in range(w.shape[0])], axis=1)
    back = dot_nt(columns(act, ids), weights) + dot_tn(low[...], low_in[...])
    level = gate[...]
    normed = nrm[...]
    chance = 1.0 / (1.0 + jnp.exp(-level))
    slope = chance * (1.0 + level * (1.0 - chance))
    back_gate = (back * normed * slope).astype(BF)
    grad = back * (level * chance)
    mean = jnp.mean(grad, axis=1, keepdims=True)
    along = jnp.mean(grad * normed, axis=1, keepdims=True)
    dgate[...] = back_gate
    dret[...] = (inverse[0, :, :1] * (grad - mean - normed * along)).astype(BF)
    grad_in[...] = dot(low[...], hold[...]).astype(BF)
    grad_gate[...] = dot(low_gate[...], back_gate).astype(BF)
    dlow[...] += dot_nt(low_out[...], back_gate)


def gate_back(ids, act, low_back, low_in, gate, nrm, inverse, hold, low_gate, low_out, pieces):
    rows, depth = row_count(act), act[0].shape[1]
    width = gate.shape[1]
    block = VALUE_DIM
    ranks = low_back.shape[0]
    column = lambda height: pl.BlockSpec((height, block), lambda n: (0, n))
    return pl.pallas_call(
        partial(gate_back_kernel, len(act)),
        grid=(width // block,),
        in_specs=[smem(), full(low_back.shape), column(ranks), column(rows),
                  column(rows), pl.BlockSpec((1, rows, 128), lambda n: (n, 0, 0)), column(rows),
                  full(low_gate.shape), column(low_out.shape[0])]
        + whole(act) + [pl.BlockSpec((w.shape[0], block, w.shape[2]), lambda n: (0, n, 0)) for w in pieces],
        out_specs=[column(rows), column(rows), full((ranks, rows)),
                   full((low_out.shape[0], rows)), column(ranks), column(ranks)],
        out_shape=[jax.ShapeDtypeStruct((rows, width), BF)] * 2
        + [jax.ShapeDtypeStruct((ranks, rows), BF),
           jax.ShapeDtypeStruct((low_out.shape[0], rows), F32),
           jax.ShapeDtypeStruct((ranks, width), BF), jax.ShapeDtypeStruct((ranks, width), BF)],
        compiler_params=params(56),
        cost_estimate=estimate(2 * rows * depth * width, 2 * depth * width + 16 * rows * width),
        name="gate_back",
    )(ids, low_back, low_in, gate, nrm, inverse, hold, low_gate, low_out, *act, *pieces)


def retention_back_kernel(spots, rates, seg_col, seg_row, cosine, sine_table, low, begin, q_out,
                          k_out, v_out, q, k, v, dret, dq, dk, dv, dlow, grad_q, grad_k, grad_v,
                          sums):
    head = pl.program_id(0)
    rate = rates[head]
    count = spots.shape[0]
    size = q.shape[0] // count
    down, across = decay_factors(rate, size)
    column_factor = jnp.exp(rate * across)
    key_scale = 1.0 / KEY_DIM**0.5

    @pl.when(head == 0)
    def _():
        dlow[...] = begin[...]

    sums[...] = jnp.zeros(sums.shape, F32)
    for j in range(count):
        there = aligned(spots[j] * size, size)
        place = slice(j * size, (j + 1) * size)
        key, value = k[there, :], v[there, :]
        seg_there = seg_col[place, :]
        key_sum = jnp.zeros((size, KEY_DIM), F32)
        value_sum = jnp.zeros((size, VALUE_DIM), F32)
        for i in range(j, count):
            here = aligned(spots[i] * size, size)
            query, back = q[here, :], dret[here, :]
            row_factor = jnp.exp(rate * ((i - j) * size - down))
            alive = seg_there == seg_row[:, i * size:(i + 1) * size]
            if i == j:
                alive = alive & (across >= down)
            weight = jnp.where(alive, row_factor * column_factor, 0.0)
            mixed = (dot_nt(key, query) * weight).astype(BF)
            grad = (dot_nt(value, back) * weight).astype(BF)
            value_sum = value_sum + dot(mixed, back)
            key_sum = key_sum + dot(grad, query)
            sums[i * size:(i + 1) * size, :] += dot_tn(grad, key)
        dk[there, :] = (
            key_scale * unrotated(key_sum, cosine[place, :], sine_table[place, :])
        ).astype(BF)
        dv[there, :] = value_sum.astype(BF)
    for i in range(count):
        place = slice(i * size, (i + 1) * size)
        dq[aligned(spots[i] * size, size), :] = unrotated(
            sums[place, :], cosine[place, :], sine_table[place, :]
        ).astype(BF)
    back_q, back_k, back_v = dq[...], dk[...], dv[...]
    dlow[...] += (
        dot_nt(q_out[...], back_q) + dot_nt(k_out[...], back_k) + dot_nt(v_out[...], back_v)
    )
    grad_q[...] = dot(low[:RANK, :], back_q).astype(BF)
    grad_k[...] = dot(low[RANK:2 * RANK, :], back_k).astype(BF)
    grad_v[...] = dot(low[2 * RANK:3 * RANK, :], back_v).astype(BF)


def retention_back(spots, rates, seg_col, seg_row, cosine, sine_table, low, begin, qk_out, v_out,
                   qk, v, dret):
    rows = qk.shape[0]
    heads = v.shape[1] // VALUE_DIM
    ranks = low.shape[0]
    key = lambda height: pl.BlockSpec((height, KEY_DIM), lambda h: (0, h))
    later = lambda height: pl.BlockSpec((height, KEY_DIM), lambda h: (0, h + heads))
    value = lambda height: pl.BlockSpec((height, VALUE_DIM), lambda h: (0, h))
    keys = heads * KEY_DIM
    return pl.pallas_call(
        retention_back_kernel,
        grid=(heads,),
        in_specs=[smem(), smem(), full(seg_col.shape), full(seg_row.shape), full(cosine.shape),
                  full(cosine.shape), full(low.shape), full(begin.shape), key(ranks),
                  later(ranks), value(ranks),
                  key(rows), later(rows), value(rows), value(rows)],
        out_specs=[key(rows), key(rows), value(rows), full((ranks, rows)), key(RANK), key(RANK),
                   value(RANK)],
        out_shape=[jax.ShapeDtypeStruct((rows, keys), BF), jax.ShapeDtypeStruct((rows, keys), BF),
                   jax.ShapeDtypeStruct(v.shape, BF), jax.ShapeDtypeStruct((ranks, rows), F32),
                   jax.ShapeDtypeStruct((RANK, keys), BF), jax.ShapeDtypeStruct((RANK, keys), BF),
                   jax.ShapeDtypeStruct((RANK, v.shape[1]), BF)],
        scratch_shapes=[pltpu.VMEM((rows, KEY_DIM), F32)],
        compiler_params=params(48),
        cost_estimate=estimate(2 * rows * rows * 1792 * heads, 30 << 20),
        name="retention_back",
    )(spots, rates, seg_col, seg_row, cosine, sine_table, low, begin, qk_out, qk_out, v_out, qk, qk,
      v, dret)


def share_kernel(heights, rank, low, *refs):
    out = refs[-1]
    at, first = 0, 0
    for height, parts in heights:
        total = jnp.zeros((height, out.shape[1]), F32)
        begin = 0
        for ref in refs[first:first + parts]:
            end = begin + ref.shape[0]
            total = total + dot(low[at:at + height, begin:end], ref[...])
            begin = end
        out[at:at + height, :] = total.astype(BF)
        at, first = at + height, first + parts


def share(rank, low, span, items):
    acts = [array for _, act in items for array in act]
    heights = tuple((height, len(act)) for height, act in items)
    return pl.pallas_call(
        partial(share_kernel, heights),
        grid_spec=pltpu.PrefetchScalarGridSpec(
            num_scalar_prefetch=1,
            grid=(1,),
            in_specs=[pl.BlockSpec(low.shape, lambda i, r: (0, 0))]
            + [pl.BlockSpec((act.shape[0], span), lambda i, r: (0, r[0])) for act in acts],
            out_specs=pl.BlockSpec((low.shape[0], span), lambda i, r: (0, 0)),
        ),
        out_shape=jax.ShapeDtypeStruct((low.shape[0], span), BF),
        compiler_params=params(24),
        cost_estimate=estimate(2 * low.shape[0] * low.shape[1] * span, 4 << 20),
        name="share",
    )(rank.reshape(1), low, *in_hbm(*acts))


def place_kernel(layout, order, places, pack, *outs):
    span = pack.shape[2]
    count = places.shape[0]
    for (begin, height, kind, stride), out in zip(layout, outs):
        if kind == "shares":
            for j in range(count):
                rows = pack[0, begin + stride * j:begin + stride * j + height, :]
                out[0, :, aligned(places[j] * span, span)] = rows.astype(F32)
        elif kind == "halves":
            for j in range(2):
                rows = pack[0, begin + stride * j:begin + stride * j + height, :]
                out[0, :, j * span:(j + 1) * span] = rows.astype(F32)
        else:
            for j in range(2):
                rows = pack[0, begin + stride * j:begin + stride * j + height, :]
                out[0, j] = rows.astype(F32)


def place(order, places, pack, layout):
    entries = order.shape[0]
    span, count = pack.shape[2], places.shape[0]
    shapes = []
    for _, height, kind, _ in layout:
        shapes.append({"shares": (height, count * span), "halves": (height, 2 * span)}.get(
            kind, (2, height, span)))
    return pl.pallas_call(
        partial(place_kernel, layout),
        grid_spec=pltpu.PrefetchScalarGridSpec(
            num_scalar_prefetch=2,
            grid=(entries,),
            in_specs=[pl.BlockSpec((1,) + pack.shape[1:], lambda e, o, p: (o[e], 0, 0))],
            out_specs=[
                pl.BlockSpec((1,) + shape, lambda e, o, p, n=len(shape): (e,) + (0,) * n)
                for shape in shapes
            ],
        ),
        out_shape=[jax.ShapeDtypeStruct((entries,) + shape, F32) for shape in shapes],
        compiler_params=params(32),
        cost_estimate=estimate(0, 10 << 20),
        name="place",
    )(order, places, pack)


def after(x, *others):
    return lax.optimization_barrier((x,) + others)[0]


class PlainLinks:
    def __init__(self, ndp, nt):
        self.ndp, self.nt = ndp, nt
        self.rank = lax.axis_index("tensor")
        self.chunks = jnp.arange(nt, dtype=jnp.int32)
        self.spots = self.chunks
        self.row_ids = jnp.zeros((1,), jnp.int32)

    def exchange(self, x):
        return x

    def mine(self, own, other):
        return own

    def gather(self, x):
        return [lax.all_gather(x, "tensor", axis=0, tiled=True)]

    def scatter(self, rows):
        total = lax.psum_scatter(
            jnp.concatenate(rows, axis=0), "tensor", scatter_dimension=0, tiled=True
        )
        zero = jnp.zeros_like(total)
        return (total, zero, zero)

    def forward(self, shards, tokens, cotangent, line, steps):
        blocks = [
            [lax.all_gather(shard, "dp", axis=int(shard.shape[1] * self.ndp == tokens.shape[1]),
                            tiled=True)[None]]
            for shard in shards
        ]
        steps.ready(line, steps.tables(line, line)[0])
        a = self.gather(steps.norm(tokens))
        dy = self.gather(cotangent)
        qkv = steps.query_key_value(a, blocks[0], blocks[1])
        mixed = steps.gate_and_mix(a, *qkv, blocks[2])
        *rows, low = steps.fold(mixed[0], blocks[3])
        middle, b = steps.join(tokens, self.scatter(rows))
        dhid = steps.hidden_grad(dy, blocks[4])
        return (blocks, tokens, a, cotangent, dy, qkv, mixed, low, middle, self.gather(b), dhid)

    def group_sum(self, x):
        return lax.psum(x.astype(BF), "tensor")

    def all_shares(self, x, height):
        first = lax.all_gather(x[:height], "tensor", tiled=True)
        every = lax.all_gather(jnp.concatenate([first, x[height:]]), "dp")
        return every, jnp.arange(self.ndp, dtype=jnp.int32), self.chunks

    def backward(self, steps):
        steps.mlp()
        dz = self.gather(steps.dz(self.scatter(steps.unfold_mlp(256, (0, 1, 2, 3)))))
        output = steps.output(self.scatter(steps.fold_down(steps.hid)))
        lows = self.group_sum(steps.early_lows())
        steps.gate_back(dz)
        early = self.all_shares(steps.early(lows, dz), steps.early_height)
        steps.retention_back(steps.dret)
        late = self.all_shares(steps.late(self.group_sum(steps.dlow)), steps.late_height)
        parts = self.scatter(steps.unfold_attn(256, (0, 1, 2, 3)))
        dx, _ = steps.dx(parts, 0, parts[0].shape[0])
        return output, dx, early, late


class PairedLinks:
    def __init__(self, ndp, nt):
        self.ndp, self.nt = ndp, nt
        d, t = lax.axis_index("dp"), lax.axis_index("tensor")
        c, p, m = d % 2, t // 2, t % 2
        self.home = c == p
        self.rank = 2 * c + m
        flips = jnp.array([0, 2, 1, 3], jnp.int32)
        self.chunks = self.rank ^ flips
        order = jnp.arange(4, dtype=jnp.int32) ^ self.rank
        self.spots = (order % 2) * 2 + order // 2
        g = d // 2
        self.row_ids = ((2 * (g ^ jnp.arange(4, dtype=jnp.int32))[:, None]
                         + jnp.arange(2, dtype=jnp.int32)[None, :]) ^ c).reshape(-1)
        self.last = {}
        self.last_round = ()
        self.slow = ()

    def pairs(self, place):
        listed = []
        for d in range(self.ndp):
            for t in range(self.nt):
                to = place(d, t)
                if to is not None:
                    listed.append((d * self.nt + t, to[0] * self.nt + to[1]))
        return listed

    def move(self, x, place, chain=None):
        if chain in self.last:
            x = after(x, *self.last[chain])
        moved = lax.ppermute(x, ("dp", "tensor"), self.pairs(place))
        if chain is not None:
            self.last[chain] = (moved,)
        return moved

    def send(self, moves):
        return [lax.ppermute(x, ("dp", "tensor"), self.pairs(place)) for x, place in moves]

    def round(self, moves, work=None, inputs=(), later=(), slow=()):
        every = list(moves) + list(slow)
        values = [x for x, _ in every]
        flat, form = jax.tree.flatten((values, inputs))
        last, _ = jax.tree.flatten(self.last_round)
        if last:
            flat = lax.optimization_barrier((*flat, *last))[:len(flat)]
        values, inputs = jax.tree.unflatten(form, flat)
        moved = self.send([(x, place) for x, (_, place) in zip(values, every)])
        moved, slowly = moved[:len(moves)], moved[len(moves):]
        second = []
        if later:
            count, make = later
            moves = make(moved[:count])
            values = [x for x, _ in moves]
            values = lax.optimization_barrier((*values, *moved[:count]))[:len(values)]
            second = self.send([(x, place) for x, (_, place) in zip(values, moves)])
        made = work(*inputs) if work is not None else ()
        self.last_round = (moved, second, made, self.slow)
        self.slow = slowly
        return moved + slowly, second, made

    def core(self, x):
        return self.move(x, lambda d, t: (d ^ 1, t))

    def pair(self, x):
        return self.move(x, lambda d, t: (d, t ^ 1), "pair")

    def mine(self, own, other):
        return jnp.where(self.home, own, other)

    def exchange(self, x):
        moved = self.move(
            x, lambda d, t: (d ^ 1, t ^ 2) if d % 2 != t // 2 else None, "middle"
        )
        return jnp.where(self.home, x, moved)

    def gather(self, x):
        across = self.pair(x)
        return [x, self.core(x), across, self.core(across)]

    def forward(self, shards, tokens, cotangent, line, steps):
        by_one = lambda d, t: (d ^ 2, t)
        by_two = lambda d, t: (d ^ 4, t)
        core = lambda d, t: (d ^ 1, t)
        pair = lambda d, t: (d, t ^ 1)
        swap = lambda d, t: (d ^ 1, t ^ 2) if d % 2 != t // 2 else None
        seat = lambda d, t: (d, t ^ 2) if d % 2 == t // 2 else None
        blocks = [[None] * 4 for _ in shards]
        doubled = [jnp.stack([shards[0], self.core(shards[0])])]

        def over(i):
            return (doubled[i], seat)

        def arrived(i, moved):
            blocks[i][0] = self.mine(doubled[i], moved)

        hops = {
            "x": lambda i: (blocks[i][0], by_one),
            "y": lambda i: (blocks[i][0], by_two),
            "xy": lambda i: (blocks[i][1], by_two),
            "yx": lambda i: (blocks[i][2], by_one),
        }
        place_of = {"x": 1, "y": 2, "xy": 3, "yx": 3}

        def go(first, second, others, work=None, inputs=()):
            def later(moved):
                for (i, way), block in zip(first, moved):
                    blocks[i][place_of[way]] = block
                return [hops[way](i) for i, way in second]

            moved, seconds, made = self.round(
                [hops[way](i) for i, way in first] + list(others), work, inputs,
                (len(first), later)
            )
            for (i, way), block in zip(second, seconds):
                blocks[i][place_of[way]] = block
            return moved[len(first):], made

        def double(rest):
            return [jnp.stack([shard, self.core(shard)]) for shard in rest]

        def whole_rows(own, across):
            return [own, self.core(own), across, self.core(across)]

        other = self.core(line)
        (moved,), made = go([], [], [over(0)], double, (shards[1:],))
        doubled += made
        arrived(0, moved)
        (moved,), (home_table, sent_table) = go(
            [(0, "x"), (0, "y")], [], [over(1)], steps.tables, (line, other)
        )
        arrived(1, moved)
        (one, two), _ = go([(1, "x"), (0, "xy")], [(1, "y")], [over(2), over(3)])
        arrived(2, one)
        arrived(3, two)
        (x, table, moved), _ = go([(2, "x"), (2, "y")], [(1, "yx"), (2, "xy")],
                                  [(tokens, swap), (sent_table, seat), over(4)])
        arrived(4, moved)
        x = self.mine(tokens, x)
        steps.ready(other, self.mine(home_table, table))
        a = steps.norm(x)
        (moved, grad, across), _ = go([(3, "x"), (3, "y")], [(4, "x"), (3, "xy")],
                                      [over(5), (cotangent, swap), (a, pair)])
        arrived(5, moved)
        grad = self.mine(cotangent, grad)

        def attend(own, across, *weights):
            a = whole_rows(own, across)
            return a, steps.query_key_value(a, *weights)

        (moved,), (a, qkv) = go([(5, "x"), (4, "y")], [], [over(6)], attend,
                                (a, across, blocks[0], blocks[1]))
        arrived(6, moved)

        def mix(a, qk, low, v, w_g, w_o):
            mixed = steps.gate_and_mix(a, qk, low, v, w_g)
            return mixed, steps.fold(mixed[0], w_o)

        (across,), (mixed, folded) = go([(4, "yx"), (5, "y")], [], [(grad, pair)], mix,
                                        (a, *qkv, blocks[2], blocks[3]))
        own, near, far, beyond, low = folded
        near, beyond = self.send([(near, core), (beyond, core)])
        far = (far.astype(F32) + beyond.astype(F32)).astype(BF)

        def grad_rows(grad, across, w_d):
            dy = whole_rows(grad, across)
            return dy, steps.hidden_grad(dy, w_d)

        (far,), (dy, dhid) = go([(6, "x"), (6, "y")], [], [(far, pair)], grad_rows,
                                (grad, across, blocks[4]))
        parts = (own, near)
        middle, b = steps.join(x, (*parts, far))
        (across,), _ = go([(5, "yx"), (6, "xy")], [], [(b, pair)])
        b = whole_rows(b, across)
        return blocks, x, a, grad, dy, qkv, mixed, low, middle, b, dhid

    def core_sum(self, x, other):
        size = x.shape[1] // 4
        other = other.astype(F32)
        return (x + jnp.concatenate(
            [other[:, i * size:(i + 1) * size] for i in (1, 0, 3, 2)], axis=1
        )).astype(BF)

    def pair_sum(self, x, other):
        size = x.shape[1] // 2
        other = jnp.concatenate([other[:, size:], other[:, :size]], axis=1)
        return (x.astype(F32) + other.astype(F32)).astype(BF)

    def backward(self, steps):
        pair = lambda d, t: (d, t ^ 1)
        swap = lambda d, t: (d ^ 1, t ^ 2) if d % 2 != t // 2 else None
        over = lambda d, t: (d, t ^ 2)
        by_one = lambda d, t: (d ^ 2, t)
        by_two = lambda d, t: (d ^ 4, t)
        core = lambda d, t: (d ^ 1, t)

        def add(one, two):
            return (one.astype(F32) + two.astype(F32)).astype(BF)

        steps.mlp()
        near, beyond = steps.unfold_mlp(256, (1, 3))
        far, = steps.unfold_mlp(256, (2,))
        near, beyond, lows = self.send([(near, core), (beyond, core), (steps.lows_low(), core)])
        far = add(far, beyond)
        lows = self.core_sum(steps.early_lows(), lows)
        self.last_round = ()
        (far, other), _, (own, folded) = self.round(
            [(far, pair), (lows, pair)],
            lambda hid: (steps.unfold_mlp(256, (0,))[0], steps.fold_down(hid)), (steps.hid,)
        )
        lows = self.pair_sum(lows, other)
        dz = steps.dz((own, near, far))
        own_out, near_out, far_out, beyond_out = folded
        (across, dz_near, near_out, beyond_out), _, _ = self.round(
            [(dz, pair), (dz, core), (near_out, core), (beyond_out, core)]
        )
        (dz_beyond, far_out), _, _ = self.round(
            [(across, core)], slow=[(add(far_out, beyond_out), pair)]
        )
        dz = [dz, dz_near, across, dz_beyond]
        _, _, (early, dret) = self.round([], steps.middle_back, (lows, dz))
        (moved,), _, dpv = self.round([(early, swap)], steps.retention_back, (dret,))
        early = self.mine(early, moved)
        first = early[:steps.early_height]
        output = steps.output((own_out, near_out, far_out))

        (moved, dlow), _, (near, beyond) = self.round(
            [(first, pair), (steps.dlow.astype(BF), core)],
            lambda dpv: steps.unfold_attn(256, (1, 3), dpv), (dpv,)
        )
        dlow = self.core_sum(steps.dlow, dlow)
        first = jnp.concatenate([first, moved])
        (moved, near, beyond, other), _, (far,) = self.round(
            [(first, over), (near, core), (beyond, core), (dlow, pair)],
            lambda dpv: steps.unfold_attn(256, (2,), dpv), (dpv,)
        )
        early = jnp.concatenate([first, moved, early[steps.early_height:]])
        far = add(far, beyond)
        half = far.shape[0] // 2
        late = steps.late(self.pair_sum(dlow, other))
        (moved, far0, far1), _, (own,) = self.round(
            [(late, swap)], lambda dpv: steps.unfold_attn(256, (0,), dpv), (dpv,),
            slow=[(far[:half], pair), (far[half:], pair)]
        )
        early = lax.all_gather(early, "dp")
        late = self.mine(late, moved)
        moved_out, = self.send([(output, swap)])
        rows = []
        for i, part in enumerate((far0, far1)):
            dx, low = steps.dx((own, near, part), i * half, half)
            moved, = self.send([(low, swap)])
            rows.append(self.mine(dx, moved.astype(F32)))
        first = late[:steps.late_height]
        first = jnp.concatenate([first, *self.send([(first, pair)])])
        first = jnp.concatenate([first, *self.send([(first, over)])])
        late = jnp.concatenate([first, late[steps.late_height:]])[None]
        for place in (by_one, by_two, core):
            late = jnp.concatenate([late, *self.send([(late, place)])])
        places = jnp.arange(self.nt, dtype=jnp.int32) ^ lax.axis_index("tensor")
        at = jnp.arange(self.ndp, dtype=jnp.int32)
        apart = at ^ lax.axis_index("dp")
        return (self.mine(output, moved_out), jnp.concatenate(rows), (early, at, places),
                (late, apart // 2 + 4 * (apart % 2), places))


def rotation_tables(seq_length, half_dim):
    positions = jnp.arange(seq_length, dtype=jnp.float32)
    frequency = jnp.exp(-jnp.log(10000.0) * jnp.arange(half_dim, dtype=jnp.float32) / half_dim)
    angles = positions[:, None] * frequency[None, :]
    return (jnp.cos(angles), jnp.sin(angles))


def shards(
    ndp,
    nt,
    tokens,
    cotangent,
    adapter_ids,
    segments,
    norm_attn,
    norm_mlp,
    weight_query,
    weight_key,
    weight_value,
    weight_gate,
    weight_out,
    weight_mlp_gate,
    weight_mlp_up,
    weight_mlp_down,
    adapt_attn_in,
    adapt_query_key,
    adapt_value_gate,
    adapt_out_in,
    adapt_out_back,
    adapt_mlp_in,
    adapt_mlp_hidden,
    adapt_down_in,
    adapt_down_back,
):
    links = PairedLinks(ndp, nt) if (ndp, nt) == (8, 4) else PlainLinks(ndp, nt)
    rank, chunks, spots, ids = links.rank, links.chunks, links.spots, links.row_ids
    adapters = adapt_attn_in.shape[0]
    depth = tokens.shape[2]
    seq_length = segments.shape[1]
    gain_attn, gain_mlp = norm_attn[None], norm_mlp[None]

    def pick(table, which):
        return lax.dynamic_index_in_dim(table, which, 0, keepdims=False)

    def packed(which):
        qk, vg = pick(adapt_query_key, which), pick(adapt_value_gate, which)
        return jnp.concatenate(
            [jnp.concatenate([qk[0], qk[1]], axis=1), vg[0], vg[1],
             pick(adapt_mlp_hidden, which).reshape(2 * RANK, -1),
             pick(adapt_out_in, which).T, pick(adapt_down_in, which).T], axis=0
        )

    own_id = adapter_ids[0, 0]
    own_line = jnp.concatenate([segments, jnp.broadcast_to(adapter_ids, (1, 128))], axis=1)
    wide = weight_gate.shape[1]
    keys = adapt_query_key.shape[3]
    heads_local = wide // VALUE_DIM
    head_ids = (rank * heads_local + jnp.arange(heads_local, dtype=jnp.int32)).astype(F32)
    rates = jnp.log(1.0 - jnp.exp2(-5.0 - head_ids))
    cosine, sine_table = rotation_tables(seq_length, HALF)

    class Steps:
        def tables(self, line, other):
            return packed(line[0, seq_length]), packed(other[0, seq_length])

        def ready(self, other, table):
            line = links.mine(own_line, other)
            self.work_id = work_id = line[0, seq_length]
            self.seg_row = line[:, :seq_length]
            self.seg_col = self.seg_row.reshape(seq_length, 1)
            blank = jnp.zeros((RANK, wide), BF)
            left = jnp.arange(wide)[None, :] < keys
            zero = jnp.zeros((), BF)
            self.qk_out = jnp.concatenate([jnp.where(left, table[:RANK], zero),
                                           jnp.where(left, zero, table[:RANK]), blank, blank])
            self.v_out = jnp.concatenate([blank, blank, table[RANK:2 * RANK], blank])
            self.g_out = jnp.concatenate([blank, blank, blank, table[2 * RANK:3 * RANK]])
            self.mg_out = jnp.concatenate([table[3 * RANK:4 * RANK], blank])
            self.mu_out = jnp.concatenate([blank, table[4 * RANK:5 * RANK]])
            self.out_in = table[5 * RANK:6 * RANK]
            self.down_in = table[6 * RANK:7 * RANK]
            self.attn_in = pick(adapt_attn_in, work_id).T
            self.out_back = pick(adapt_out_back, work_id)
            self.mlp_in = pick(adapt_mlp_in, work_id).T
            self.down_back = pick(adapt_down_back, work_id)

        def norm(self, x):
            return norm_rows(x, gain_attn)

        def query_key_value(self, a, w_qk, w_v):
            qk, low = project_query_key(
                ids, chunks, a, self.attn_in, self.qk_out, cosine, sine_table, w_qk
            )
            return qk, low, project(ids, a, low, self.v_out, w_v, BF)

        def gate_and_mix(self, a, qk, low, v, w_g):
            gate = project(ids, a, low, self.g_out, w_g, F32)
            return (*retention(spots, rates, self.seg_col, self.seg_row, qk, v, gate), gate)

        def fold(self, o, w_o):
            return fold(ids, o, self.out_in, self.out_back, w_o)

        def join(self, x, parts):
            return join_rows(x, parts, gain_mlp)

        def hidden_grad(self, dy, w_d):
            return hidden_grad(ids, dy, self.down_back, self.down_in, w_d)

    steps = Steps()
    ((w_qk, w_v, w_g, w_o, w_d, w_mg, w_mu), x, a, grad, dy, (qk, low_a, v),
     (o, nrm, inverse, gate), low_o, middle, b, (dhid, low_dy)) = links.forward(
        [jnp.concatenate([weight_query, weight_key], axis=1), weight_value, weight_gate,
         weight_out, weight_mlp_down, weight_mlp_gate, weight_mlp_up],
        tokens[0], cotangent[0], own_line, steps,
    )
    seg_row, seg_col, work_id = steps.seg_row, steps.seg_col, steps.work_id
    qk_out, v_out, g_out, mg_out, mu_out = (
        steps.qk_out, steps.v_out, steps.g_out, steps.mg_out, steps.mu_out
    )
    attn_in, out_in, out_back = steps.attn_in, steps.out_in, steps.out_back
    mlp_in, down_in, down_back = steps.mlp_in, steps.down_in, steps.down_back

    span = depth // nt
    halves = lambda y: jnp.concatenate([y[:, :wide // 2], y[:, wide // 2:]])

    class Back:
        early_height = 4 * RANK
        late_height = 4 * RANK

        def mlp(self):
            (self.hid, self.dgate, self.dup, _, self.lows, self.grad_hidden,
             self.grad_down) = mlp(
                ids, b, mlp_in, mg_out, mu_out, down_in, dhid, low_dy, w_mg, w_mu
            )

        def unfold_mlp(self, size, blocks):
            return unfold(ids, (self.dgate, self.dup), self.lows[RANK:], mlp_in, (w_mg, w_mu),
                          size, blocks)

        def dz(self, parts):
            self.dmid, low = rms_back(middle, grad, parts, gain_mlp, 0, middle.shape[0])
            return low

        def fold_down(self, hid):
            return fold(ids, hid, down_in, down_back, w_d)[:4]

        def output(self, parts):
            return (middle + (
                parts[0].astype(F32) + parts[1].astype(F32) + parts[2].astype(F32)
            )).astype(BF)

        def early_lows(self):
            return jnp.concatenate([self.lows, low_o])

        def lows_low(self):
            return self.early_lows().astype(BF)

        def early(self, lows, dz):
            mark = jnp.full((RANK, span), work_id, F32).astype(BF)
            return jnp.concatenate(
                [share(rank, lows, span, ((RANK, dy), (2 * RANK, b), (RANK, dz))),
                 halves(jnp.concatenate([self.grad_hidden, self.grad_down, self.grad_out_in,
                                         self.grad_gate])), mark]
            )

        def gate_back(self, dz):
            (self.dpg, self.dret, _, self.dlow, self.grad_out_in, self.grad_gate) = gate_back(
                ids, dz, out_back, out_in, gate, nrm, inverse, o, low_a[3 * RANK:], g_out, w_o
            )

        def middle_back(self, lows, dz):
            self.gate_back(dz)
            return self.early(lows, dz), self.dret

        def retention_back(self, dret):
            (self.dpq, self.dpk, self.dpv, self.dlow, self.grad_q, self.grad_k,
             self.grad_v) = retention_back(
                spots, rates, seg_col, seg_row, cosine, sine_table, low_a, self.dlow, qk_out,
                v_out, qk, v, dret
            )
            self.dpqk = jnp.concatenate([self.dpq, self.dpk], axis=1)
            return self.dpv

        def late(self, lows):
            return jnp.concatenate(
                [share(rank, lows, span, ((4 * RANK, a),)),
                 halves(jnp.concatenate(
                     [jnp.concatenate([self.grad_q, self.grad_k], axis=1), self.grad_v]
                 ))]
            )

        def unfold_attn(self, size, blocks, dpv=None):
            dpv = self.dpv if dpv is None else dpv
            return unfold(ids, (self.dpqk, dpv, self.dpg), self.dlow, attn_in,
                          (w_qk, w_v, w_g), size, blocks)

        def dx(self, parts, begin, count):
            return rms_back(x, self.dmid, parts, gain_attn, begin, count)

    output, input_grad, early, late = links.backward(Back())
    early, early_at, early_places = early
    late, late_at, late_places = late
    shares = nt * Back.early_height
    all_ids = early[:, shares + 10 * RANK, 0].astype(jnp.int32)
    chosen = jnp.arange(adapters, dtype=jnp.int32)[:, None] == all_ids[None, :]
    if all_ids.shape[0] == adapters:
        order = jnp.sum(
            jnp.where(chosen, jnp.arange(adapters, dtype=jnp.int32)[None, :], 0), axis=1
        )
    else:
        total = lambda y: jnp.einsum(
            "es,sij->eij", chosen.astype(BF), y, preferred_element_type=F32
        )
        early, late = total(early), total(late)
        order = jnp.arange(adapters, dtype=jnp.int32)
        early_at = late_at = order
    pitch = Back.early_height
    down_back_out, mlp_out, out_back_out, hidden_out, down_out, out_out, gate_out = place(
        early_at[order], early_places, early,
        ((0, RANK, "shares", pitch), (RANK, 2 * RANK, "shares", pitch),
         (3 * RANK, RANK, "shares", pitch), (shares, 2 * RANK, "halves", 5 * RANK),
         (shares + 2 * RANK, RANK, "halves", 5 * RANK),
         (shares + 3 * RANK, RANK, "halves", 5 * RANK),
         (shares + 4 * RANK, RANK, "halves", 5 * RANK))
    )
    pitch = Back.late_height
    shares = nt * pitch
    attn_out, qk_grads, value_out = place(
        late_at[order], late_places, late,
        ((0, 4 * RANK, "shares", pitch), (shares, RANK, "apart", 2 * RANK),
         (shares + RANK, RANK, "halves", 2 * RANK))
    )
    return (
        output[None],
        input_grad[None],
        jnp.swapaxes(attn_out, 1, 2),
        qk_grads,
        jnp.stack([value_out, gate_out], axis=1),
        jnp.swapaxes(out_out, 1, 2),
        out_back_out,
        jnp.swapaxes(mlp_out, 1, 2),
        hidden_out.reshape(adapters, 2, RANK, wide),
        jnp.swapaxes(down_out, 1, 2),
        down_back_out,
    )


def solution(mesh):
    in_specs = (
        P("dp", "tensor", None),
        P("dp", "tensor", None),
        P("dp", None),
        P("dp", None),
        P(),
        P(),
        P("dp", "tensor"),
        P("dp", "tensor"),
        P("dp", "tensor"),
        P("dp", "tensor"),
        P("tensor", "dp"),
        P("dp", "tensor"),
        P("dp", "tensor"),
        P("tensor", "dp"),
        P(),
        P(None, None, None, "tensor"),
        P(None, None, None, "tensor"),
        P(None, "tensor", None),
        P(),
        P(),
        P(None, None, None, "tensor"),
        P(None, "tensor", None),
        P(),
    )
    out_specs = (
        P("dp", "tensor", None),
        P("dp", "tensor", None),
        P(),
        P(None, None, None, "tensor"),
        P(None, None, None, "tensor"),
        P(None, "tensor", None),
        P(),
        P(),
        P(None, None, None, "tensor"),
        P(None, "tensor", None),
        P(),
    )
    local = partial(shards, mesh.shape["dp"], mesh.shape["tensor"])
    return jax.shard_map(local, mesh=mesh, in_specs=in_specs, out_specs=out_specs, check_vma=False)
```

```python
from functools import partial

import jax
import jax.numpy as jnp
from jax import lax
from jax.experimental import pallas as pl
from jax.experimental.pallas import tpu as pltpu
from jax.sharding import PartitionSpec as P

KEY_DIM = 256
VALUE_DIM = 512
RANK = 16
HALF = KEY_DIM // 2

rms_epsilon = 1e-06
group_floor = 1.0
BF = jnp.bfloat16
F32 = jnp.float32


def dot(a, b):
    return jnp.dot(a, b, preferred_element_type=F32)


def dot_nt(a, b):
    return lax.dot_general(a, b, (((1,), (1,)), ((), ())), preferred_element_type=F32)


def dot_tn(a, b):
    return lax.dot_general(a, b, (((0,), (0,)), ((), ())), preferred_element_type=F32)


def aligned(start, size):
    return pl.ds(pl.multiple_of(start, size), size)


def params(mib):
    return pltpu.CompilerParams(
        vmem_limit_bytes=mib << 20, dimension_semantics=("arbitrary",)
    )


def estimate(flops, moved):
    return pl.CostEstimate(flops=1, bytes_accessed=1, transcendentals=0)


def full(shape):
    return pl.BlockSpec(shape, lambda *_: (0,) * len(shape))


def in_hbm(*arrays):
    return [pltpu.with_memory_space_constraint(array, pltpu.HBM) for array in arrays]


def far(shape, kind):
    return pltpu.HBM(shape, kind)


def smem():
    return pl.BlockSpec(memory_space=pltpu.SMEM)


def columns(refs, ids):
    count = ids.shape[0]
    width = refs[0].shape[1] // count
    if count == 1:
        return all_rows(refs)
    return jnp.concatenate(
        [
            jnp.concatenate([ref[:, aligned(ids[i] * width, width)] for i in range(count)], axis=1)
            for ref in refs
        ],
        axis=0,
    )


def all_rows(refs):
    return refs[0][...] if len(refs) == 1 else jnp.concatenate([ref[...] for ref in refs], axis=0)


def low_rows(low_in, refs):
    return jnp.concatenate([dot_nt(low_in, ref[...]) for ref in refs], axis=1)


def whole(arrays):
    return [full(array.shape) for array in arrays]


def row_count(arrays):
    return sum(array.shape[0] for array in arrays)


def stacked(refs):
    return jnp.concatenate([w[s] for w in refs for s in range(w.shape[0])], axis=0)


def rotated(values, cosine, sine_table):
    first = values[:, :HALF]
    second = values[:, HALF:]
    return jnp.concatenate(
        [first * cosine - second * sine_table, second * cosine + first * sine_table], axis=1
    )


def unrotated(values, cosine, sine_table):
    first = values[:, :HALF]
    second = values[:, HALF:]
    return jnp.concatenate(
        [first * cosine + second * sine_table, second * cosine - first * sine_table], axis=1
    )


def norm_kernel(x, gain, out):
    rows = x[...].astype(F32)
    inverse = lax.rsqrt(jnp.mean(rows * rows, axis=1, keepdims=True) + rms_epsilon)
    out[...] = (rows * inverse * gain[...]).astype(BF)


def norm_rows(x, gain):
    return pl.pallas_call(
        norm_kernel,
        out_shape=far(x.shape, BF),
        compiler_params=pltpu.CompilerParams(vmem_limit_bytes=24 << 20),
        name="norm_rows",
    )(x, gain)


def piece_specs(pieces, width):
    return [
        pl.BlockSpec((w.shape[0], w.shape[1], width), lambda n: (0, 0, n)) for w in pieces
    ]


def project_kernel(layout, ids, chunks, low_in, low_out, *refs):
    parts, count, lengths, turn = layout
    if turn:
        (cosine, sine_table), refs = refs[:2], refs[2:]
    act, refs = refs[:parts], refs[parts:]
    groups = len(lengths)
    pieces, outs = refs[:groups * count], refs[groups * count:]
    if turn:
        low = outs[-1]

        @pl.when(pl.program_id(0) == 0)
        def _():
            low[...] = low_rows(low_in[...], act).astype(BF)
    else:
        low = low_in
    n = pl.program_id(0)
    begin = 0
    for i, length in enumerate(lengths):

        @pl.when((n >= begin) & (n < begin + length))
        def _(i=i, length=length):
            made = dot(columns(act, ids), stacked(pieces[i * count:(i + 1) * count]))
            made = made + dot_tn(low[...], low_out[...])
            if i > 0 or not turn:
                outs[i][...] = made.astype(BF)
                return
            scale = jnp.where(n >= length // 2, 1.0 / KEY_DIM**0.5, 1.0)
            size = made.shape[0] // chunks.shape[0]
            for j in range(chunks.shape[0]):
                at = aligned(chunks[j] * size, size)
                rows = slice(j * size, (j + 1) * size)
                turned = rotated(made[rows], cosine[at, :], sine_table[at, :])
                outs[i][rows, :] = (scale * turned).astype(BF)

        begin += length


def project(ids, chunks, act, low_in, low_out, weights, turn):
    rows, depth = row_count(act), act[0].shape[1]
    block = KEY_DIM
    lengths = tuple(w[0].shape[2] // block for w in weights)
    begins = [sum(lengths[:i]) for i in range(len(lengths))]

    def at(group):
        return lambda n: jnp.clip(n - begins[group], 0, lengths[group] - 1)

    pieces = [
        pl.BlockSpec((w.shape[0], w.shape[1], block), lambda n, at=at(i): (0, 0, at(n)))
        for i, weight in enumerate(weights) for w in weight
    ]
    outs = [pl.BlockSpec((rows, block), lambda n, at=at(i): (0, at(n))) for i in range(len(weights))]
    shapes = [far((rows, length * block), BF) for length in lengths]
    ranks = low_in.shape[0]
    if turn:
        outs.append(full((ranks, rows)))
        shapes.append(jax.ShapeDtypeStruct((ranks, rows), BF))
    return pl.pallas_call(
        partial(project_kernel, (len(act), len(weights[0]), lengths, bool(turn))),
        grid=(sum(lengths),),
        in_specs=[smem(), smem(), full(low_in.shape),
                  pl.BlockSpec((ranks, block), lambda n: (0, n))]
        + whole(turn) + whole(act) + pieces,
        out_specs=outs,
        out_shape=shapes,
        compiler_params=params(48),
        cost_estimate=estimate(0, 0),
        name="project",
    )(ids, chunks, low_in, low_out, *turn, *in_hbm(*act, *[w for x in weights for w in x]))


def decay_factors(rate, size):
    down = lax.broadcasted_iota(jnp.int32, (size, 1), 0).astype(F32)
    across = lax.broadcasted_iota(jnp.int32, (1, size), 1).astype(F32)
    return down, across


def retention_kernel(spots, rates, seg_col, seg_row, q, k, v, gate, out, nrm, inverse):
    rate = rates[pl.program_id(0)]
    count = spots.shape[0]
    size = q.shape[0] // count
    down, across = decay_factors(rate, size)
    row_factor = jnp.exp(rate * down)
    for i in range(count):
        here = aligned(spots[i] * size, size)
        query = q[here, :]
        seg_here = seg_col[i * size:(i + 1) * size, :]
        total = jnp.zeros((size, v.shape[1]), F32)
        for j in range(i + 1):
            there = aligned(spots[j] * size, size)
            column_factor = jnp.exp(rate * ((i - j) * size - across))
            alive = seg_here == seg_row[:, j * size:(j + 1) * size]
            if i == j:
                alive = alive & (down >= across)
            scores = dot_nt(query, k[there, :])
            mixed = jnp.where(alive, scores * row_factor * column_factor, 0.0).astype(BF)
            total = total + dot(mixed, v[there, :])
        centered = total - jnp.mean(total, axis=1, keepdims=True)
        scale = lax.rsqrt(jnp.mean(centered * centered, axis=1, keepdims=True) + group_floor)
        normed = centered * scale
        level = gate[here, :].astype(F32)
        out[here, :] = (level / (1.0 + jnp.exp(-level)) * normed).astype(BF)
        nrm[here, :] = normed.astype(nrm.dtype)
        inverse[0, here, :] = jnp.broadcast_to(scale, (size, 128))


def retention(spots, rates, seg_col, seg_row, qk, v, gate):
    rows = qk.shape[0]
    heads = v.shape[1] // VALUE_DIM
    return pl.pallas_call(
        retention_kernel,
        grid=(heads,),
        in_specs=[smem(), smem(), full(seg_col.shape), full(seg_row.shape),
                  pl.BlockSpec((rows, KEY_DIM), lambda h: (0, h)),
                  pl.BlockSpec((rows, KEY_DIM), lambda h: (0, h + heads)),
                  pl.BlockSpec((rows, VALUE_DIM), lambda h: (0, h)),
                  pl.BlockSpec((rows, VALUE_DIM), lambda h: (0, h))],
        out_specs=[pl.BlockSpec((rows, VALUE_DIM), lambda h: (0, h)),
                   pl.BlockSpec((rows, VALUE_DIM), lambda h: (0, h)),
                   pl.BlockSpec((1, rows, 128), lambda h: (h, 0, 0))],
        out_shape=[far(v.shape, BF), far(v.shape, BF),
                   far((heads, rows, 128), F32)],
        compiler_params=params(40),
        cost_estimate=estimate(2 * rows * rows * 768 * heads, 30 << 20),
        name="retention",
    )(spots, rates, seg_col, seg_row, qk, qk, *in_hbm(v, gate))


def fold_kernel(ids, act, low_in, low_out, *refs):
    pieces, (outs, low) = refs[:-5], (refs[-5:-1], refs[-1])
    step = pl.program_id(0)
    subs = pl.num_programs(0)
    width = pieces[0].shape[2]
    size = outs[0].shape[0]

    @pl.when(step == 0)
    def _():
        low[...] = dot_nt(low_in[...], act[...])

    extra = low[...].astype(BF)
    rows = act[...]
    for i, piece in enumerate(pieces):
        at = aligned(ids[i * subs + step] * width, width)
        product = (dot(rows, piece[0]) + dot_tn(extra, low_out[:, at])).astype(BF)
        for j, out in enumerate(outs):
            out[:, at] = product[j * size:(j + 1) * size]


def fold(ids, act, low_in, low_out, pieces):
    rows, depth = act.shape
    subs = pieces[0].shape[0]
    width = low_out.shape[1]
    return pl.pallas_call(
        fold_kernel,
        grid=(subs,),
        in_specs=[smem(), full(act.shape), full(low_in.shape), full(low_out.shape)]
        + [pl.BlockSpec((1,) + w.shape[1:], lambda s: (s, 0, 0)) for w in pieces],
        out_specs=[full((rows // 4, width))] * 4 + [full((low_in.shape[0], rows))],
        out_shape=[far((rows // 4, width), BF)] * 4
        + [jax.ShapeDtypeStruct((low_in.shape[0], rows), F32)],
        compiler_params=params(48),
        cost_estimate=estimate(2 * rows * depth * width, 2 * depth * width + 4 * rows * depth),
        name="fold",
    )(ids, act, low_in, low_out, *pieces)


def join_kernel(x, part0, part1, part2, gain, middle, normed):
    rows = x[...].astype(F32) + (
        part0[...].astype(F32) + part1[...].astype(F32) + part2[...].astype(F32)
    )
    inverse = lax.rsqrt(jnp.mean(rows * rows, axis=1, keepdims=True) + rms_epsilon)
    middle[...] = rows.astype(BF)
    normed[...] = (rows * inverse * gain[...]).astype(BF)


def join_rows(x, parts, gain):
    return pl.pallas_call(
        join_kernel,
        out_shape=[jax.ShapeDtypeStruct(x.shape, BF), jax.ShapeDtypeStruct(x.shape, BF)],
        compiler_params=pltpu.CompilerParams(vmem_limit_bytes=24 << 20),
        name="join_rows",
    )(x, *parts, gain)


def rms_back_kernel(rows_in, grad_in, part0, part1, part2, gain, *outs):
    rows = rows_in[...].astype(F32)
    inverse = lax.rsqrt(jnp.mean(rows * rows, axis=1, keepdims=True) + rms_epsilon)
    normed = rows * inverse
    scaled = gain[...] * (
        part0[...].astype(F32) + part1[...].astype(F32) + part2[...].astype(F32)
    )
    result = grad_in[...].astype(F32) + inverse * (
        scaled - normed * jnp.mean(scaled * normed, axis=1, keepdims=True)
    )
    for out in outs:
        out[...] = result.astype(out.dtype)


def rms_back(rows_in, grad_in, parts, gain, kinds):
    count, width = rows_in.shape
    block = pl.BlockSpec((count // 2, width), lambda i: (i, 0))
    return pl.pallas_call(
        rms_back_kernel,
        grid=(2,),
        in_specs=[block] * 5 + [full(gain.shape)],
        out_specs=[block] * len(kinds),
        out_shape=[far((count, width), kind) for kind in kinds],
        compiler_params=params(24),
        name="rms_back",
    )(rows_in, grad_in, *parts, gain)


def hidden_grad_kernel(parts, ids, low_back, low_in, *refs):
    act, pieces, (out, low) = refs[:parts], refs[parts:-2], refs[-2:]

    @pl.when(pl.program_id(0) == 0)
    def _():
        low[...] = low_rows(low_back[...], act).astype(BF)

    weights = jnp.concatenate([w[s] for w in pieces for s in range(w.shape[0])], axis=1)
    out[...] = dot_nt(columns(act, ids), weights) + dot_tn(low[...], low_in[...])


def hidden_grad(ids, act, low_back, low_in, pieces):
    rows, depth = row_count(act), act[0].shape[1]
    width = pieces[0].shape[1]
    block = 256
    return pl.pallas_call(
        partial(hidden_grad_kernel, len(act)),
        grid=(width // block,),
        in_specs=[smem(), full(low_back.shape),
                  pl.BlockSpec((low_in.shape[0], block), lambda n: (0, n))]
        + whole(act) + [pl.BlockSpec((w.shape[0], block, w.shape[2]), lambda n: (0, n, 0)) for w in pieces],
        out_specs=[pl.BlockSpec((rows, block), lambda n: (0, n)),
                   full((low_back.shape[0], rows))],
        out_shape=[jax.ShapeDtypeStruct((rows, width), F32),
                   jax.ShapeDtypeStruct((low_back.shape[0], rows), BF)],
        compiler_params=params(40),
        cost_estimate=estimate(2 * rows * depth * width, 2 * depth * width + 8 * rows * depth),
        name="hidden_grad",
    )(ids, low_back, low_in, *act, *pieces)


def mlp_kernel(parts, count, ids, low_in, gate_out, up_out, down_in, grad, grad_low, *refs):
    act, refs = refs[:parts], refs[parts:]
    gate_pieces, up_pieces = refs[:count], refs[count:2 * count]
    hid, dgate, dup, low, lows, grad_hidden, grad_down = refs[2 * count:]

    @pl.when(pl.program_id(0) == 0)
    def _():
        low[...] = low_rows(low_in[...], act).astype(BF)
        lows[...] = jnp.zeros(lows.shape, F32)

    rows = columns(act, ids)
    extra = low[...]
    gate = dot(rows, stacked(gate_pieces)) + dot_tn(extra, gate_out[...])
    up = dot(rows, stacked(up_pieces)) + dot_tn(extra, up_out[...])
    chance = 0.5 * (1.0 + lax.erf(gate * (0.5**0.5)))
    active = gate * chance
    slope = chance + gate * (jnp.exp(-0.5 * gate * gate) * 0.3989422804014327)
    hidden = (active * up).astype(BF)
    back = grad[...]
    back_gate = (back * up * slope).astype(BF)
    back_up = (back * active).astype(BF)
    hid[...] = hidden
    dgate[...] = back_gate
    dup[...] = back_up
    lows[:RANK, :] += dot_nt(down_in[...], hidden)
    lows[RANK:, :] += dot_nt(gate_out[...], back_gate) + dot_nt(up_out[...], back_up)
    grad_hidden[:RANK, :] = dot(extra[:RANK], back_gate).astype(BF)
    grad_hidden[RANK:, :] = dot(extra[RANK:], back_up).astype(BF)
    grad_down[...] = dot(grad_low[...], hidden).astype(BF)


def mlp(ids, act, low_in, gate_out, up_out, down_in, grad, grad_low, gate_pieces, up_pieces):
    rows, depth = row_count(act), act[0].shape[1]
    width = gate_pieces[0].shape[2]
    block = 256
    ranks = low_in.shape[0]
    column = lambda height: pl.BlockSpec((height, block), lambda n: (0, n))
    return pl.pallas_call(
        partial(mlp_kernel, len(act), len(gate_pieces)),
        grid=(width // block,),
        in_specs=[smem(), full(low_in.shape), column(ranks), column(ranks),
                  column(down_in.shape[0]), column(rows), full(grad_low.shape)]
        + whole(act) + piece_specs(gate_pieces, block) + piece_specs(up_pieces, block),
        out_specs=[column(rows), column(rows), column(rows), full((ranks, rows)),
                   full((ranks + RANK, rows)), column(ranks), column(grad_low.shape[0])],
        out_shape=[jax.ShapeDtypeStruct((rows, width), BF)] * 3
        + [jax.ShapeDtypeStruct((ranks, rows), BF),
           jax.ShapeDtypeStruct((ranks + RANK, rows), F32),
           jax.ShapeDtypeStruct((ranks, width), BF),
           jax.ShapeDtypeStruct((grad_low.shape[0], width), BF)],
        compiler_params=params(48),
        cost_estimate=estimate(4 * rows * depth * width, 4 * depth * width + 8 * rows * depth),
        name="mlp",
    )(ids, low_in, gate_out, up_out, down_in, grad, grad_low, *act, *gate_pieces, *up_pieces)


def unfold_kernel(layout, ids, low_in, *refs):
    blocks, count, weights = layout
    lows, refs = refs[:blocks], refs[blocks:]
    acts, pieces, outs = refs[:blocks * count], refs[blocks * count:-blocks], refs[-blocks:]
    size = outs[0].shape[0]
    step = pl.program_id(0)
    subs = pl.num_programs(0)
    width = pieces[0].shape[1]
    extra = jnp.concatenate([low[...] for low in lows], axis=1).T.astype(BF)
    per = len(pieces) // weights
    rows = jnp.concatenate(
        [jnp.concatenate([act[...] for act in acts[i * count:(i + 1) * count]], axis=1)
         for i in range(blocks)], axis=0
    )
    for i in range(per):
        at = aligned(ids[i * subs + step] * width, width)
        weight = jnp.concatenate([pieces[k * per + i][0] for k in range(weights)], axis=1)
        product = (dot_nt(rows, weight) + dot(extra, low_in[:, at])).astype(BF)
        for j, out in enumerate(outs):
            out[:, at] = product[j * size:(j + 1) * size]


def unfold(ids, acts, low, low_in, weights, size, blocks):
    subs = weights[0][0].shape[0]
    width = low_in.shape[1]
    pieces = [piece for weight in weights for piece in weight]
    depth = sum(act.shape[1] for act in acts)
    count = len(blocks)
    return pl.pallas_call(
        partial(unfold_kernel, (count, len(acts), len(weights))),
        grid=(subs,),
        in_specs=[smem(), full(low_in.shape)]
        + [pl.BlockSpec((low.shape[0], size), lambda s, at=at: (0, at)) for at in blocks]
        + [pl.BlockSpec((size, act.shape[1]), lambda s, at=at: (at, 0))
           for at in blocks for act in acts]
        + [pl.BlockSpec((1,) + w.shape[1:], lambda s: (s, 0, 0)) for w in pieces],
        out_specs=[full((size, width))] * count,
        out_shape=[far((size, width), BF)] * count,
        compiler_params=params(48),
        cost_estimate=estimate(
            2 * count * size * depth * width, 2 * depth * width + 4 * count * size * depth
        ),
        name="unfold",
    )(ids, low_in, *[low] * count, *in_hbm(*list(acts) * count, *pieces))


def gate_back_kernel(parts, ids, low_back, low_in, gate, nrm, inverse, hold, low_gate, low_out,
                     *refs):
    act, pieces = refs[:parts], refs[parts:-6]
    dgate, dret, low, dlow, grad_in, grad_gate = refs[-6:]

    @pl.when(pl.program_id(0) == 0)
    def _():
        low[...] = low_rows(low_back[...], act).astype(BF)
        dlow[...] = jnp.zeros(dlow.shape, F32)

    weights = jnp.concatenate([w[s] for w in pieces for s in range(w.shape[0])], axis=1)
    back = dot_nt(columns(act, ids), weights) + dot_tn(low[...], low_in[...])
    level = gate[...].astype(F32)
    normed = nrm[...].astype(F32)
    chance = 1.0 / (1.0 + jnp.exp(-level))
    slope = chance * (1.0 + level * (1.0 - chance))
    back_gate = (back * normed * slope).astype(BF)
    grad = back * (level * chance)
    mean = jnp.mean(grad, axis=1, keepdims=True)
    along = jnp.mean(grad * normed, axis=1, keepdims=True)
    dgate[...] = back_gate
    dret[...] = (inverse[0, :, :1] * (grad - mean - normed * along)).astype(BF)
    grad_in[...] = dot(low[...], hold[...]).astype(BF)
    grad_gate[...] = dot(low_gate[...], back_gate).astype(BF)
    dlow[...] += dot_nt(low_out[...], back_gate)


def gate_back(ids, act, low_back, low_in, gate, nrm, inverse, hold, low_gate, low_out, pieces):
    rows, depth = row_count(act), act[0].shape[1]
    width = gate.shape[1]
    block = VALUE_DIM
    ranks = low_back.shape[0]
    column = lambda height: pl.BlockSpec((height, block), lambda n: (0, n))
    return pl.pallas_call(
        partial(gate_back_kernel, len(act)),
        grid=(width // block,),
        in_specs=[smem(), full(low_back.shape), column(ranks), column(rows),
                  column(rows), pl.BlockSpec((1, rows, 128), lambda n: (n, 0, 0)), column(rows),
                  pl.BlockSpec((ranks, rows), lambda n: (low_gate.shape[0] // ranks - 1, 0)),
                  column(low_out.shape[0])]
        + whole(act) + [pl.BlockSpec((w.shape[0], block, w.shape[2]), lambda n: (0, n, 0)) for w in pieces],
        out_specs=[column(rows), column(rows), full((ranks, rows)),
                   full((low_out.shape[0], rows)), column(ranks), column(ranks)],
        out_shape=[jax.ShapeDtypeStruct((rows, width), BF)] * 2
        + [jax.ShapeDtypeStruct((ranks, rows), BF),
           jax.ShapeDtypeStruct((low_out.shape[0], rows), F32),
           jax.ShapeDtypeStruct((ranks, width), BF), jax.ShapeDtypeStruct((ranks, width), BF)],
        compiler_params=params(56),
        cost_estimate=estimate(2 * rows * depth * width, 2 * depth * width + 16 * rows * width),
        name="gate_back",
    )(ids, low_back, low_in, *in_hbm(gate, nrm, inverse, hold), low_gate, low_out, *act, *pieces)


def retention_back_kernel(spots, rates, seg_col, seg_row, cosine, sine_table, low, begin, q_out,
                          k_out, v_out, q, k, v, dret, dq, dk, dv, dlow, grad_q, grad_k, grad_v,
                          sums):
    head = pl.program_id(0)
    rate = rates[head]
    count = spots.shape[0]
    size = q.shape[0] // count
    down, across = decay_factors(rate, size)
    column_factor = jnp.exp(rate * across)
    key_scale = 1.0 / KEY_DIM**0.5

    @pl.when(head == 0)
    def _():
        dlow[...] = begin[...]

    sums[...] = jnp.zeros(sums.shape, F32)
    for j in range(count):
        there = aligned(spots[j] * size, size)
        place = slice(j * size, (j + 1) * size)
        key, value = k[there, :], v[there, :]
        seg_there = seg_col[place, :]
        key_sum = jnp.zeros((size, KEY_DIM), F32)
        value_sum = jnp.zeros((size, VALUE_DIM), F32)
        for i in range(j, count):
            here = aligned(spots[i] * size, size)
            query, back = q[here, :], dret[here, :]
            row_factor = jnp.exp(rate * ((i - j) * size - down))
            alive = seg_there == seg_row[:, i * size:(i + 1) * size]
            if i == j:
                alive = alive & (across >= down)
            weight = jnp.where(alive, row_factor * column_factor, 0.0)
            mixed = (dot_nt(key, query) * weight).astype(BF)
            grad = (dot_nt(value, back) * weight).astype(BF)
            value_sum = value_sum + dot(mixed, back)
            key_sum = key_sum + dot(grad, query)
            sums[i * size:(i + 1) * size, :] += dot_tn(grad, key)
        dk[there, :] = (
            key_scale * unrotated(key_sum, cosine[place, :], sine_table[place, :])
        ).astype(BF)
        dv[there, :] = value_sum.astype(BF)
    for i in range(count):
        place = slice(i * size, (i + 1) * size)
        dq[aligned(spots[i] * size, size), :] = unrotated(
            sums[place, :], cosine[place, :], sine_table[place, :]
        ).astype(BF)
    back_q, back_k, back_v = dq[...], dk[...], dv[...]
    dlow[...] += (
        dot_nt(q_out[...], back_q) + dot_nt(k_out[...], back_k) + dot_nt(v_out[...], back_v)
    )
    grad_q[...] = dot(low[:RANK, :], back_q).astype(BF)
    grad_k[...] = dot(low[RANK:2 * RANK, :], back_k).astype(BF)
    grad_v[...] = dot(low[2 * RANK:3 * RANK, :], back_v).astype(BF)


def retention_back(spots, rates, seg_col, seg_row, cosine, sine_table, low, begin, qk_out, v_out,
                   qk, v, dret):
    rows = qk.shape[0]
    heads = v.shape[1] // VALUE_DIM
    ranks = low.shape[0]
    key = lambda height: pl.BlockSpec((height, KEY_DIM), lambda h: (0, h))
    later = lambda height: pl.BlockSpec((height, KEY_DIM), lambda h: (0, h + heads))
    value = lambda height: pl.BlockSpec((height, VALUE_DIM), lambda h: (0, h))
    keys = heads * KEY_DIM
    return pl.pallas_call(
        retention_back_kernel,
        grid=(heads,),
        in_specs=[smem(), smem(), full(seg_col.shape), full(seg_row.shape), full(cosine.shape),
                  full(cosine.shape), full(low.shape), full(begin.shape), key(ranks),
                  later(ranks), value(ranks),
                  key(rows), later(rows), value(rows), value(rows)],
        out_specs=[key(rows), key(rows), value(rows), full((ranks, rows)), key(RANK), key(RANK),
                   value(RANK)],
        out_shape=[jax.ShapeDtypeStruct((rows, keys), BF), jax.ShapeDtypeStruct((rows, keys), BF),
                   jax.ShapeDtypeStruct(v.shape, BF), jax.ShapeDtypeStruct((ranks, rows), F32),
                   jax.ShapeDtypeStruct((RANK, keys), BF), jax.ShapeDtypeStruct((RANK, keys), BF),
                   jax.ShapeDtypeStruct((RANK, v.shape[1]), BF)],
        scratch_shapes=[pltpu.VMEM((rows, KEY_DIM), F32)],
        compiler_params=params(48),
        cost_estimate=estimate(2 * rows * rows * 1792 * heads, 30 << 20),
        name="retention_back",
    )(spots, rates, seg_col, seg_row,
      cosine, sine_table, low, begin, qk_out, qk_out, v_out, qk, qk, v, dret)


def share_kernel(heights, low, *refs):
    out = refs[-1]
    at, first = 0, 0
    for height, parts in heights:
        total = jnp.zeros((height, out.shape[2]), F32)
        begin = 0
        for ref in refs[first:first + parts]:
            end = begin + ref.shape[0]
            total = total + dot(low[at:at + height, begin:end], ref[...])
            begin = end
        out[0, at:at + height, :] = total.astype(BF)
        at, first = at + height, first + parts


def share(low, span, items):
    acts = [array for _, act in items for array in act]
    heights = tuple((height, len(act)) for height, act in items)
    count = acts[0].shape[1] // span
    made = pl.pallas_call(
        partial(share_kernel, heights),
        grid=(count,),
        in_specs=[full(low.shape)]
        + [pl.BlockSpec((act.shape[0], span), lambda i: (0, i)) for act in acts],
        out_specs=pl.BlockSpec((1, low.shape[0], span), lambda i: (i, 0, 0)),
        out_shape=jax.ShapeDtypeStruct((count, low.shape[0], span), BF),
        compiler_params=params(32),
        cost_estimate=estimate(0, 0),
        name="share",
    )(low, *in_hbm(*acts))
    return made.reshape(count * low.shape[0], span)


def place_kernel(layout, arrays, order, *refs):
    packs, outs = refs[:arrays], refs[arrays:]
    pack = packs[0][0]
    if arrays == 2:
        which = order[pl.program_id(0)] >= order[pl.num_programs(0)]
        pack = jnp.where(which, packs[1][0], pack)
    span = pack.shape[1]
    for (begin, height, kind, stride), out in zip(layout, outs):
        if kind == "shares":
            for j in range(out.shape[2] // span):
                rows = pack[begin + stride * j:begin + stride * j + height]
                out[0, :, j * span:(j + 1) * span] = rows.astype(F32)
            continue
        for j in range(2):
            rows = pack[begin + stride * j:begin + stride * j + height].astype(F32)
            if kind == "halves":
                out[0, :, j * span:(j + 1) * span] = rows
            else:
                out[0, j] = rows


def place(order, arrays, layout, shares):
    entries = order.shape[0]
    size, _, span = arrays[0].shape
    shapes = []
    for _, height, kind, _ in layout:
        shapes.append({"shares": (height, shares * span),
                       "halves": (height, 2 * span)}.get(kind, (2, height, span)))

    def spec(number):
        def index(e, o):
            return (jnp.clip(o[e] - number * size, 0, size - 1), 0, 0)
        return pl.BlockSpec((1,) + arrays[0].shape[1:], index)

    order = jnp.concatenate([order, jnp.full((1,), size, jnp.int32)])
    return pl.pallas_call(
        partial(place_kernel, layout, len(arrays)),
        grid_spec=pltpu.PrefetchScalarGridSpec(
            num_scalar_prefetch=1,
            grid=(entries,),
            in_specs=[spec(number) for number in range(len(arrays))],
            out_specs=[
                pl.BlockSpec((1,) + shape, lambda e, o, n=len(shape): (e,) + (0,) * n)
                for shape in shapes
            ],
        ),
        out_shape=[jax.ShapeDtypeStruct((entries,) + shape, F32) for shape in shapes],
        compiler_params=params(32),
        cost_estimate=estimate(0, 10 << 20),
        name="place",
    )(order, *in_hbm(*arrays))


def after(x, *others):
    return lax.optimization_barrier((x,) + others)[0]


class PlainLinks:
    def __init__(self, ndp, nt):
        self.ndp, self.nt = ndp, nt
        self.rank = lax.axis_index("tensor")
        self.chunks = jnp.arange(nt, dtype=jnp.int32)
        self.spots = self.chunks
        self.row_ids = jnp.zeros((1,), jnp.int32)

    def exchange(self, x):
        return x

    def mine(self, own, other):
        return own

    def gather(self, x):
        return [lax.all_gather(x, "tensor", axis=0, tiled=True)]

    def scatter(self, rows):
        total = lax.psum_scatter(
            jnp.concatenate(rows, axis=0), "tensor", scatter_dimension=0, tiled=True
        )
        zero = jnp.zeros_like(total)
        return (total, zero, zero)

    def forward(self, shards, tokens, cotangent, line, steps):
        blocks = [
            [lax.all_gather(shard, "dp", axis=int(shard.shape[1] * self.ndp == tokens.shape[1]),
                            tiled=True)[None]]
            for shard in shards
        ]
        steps.ready(line, steps.tables(line, line)[0])
        a = self.gather(steps.norm(tokens))
        dy = self.gather(cotangent)
        projected = steps.project(a, *blocks[:2])
        mixed = steps.mix(a, *projected, blocks[2])
        *rows, low = steps.fold(mixed[0], blocks[3])
        middle, b = steps.join(tokens, self.scatter(rows))
        dhid = steps.hidden_grad(dy, blocks[4])
        return (blocks, tokens, a, cotangent, dy, projected, mixed, low, middle,
                self.gather(b), dhid)

    def group_sum(self, x):
        return lax.psum(x.astype(BF), "tensor")

    def backward(self, steps):
        steps.mlp()
        dz = self.gather(steps.dz(self.scatter(steps.unfold_mlp(256, (0, 1, 2, 3)))))
        output = steps.output(self.scatter(steps.fold_down(steps.hid)))
        early = lax.all_gather(steps.early(self.group_sum(steps.lows)), "dp")
        early = steps.place_early(early)
        steps.gate_back(dz)
        steps.retention_back(steps.dret)
        late = lax.all_gather(steps.late(self.group_sum(steps.late_lows()), dz), "dp")
        late = steps.place_late([late], jnp.arange(self.ndp, dtype=jnp.int32))
        parts = self.scatter(steps.unfold_attn(256, (0, 1, 2, 3)))
        dx, _ = steps.dx(parts)
        return output, dx, early, late


class PairedLinks:
    def __init__(self, ndp, nt):
        self.ndp, self.nt = ndp, nt
        d, t = lax.axis_index("dp"), lax.axis_index("tensor")
        c, p, m = d % 2, t // 2, t % 2
        self.home = c == p
        self.rank = 2 * c + m
        flips = jnp.array([0, 2, 1, 3], jnp.int32)
        self.chunks = self.rank ^ flips
        order = jnp.arange(4, dtype=jnp.int32) ^ self.rank
        self.spots = (order % 2) * 2 + order // 2
        g = d // 2
        self.row_ids = ((2 * (g ^ jnp.arange(4, dtype=jnp.int32))[:, None]
                         + jnp.arange(2, dtype=jnp.int32)[None, :]) ^ c).reshape(-1)
        self.last = {}
        self.last_round = ()
        self.slow = ()

    def pairs(self, place):
        listed = []
        for d in range(self.ndp):
            for t in range(self.nt):
                to = place(d, t)
                if to is not None:
                    listed.append((d * self.nt + t, to[0] * self.nt + to[1]))
        return listed

    def move(self, x, place, chain=None):
        if chain in self.last:
            x = after(x, *self.last[chain])
        moved = lax.ppermute(x, ("dp", "tensor"), self.pairs(place))
        if chain is not None:
            self.last[chain] = (moved,)
        return moved

    def send(self, moves):
        return [lax.ppermute(x, ("dp", "tensor"), self.pairs(place)) for x, place in moves]

    def round(self, moves, work=None, inputs=(), later=(), slow=(), feed=0):
        every = list(moves) + list(slow)
        values = [x for x, _ in every]
        flat, form = jax.tree.flatten((values, inputs))
        last, _ = jax.tree.flatten(self.last_round)
        if last:
            flat = lax.optimization_barrier((*flat, *last))[:len(flat)]
        values, inputs = jax.tree.unflatten(form, flat)
        moved = self.send([(x, place) for x, (_, place) in zip(values, every)])
        moved, slowly = moved[:len(moves)], moved[len(moves):]
        second = []
        if later:
            count, make = later
            moves = make(moved[:count])
            values = [x for x, _ in moves]
            values = lax.optimization_barrier((*values, *moved[:count]))[:len(values)]
            second = self.send([(x, place) for x, (_, place) in zip(values, moves)])
        made = work(*moved[:feed], *inputs) if work is not None else ()
        self.last_round = (moved, second, made, self.slow)
        self.slow = slowly
        return moved + slowly, second, made

    def core(self, x):
        return self.move(x, lambda d, t: (d ^ 1, t))

    def pair(self, x):
        return self.move(x, lambda d, t: (d, t ^ 1), "pair")

    def mine(self, own, other):
        return jnp.where(self.home, own, other)

    def exchange(self, x):
        moved = self.move(
            x, lambda d, t: (d ^ 1, t ^ 2) if d % 2 != t // 2 else None, "middle"
        )
        return jnp.where(self.home, x, moved)

    def gather(self, x):
        across = self.pair(x)
        return [x, self.core(x), across, self.core(across)]

    def forward(self, shards, tokens, cotangent, line, steps):
        by_one = lambda d, t: (d ^ 2, t)
        by_two = lambda d, t: (d ^ 4, t)
        core = lambda d, t: (d ^ 1, t)
        pair = lambda d, t: (d, t ^ 1)
        swap = lambda d, t: (d ^ 1, t ^ 2) if d % 2 != t // 2 else None
        seat = lambda d, t: (d, t ^ 2) if d % 2 == t // 2 else None
        blocks = [[None] * 4 for _ in shards]
        doubled = [jnp.stack([shards[0], self.core(shards[0])])]

        def over(i):
            return (doubled[i], seat)

        def arrived(i, moved):
            blocks[i][0] = self.mine(doubled[i], moved)

        hops = {
            "x": lambda i: (blocks[i][0], by_one),
            "y": lambda i: (blocks[i][0], by_two),
            "xy": lambda i: (blocks[i][1], by_two),
            "yx": lambda i: (blocks[i][2], by_one),
        }
        place_of = {"x": 1, "y": 2, "xy": 3, "yx": 3}

        def go(first, second, others, work=None, inputs=()):
            def later(moved):
                for (i, way), block in zip(first, moved):
                    blocks[i][place_of[way]] = block
                return [hops[way](i) for i, way in second]

            moved, seconds, made = self.round(
                [hops[way](i) for i, way in first] + list(others), work, inputs,
                (len(first), later)
            )
            for (i, way), block in zip(second, seconds):
                blocks[i][place_of[way]] = block
            return moved[len(first):], made

        def double(rest):
            return [jnp.stack([shard, self.core(shard)]) for shard in rest]

        other = self.core(line)
        (moved,), made = go([], [], [over(0)], double, (shards[1:],))
        doubled += made
        arrived(0, moved)
        (moved,), (home_table, sent_table) = go(
            [(0, "x"), (0, "y")], [], [over(1)], steps.tables, (line, other)
        )
        arrived(1, moved)
        (x, table, moved), _ = go([(1, "x"), (0, "xy")], [(1, "y")],
                                  [(tokens, swap), (sent_table, seat), over(2)])
        arrived(2, moved)
        x = self.mine(tokens, x)
        steps.ready(other, self.mine(home_table, table))
        a = steps.norm(x)
        (across, moved, grad), _ = go([(2, "x"), (2, "y")], [(1, "yx"), (2, "xy")],
                                      [(a, pair), over(3), (cotangent, swap)])
        arrived(3, moved)
        grad = self.mine(cotangent, grad)
        def attend(near, beyond, own, across, *weights):
            a = [own, near, across, beyond]
            return a, steps.project(a, *weights)

        moves = [(a, core), (across, core), hops["x"](3), hops["y"](3), over(4)]
        moved, _, (a, projected) = self.round(
            moves, attend, (a, across, *blocks[:2]), feed=2
        )
        _, _, blocks[3][1], blocks[3][2], moved = moved
        arrived(4, moved)
        half = grad.shape[0] // 2
        (moved, across0), mixed = go(
            [(4, "x"), (3, "xy")], [], [over(5), (grad[:half], pair)], steps.mix,
            (a, *projected, blocks[2])
        )
        arrived(5, moved)
        (moved, across1), folded = go(
            [(5, "x"), (4, "y")], [], [over(6), (grad[half:], pair)], steps.fold,
            (mixed[0], blocks[3])
        )
        across = jnp.concatenate([across0, across1])
        arrived(6, moved)
        own, near, far, beyond, low = folded
        moves = [(near, core), (beyond, core), hops["yx"](4), hops["y"](5)]
        moved, (far,), _ = self.round(
            moves, later=(2, lambda moved: [(self.add(far, moved[1]), pair)])
        )
        near, _, blocks[4][3], blocks[5][2] = moved
        middle, b = steps.join(x, (own, near, far))
        (far, near_grad, beyond_grad), _ = go([(6, "x"), (6, "y")], [],
                                              [(b, pair), (grad, core), (across, core)])
        dy = [grad, near_grad, across, beyond_grad]
        (near, beyond), dhid = go([(5, "yx"), (6, "xy")], [], [(b, core), (far, core)],
                                  steps.hidden_grad, (dy, blocks[4]))
        b = [b, near, far, beyond]
        return blocks, x, a, grad, dy, projected, mixed, low, middle, b, dhid

    def add(self, one, two):
        return (one.astype(F32) + two.astype(F32)).astype(BF)

    def core_sum(self, x, other):
        size = x.shape[1] // 4
        other = other.astype(F32)
        return (x + jnp.concatenate(
            [other[:, i * size:(i + 1) * size] for i in (1, 0, 3, 2)], axis=1
        )).astype(BF)

    def pair_sum(self, x, other):
        size = x.shape[1] // 2
        other = jnp.concatenate([other[:, size:], other[:, :size]], axis=1)
        return (x.astype(F32) + other.astype(F32)).astype(BF)

    def backward(self, steps):
        pair = lambda d, t: (d, t ^ 1)
        swap = lambda d, t: (d ^ 1, t ^ 2) if d % 2 != t // 2 else None
        by_one = lambda d, t: (d ^ 2, t)
        by_two = lambda d, t: (d ^ 4, t)
        core = lambda d, t: (d ^ 1, t)

        self.last_round = ()
        steps.mlp()
        (lows,), _, (near, far, beyond) = self.round(
            [(steps.lows.astype(BF), core)],
            lambda dup: steps.unfold_mlp(256, (1, 2, 3), dup), (steps.dup,)
        )
        lows = self.core_sum(steps.lows, lows)
        (beyond, near, other), _, _ = self.round([(beyond, core), (near, core), (lows, pair)])
        far = self.add(far, beyond)
        half = far.shape[0] // 2
        lows = self.pair_sum(lows, other)
        (far,), _, ((own,), folded, early) = self.round(
            [(far, pair)],
            lambda dup, hid, lows: (steps.unfold_mlp(256, (0,), dup), steps.fold_down(hid),
                                    steps.early(lows)),
            (steps.dup, steps.hid, lows)
        )
        own_out, near_out, far_out, beyond_out = folded
        dz = steps.dz((own, near, far))

        (_, across, moved, dz_near, near_out), _, far_out = self.round(
            [(beyond_out, core), (dz, pair), (early, swap), (dz, core), (near_out, core)],
            self.add, (far_out,), feed=1
        )
        early = lax.all_gather(self.mine(early, moved), "dp")
        (dz_beyond,), _, _ = self.round([(across, core)])
        dz = [dz, dz_near, across, dz_beyond]
        (far_out,), _, dret = self.round([], steps.gate_back, (dz,), slow=[(far_out, pair)])
        _, _, dpv = self.round([], steps.retention_back, (dret,))
        output = steps.output((own_out, near_out, far_out))

        (dlow, out0), _, (far, beyond) = self.round(
            [(steps.late_lows().astype(BF), core), (output[:half], swap)],
            lambda dpv: steps.unfold_attn(256, (2, 3), dpv), (dpv,)
        )
        dlow = self.core_sum(steps.late_lows(), dlow)
        def beside(other, dpv, dlow):
            near, = steps.unfold_attn(256, (1,), dpv)
            return near, steps.late(self.pair_sum(dlow, other), dz)

        (_, beyond, out1), _, (near, late) = self.round(
            [(dlow, pair), (beyond, core), (output[half:], swap)], beside, (dpv, dlow), feed=1
        )
        far = self.add(far, beyond)
        (far0, near, moved), _, (own,) = self.round(
            [(far[:half], pair), (near, core), (late, swap)],
            lambda dpv: steps.unfold_attn(256, (0,), dpv), (dpv,)
        )
        late = self.mine(late, moved)
        size = late.shape[0] // 2
        late = [late[:size][None], late[size:][None]]
        three = half + half // 2
        (one, two, far1), _, _ = self.round(
            [(late[0], by_one), (late[1], by_two), (far[half:three], pair)]
        )
        late = [jnp.concatenate([late[0], one]), jnp.concatenate([late[1], two])]
        (one, two, far2), _, _ = self.round(
            [(late[0], by_two), (late[1], by_one), (far[three:], pair)]
        )
        dx, low = steps.dx((own, near, jnp.concatenate([far0, far1, far2])))
        late = jnp.concatenate(
            [jnp.concatenate([late[0], one]),
             jnp.concatenate([late[1][:1], two[:1], late[1][1:], two[1:]])], axis=1
        )
        apart = jnp.arange(self.ndp, dtype=jnp.int32) ^ lax.axis_index("dp")

        def put(other, late, early):
            early = steps.place_early(early)
            return early, steps.place_late([late, other], apart // 2 + 4 * (apart % 2))

        (_, moved), _, (early, late) = self.round(
            [(late, core), (low, swap)], put, (late, early), feed=1
        )
        moved, early, late = lax.optimization_barrier((moved, early, late))
        return (self.mine(output, jnp.concatenate([out0, out1])),
                self.mine(dx, moved.astype(F32)), early, late)


def rotation_tables(seq_length, half_dim):
    positions = jnp.arange(seq_length, dtype=jnp.float32)
    frequency = jnp.exp(-jnp.log(10000.0) * jnp.arange(half_dim, dtype=jnp.float32) / half_dim)
    angles = positions[:, None] * frequency[None, :]
    return (jnp.cos(angles), jnp.sin(angles))


def shards(
    ndp,
    nt,
    tokens,
    cotangent,
    adapter_ids,
    segments,
    norm_attn,
    norm_mlp,
    weight_query,
    weight_key,
    weight_value,
    weight_gate,
    weight_out,
    weight_mlp_gate,
    weight_mlp_up,
    weight_mlp_down,
    adapt_attn_in,
    adapt_query_key,
    adapt_value_gate,
    adapt_out_in,
    adapt_out_back,
    adapt_mlp_in,
    adapt_mlp_hidden,
    adapt_down_in,
    adapt_down_back,
):
    links = PairedLinks(ndp, nt) if (ndp, nt) == (8, 4) else PlainLinks(ndp, nt)
    rank, chunks, spots, ids = links.rank, links.chunks, links.spots, links.row_ids
    adapters = adapt_attn_in.shape[0]
    depth = tokens.shape[2]
    seq_length = segments.shape[1]
    gain_attn, gain_mlp = norm_attn[None], norm_mlp[None]

    def pick(table, which):
        return lax.dynamic_index_in_dim(table, which, 0, keepdims=False)

    def packed(which):
        qk, vg = pick(adapt_query_key, which), pick(adapt_value_gate, which)
        return jnp.concatenate(
            [jnp.concatenate([qk[0], qk[1]], axis=1), vg[0], vg[1],
             pick(adapt_mlp_hidden, which).reshape(2 * RANK, -1),
             pick(adapt_out_in, which).T, pick(adapt_down_in, which).T], axis=0
        )

    own_id = adapter_ids[0, 0]
    own_line = jnp.concatenate([segments, jnp.broadcast_to(adapter_ids, (1, 128))], axis=1)
    wide = weight_gate.shape[1]
    keys = adapt_query_key.shape[3]
    heads_local = wide // VALUE_DIM
    head_ids = (rank * heads_local + jnp.arange(heads_local, dtype=jnp.int32)).astype(F32)
    rates = jnp.log(1.0 - jnp.exp2(-5.0 - head_ids))
    cosine, sine_table = rotation_tables(seq_length, HALF)

    class Steps:
        def tables(self, line, other):
            return packed(line[0, seq_length]), packed(other[0, seq_length])

        def ready(self, other, table):
            line = links.mine(own_line, other)
            self.work_id = work_id = line[0, seq_length]
            self.seg_row = line[:, :seq_length]
            self.seg_col = self.seg_row.reshape(seq_length, 1)
            blank = jnp.zeros((RANK, wide), BF)
            left = jnp.arange(wide)[None, :] < keys
            zero = jnp.zeros((), BF)
            self.qk_out = jnp.concatenate([jnp.where(left, table[:RANK], zero),
                                           jnp.where(left, zero, table[:RANK]), blank, blank])
            self.v_out = jnp.concatenate([blank, blank, table[RANK:2 * RANK], blank])
            self.g_out = jnp.concatenate([blank, blank, blank, table[2 * RANK:3 * RANK]])
            self.mg_out = jnp.concatenate([table[3 * RANK:4 * RANK], blank])
            self.mu_out = jnp.concatenate([blank, table[4 * RANK:5 * RANK]])
            self.out_in = table[5 * RANK:6 * RANK]
            self.down_in = table[6 * RANK:7 * RANK]
            self.attn_in = pick(adapt_attn_in, work_id).T
            self.out_back = pick(adapt_out_back, work_id)
            self.mlp_in = pick(adapt_mlp_in, work_id).T
            self.down_back = pick(adapt_down_back, work_id)

        def norm(self, x):
            return norm_rows(x, gain_attn)

        def project(self, a, w_qk, w_v):
            return project(
                ids, chunks, a, self.attn_in, jnp.concatenate([self.qk_out, self.v_out], axis=1),
                (w_qk, w_v), (cosine, sine_table)
            )

        def mix(self, a, qk, v, low, w_g):
            gate, = project(ids, chunks, a, low, self.g_out, (w_g,), ())
            return (*retention(spots, rates, self.seg_col, self.seg_row, qk, v, gate), gate)

        def fold(self, o, w_o):
            return fold(ids, o, self.out_in, self.out_back, w_o)

        def join(self, x, parts):
            return join_rows(x, parts, gain_mlp)

        def hidden_grad(self, dy, w_d):
            return hidden_grad(ids, dy, self.down_back, self.down_in, w_d)

    steps = Steps()
    ((w_qk, w_v, w_g, w_o, w_d, w_mg, w_mu), x, a, grad, dy, (qk, v, low_a),
     (o, nrm, inverse, gate), low_o, middle, b, (dhid, low_dy)) = links.forward(
        [jnp.concatenate([weight_query, weight_key], axis=1), weight_value, weight_gate,
         weight_out, weight_mlp_down, weight_mlp_gate, weight_mlp_up],
        tokens[0], cotangent[0], own_line, steps,
    )
    seg_row, seg_col, work_id = steps.seg_row, steps.seg_col, steps.work_id
    qk_out, v_out, g_out, mg_out, mu_out = (
        steps.qk_out, steps.v_out, steps.g_out, steps.mg_out, steps.mu_out
    )
    attn_in, out_in, out_back = steps.attn_in, steps.out_in, steps.out_back
    mlp_in, down_in, down_back = steps.mlp_in, steps.down_in, steps.down_back

    span = depth // nt
    halves = lambda y: jnp.concatenate([y[:, :wide // 2], y[:, wide // 2:]])

    class Back:
        early_height = 3 * RANK
        late_height = 5 * RANK

        def mlp(self):
            (self.hid, self.dgate, self.dup, _, self.lows, self.grad_hidden,
             self.grad_down) = mlp(
                ids, b, mlp_in, mg_out, mu_out, down_in, dhid, low_dy, w_mg, w_mu
            )

        def unfold_mlp(self, size, blocks, dup=None):
            dup = self.dup if dup is None else dup
            return unfold(ids, (self.dgate, dup), self.lows[RANK:], mlp_in, (w_mg, w_mu),
                          size, blocks)

        def dz(self, parts):
            self.dmid, = rms_back(middle, grad, parts, gain_mlp, (BF,))
            return self.dmid

        def fold_down(self, hid):
            return fold(ids, hid, down_in, down_back, w_d)[:4]

        def output(self, parts):
            return (middle.astype(F32) + (
                parts[0].astype(F32) + parts[1].astype(F32) + parts[2].astype(F32)
            )).astype(BF)

        def early(self, lows):
            mark = jnp.full((RANK, span), work_id, F32).astype(BF)
            return jnp.concatenate(
                [share(lows, span, ((RANK, dy), (2 * RANK, b))),
                 halves(jnp.concatenate([self.grad_hidden, self.grad_down])), mark]
            )

        def gate_back(self, dz):
            (self.dpg, self.dret, _, self.dlow, self.grad_out_in, self.grad_gate) = gate_back(
                ids, dz, out_back, out_in, gate, nrm, inverse, o, low_a, g_out, w_o
            )
            return self.dret

        def late_lows(self):
            return jnp.concatenate([self.dlow, low_o])

        def retention_back(self, dret):
            (self.dpq, self.dpk, self.dpv, self.dlow, self.grad_q, self.grad_k,
             self.grad_v) = retention_back(
                spots, rates, seg_col, seg_row, cosine, sine_table, low_a, self.dlow, qk_out,
                v_out, qk, v, dret
            )
            return self.dpv

        def late(self, lows, dz):
            return jnp.concatenate(
                [share(lows, span, ((4 * RANK, a), (RANK, dz))),
                 halves(jnp.concatenate(
                     [jnp.concatenate([self.grad_q, self.grad_k], axis=1), self.grad_v,
                      self.grad_gate, self.grad_out_in]
                 ))]
            )

        def unfold_attn(self, size, blocks, dpv=None):
            dpv = self.dpv if dpv is None else dpv
            return unfold(ids, (self.dpq, self.dpk, dpv, self.dpg), self.dlow, attn_in,
                          (w_qk, w_v, w_g), size, blocks)

        def dx(self, parts):
            return rms_back(x, self.dmid, parts, gain_attn, (F32, BF))

        def place_early(self, early):
            sequences = early.shape[0]
            shares = nt * self.early_height
            all_ids = early[:, shares + 6 * RANK, 0].astype(jnp.int32)
            numbers = jnp.arange(adapters, dtype=jnp.int32)
            chosen = numbers[:, None] == all_ids[None, :]
            if sequences == adapters:
                self.order = jnp.sum(jnp.where(chosen, numbers[None, :], 0), axis=1)
                self.total = lambda y: y
            else:
                self.order = numbers
                self.total = lambda y: jnp.einsum(
                    "es,sij->eij", chosen.astype(BF), y, preferred_element_type=F32
                )
            pitch = self.early_height
            return place(
                self.order, [self.total(early)],
                ((0, RANK, "shares", pitch), (RANK, 2 * RANK, "shares", pitch),
                 (shares, 2 * RANK, "halves", 3 * RANK),
                 (shares + 2 * RANK, RANK, "halves", 3 * RANK)), nt
            )

        def place_late(self, arrays, at):
            if arrays[0].shape[0] * len(arrays) != adapters:
                arrays = [self.total(arrays[0])]
                at = self.order
            pitch = self.late_height
            shares = nt * pitch
            return place(
                at[self.order], arrays,
                ((0, 4 * RANK, "shares", pitch), (4 * RANK, RANK, "shares", pitch),
                 (shares, RANK, "two", 4 * RANK), (shares + RANK, 2 * RANK, "halves", 4 * RANK),
                 (shares + 3 * RANK, RANK, "halves", 4 * RANK)), nt
            )

    output, input_grad, early, late = links.backward(Back())
    down_back_out, mlp_out, hidden_out, down_out = early
    attn_out, out_back_out, qk_grads, vg_grads, out_out = late
    return (
        output[None],
        input_grad[None],
        jnp.swapaxes(attn_out, 1, 2),
        qk_grads,
        vg_grads.reshape(adapters, 2, RANK, wide),
        jnp.swapaxes(out_out, 1, 2),
        out_back_out,
        jnp.swapaxes(mlp_out, 1, 2),
        hidden_out.reshape(adapters, 2, RANK, wide),
        jnp.swapaxes(down_out, 1, 2),
        down_back_out,
    )


def solution(mesh):
    in_specs = (
        P("dp", "tensor", None),
        P("dp", "tensor", None),
        P("dp", None),
        P("dp", None),
        P(),
        P(),
        P("dp", "tensor"),
        P("dp", "tensor"),
        P("dp", "tensor"),
        P("dp", "tensor"),
        P("tensor", "dp"),
        P("dp", "tensor"),
        P("dp", "tensor"),
        P("tensor", "dp"),
        P(),
        P(None, None, None, "tensor"),
        P(None, None, None, "tensor"),
        P(None, "tensor", None),
        P(),
        P(),
        P(None, None, None, "tensor"),
        P(None, "tensor", None),
        P(),
    )
    out_specs = (
        P("dp", "tensor", None),
        P("dp", "tensor", None),
        P(),
        P(None, None, None, "tensor"),
        P(None, None, None, "tensor"),
        P(None, "tensor", None),
        P(),
        P(),
        P(None, None, None, "tensor"),
        P(None, "tensor", None),
        P(),
    )
    local = partial(shards, mesh.shape["dp"], mesh.shape["tensor"])
    return jax.shard_map(local, mesh=mesh, in_specs=in_specs, out_specs=out_specs, check_vma=False)
```

```python
from functools import partial

import jax
import jax.numpy as jnp
from jax import lax
from jax.experimental import pallas as pl
from jax.experimental.pallas import tpu as pltpu
from jax.sharding import PartitionSpec as P

KEY_DIM = 256
VALUE_DIM = 512
RANK = 16
HALF = KEY_DIM // 2

rms_epsilon = 1e-06
group_floor = 1.0
BF = jnp.bfloat16
F32 = jnp.float32


def dot(a, b):
    return jnp.dot(a, b, preferred_element_type=F32)


def dot_nt(a, b):
    return lax.dot_general(a, b, (((1,), (1,)), ((), ())), preferred_element_type=F32)


def dot_tn(a, b):
    return lax.dot_general(a, b, (((0,), (0,)), ((), ())), preferred_element_type=F32)


def aligned(start, size):
    return pl.ds(pl.multiple_of(start, size), size)


def params(mib):
    return pltpu.CompilerParams(
        vmem_limit_bytes=mib << 20, dimension_semantics=("arbitrary",)
    )


def estimate(flops, moved):
    return pl.CostEstimate(flops=1, bytes_accessed=1, transcendentals=0)


def full(shape):
    return pl.BlockSpec(shape, lambda *_: (0,) * len(shape))


def in_hbm(*arrays):
    return [pltpu.with_memory_space_constraint(array, pltpu.HBM) for array in arrays]


def far(shape, kind):
    return pltpu.HBM(shape, kind)


def smem():
    return pl.BlockSpec(memory_space=pltpu.SMEM)


def columns(refs, ids):
    count = ids.shape[0]
    width = refs[0].shape[1] // count
    if count == 1:
        return all_rows(refs)
    return jnp.concatenate(
        [
            jnp.concatenate([ref[:, aligned(ids[i] * width, width)] for i in range(count)], axis=1)
            for ref in refs
        ],
        axis=0,
    )


def all_rows(refs):
    return refs[0][...] if len(refs) == 1 else jnp.concatenate([ref[...] for ref in refs], axis=0)


def low_rows(low_in, refs):
    return jnp.concatenate([dot_nt(low_in, ref[...]) for ref in refs], axis=1)


def whole(arrays):
    return [full(array.shape) for array in arrays]


def row_count(arrays):
    return sum(array.shape[0] for array in arrays)


def stacked(refs):
    return jnp.concatenate([w[s] for w in refs for s in range(w.shape[0])], axis=0)


def rotated(values, cosine, sine_table):
    first = values[:, :HALF]
    second = values[:, HALF:]
    return jnp.concatenate(
        [first * cosine - second * sine_table, second * cosine + first * sine_table], axis=1
    )


def unrotated(values, cosine, sine_table):
    first = values[:, :HALF]
    second = values[:, HALF:]
    return jnp.concatenate(
        [first * cosine + second * sine_table, second * cosine - first * sine_table], axis=1
    )


def norm_kernel(x, gain, out):
    rows = x[...].astype(F32)
    inverse = lax.rsqrt(jnp.mean(rows * rows, axis=1, keepdims=True) + rms_epsilon)
    out[...] = (rows * inverse * gain[...]).astype(BF)


def norm_rows(x, gain):
    return pl.pallas_call(
        norm_kernel,
        out_shape=far(x.shape, BF),
        compiler_params=pltpu.CompilerParams(vmem_limit_bytes=24 << 20),
        name="norm_rows",
    )(x, gain)


def piece_specs(pieces, width):
    return [
        pl.BlockSpec((w.shape[0], w.shape[1], width), lambda n: (0, 0, n)) for w in pieces
    ]


def project_kernel(layout, ids, chunks, low_in, low_out, *refs):
    parts, count, lengths, turn = layout
    if turn:
        (cosine, sine_table), refs = refs[:2], refs[2:]
    act, refs = refs[:parts], refs[parts:]
    groups = len(lengths)
    pieces, outs = refs[:groups * count], refs[groups * count:]
    if turn:
        low = outs[-1]

        @pl.when(pl.program_id(0) == 0)
        def _():
            low[...] = low_rows(low_in[...], act).astype(BF)
    else:
        low = low_in
    n = pl.program_id(0)
    begin = 0
    for i, length in enumerate(lengths):

        @pl.when((n >= begin) & (n < begin + length))
        def _(i=i, length=length):
            made = dot(columns(act, ids), stacked(pieces[i * count:(i + 1) * count]))
            made = made + dot_tn(low[...], low_out[...])
            if i > 0 or not turn:
                outs[i][...] = made.astype(BF)
                return
            scale = jnp.where(n >= length // 2, 1.0 / KEY_DIM**0.5, 1.0)
            size = made.shape[0] // chunks.shape[0]
            for j in range(chunks.shape[0]):
                at = aligned(chunks[j] * size, size)
                rows = slice(j * size, (j + 1) * size)
                turned = rotated(made[rows], cosine[at, :], sine_table[at, :])
                outs[i][rows, :] = (scale * turned).astype(BF)

        begin += length


def project(ids, chunks, act, low_in, low_out, weights, turn):
    rows, depth = row_count(act), act[0].shape[1]
    block = KEY_DIM
    lengths = tuple(w[0].shape[2] // block for w in weights)
    begins = [sum(lengths[:i]) for i in range(len(lengths))]

    def at(group):
        return lambda n: jnp.clip(n - begins[group], 0, lengths[group] - 1)

    pieces = [
        pl.BlockSpec((w.shape[0], w.shape[1], block), lambda n, at=at(i): (0, 0, at(n)))
        for i, weight in enumerate(weights) for w in weight
    ]
    outs = [pl.BlockSpec((rows, block), lambda n, at=at(i): (0, at(n))) for i in range(len(weights))]
    shapes = [far((rows, length * block), BF) for length in lengths]
    ranks = low_in.shape[0]
    if turn:
        outs.append(full((ranks, rows)))
        shapes.append(jax.ShapeDtypeStruct((ranks, rows), BF))
    return pl.pallas_call(
        partial(project_kernel, (len(act), len(weights[0]), lengths, bool(turn))),
        grid=(sum(lengths),),
        in_specs=[smem(), smem(), full(low_in.shape),
                  pl.BlockSpec((ranks, block), lambda n: (0, n))]
        + whole(turn) + whole(act) + pieces,
        out_specs=outs,
        out_shape=shapes,
        compiler_params=params(48),
        cost_estimate=estimate(0, 0),
        name="project",
    )(ids, chunks, low_in, low_out, *turn, *in_hbm(*act, *[w for x in weights for w in x]))


def decay_factors(rate, size):
    down = lax.broadcasted_iota(jnp.int32, (size, 1), 0).astype(F32)
    across = lax.broadcasted_iota(jnp.int32, (1, size), 1).astype(F32)
    return down, across


def retention_kernel(spots, rates, seg_col, seg_row, q, k, v, gate, out, nrm, inverse):
    rate = rates[pl.program_id(0)]
    count = spots.shape[0]
    size = q.shape[0] // count
    down, across = decay_factors(rate, size)
    row_factor = jnp.exp(rate * down)
    for i in range(count):
        here = aligned(spots[i] * size, size)
        query = q[here, :]
        seg_here = seg_col[i * size:(i + 1) * size, :]
        total = jnp.zeros((size, v.shape[1]), F32)
        for j in range(i + 1):
            there = aligned(spots[j] * size, size)
            column_factor = jnp.exp(rate * ((i - j) * size - across))
            alive = seg_here == seg_row[:, j * size:(j + 1) * size]
            if i == j:
                alive = alive & (down >= across)
            scores = dot_nt(query, k[there, :])
            mixed = jnp.where(alive, scores * row_factor * column_factor, 0.0).astype(BF)
            total = total + dot(mixed, v[there, :])
        centered = total - jnp.mean(total, axis=1, keepdims=True)
        scale = lax.rsqrt(jnp.mean(centered * centered, axis=1, keepdims=True) + group_floor)
        normed = centered * scale
        level = gate[here, :].astype(F32)
        out[here, :] = (level / (1.0 + jnp.exp(-level)) * normed).astype(BF)
        nrm[here, :] = normed.astype(nrm.dtype)
        inverse[0, here, :] = jnp.broadcast_to(scale, (size, 128))


def retention(spots, rates, seg_col, seg_row, qk, v, gate):
    rows = qk.shape[0]
    heads = v.shape[1] // VALUE_DIM
    return pl.pallas_call(
        retention_kernel,
        grid=(heads,),
        in_specs=[smem(), smem(), full(seg_col.shape), full(seg_row.shape),
                  pl.BlockSpec((rows, KEY_DIM), lambda h: (0, h)),
                  pl.BlockSpec((rows, KEY_DIM), lambda h: (0, h + heads)),
                  pl.BlockSpec((rows, VALUE_DIM), lambda h: (0, h)),
                  pl.BlockSpec((rows, VALUE_DIM), lambda h: (0, h))],
        out_specs=[pl.BlockSpec((rows, VALUE_DIM), lambda h: (0, h)),
                   pl.BlockSpec((rows, VALUE_DIM), lambda h: (0, h)),
                   pl.BlockSpec((1, rows, 128), lambda h: (h, 0, 0))],
        out_shape=[far(v.shape, BF), far(v.shape, BF),
                   far((heads, rows, 128), F32)],
        compiler_params=params(40),
        cost_estimate=estimate(2 * rows * rows * 768 * heads, 30 << 20),
        name="retention",
    )(spots, rates, seg_col, seg_row, qk, qk, *in_hbm(v, gate))


def fold_kernel(ids, act, low_in, low_out, *refs):
    pieces, (outs, low) = refs[:-5], (refs[-5:-1], refs[-1])
    step = pl.program_id(0)
    subs = pl.num_programs(0)
    width = pieces[0].shape[2]
    size = outs[0].shape[0]

    @pl.when(step == 0)
    def _():
        low[...] = dot_nt(low_in[...], act[...])

    extra = low[...].astype(BF)
    rows = act[...]
    for i, piece in enumerate(pieces):
        at = aligned(ids[i * subs + step] * width, width)
        product = (dot(rows, piece[0]) + dot_tn(extra, low_out[:, at])).astype(BF)
        for j, out in enumerate(outs):
            out[:, at] = product[j * size:(j + 1) * size]


def fold(ids, act, low_in, low_out, pieces):
    rows, depth = act.shape
    subs = pieces[0].shape[0]
    width = low_out.shape[1]
    return pl.pallas_call(
        fold_kernel,
        grid=(subs,),
        in_specs=[smem(), full(act.shape), full(low_in.shape), full(low_out.shape)]
        + [pl.BlockSpec((1,) + w.shape[1:], lambda s: (s, 0, 0)) for w in pieces],
        out_specs=[full((rows // 4, width))] * 4 + [full((low_in.shape[0], rows))],
        out_shape=[far((rows // 4, width), BF)] * 4
        + [jax.ShapeDtypeStruct((low_in.shape[0], rows), F32)],
        compiler_params=params(48),
        cost_estimate=estimate(2 * rows * depth * width, 2 * depth * width + 4 * rows * depth),
        name="fold",
    )(ids, act, low_in, low_out, *pieces)


def join_kernel(x, part0, part1, part2, gain, middle, normed):
    rows = x[...].astype(F32) + (
        part0[...].astype(F32) + part1[...].astype(F32) + part2[...].astype(F32)
    )
    inverse = lax.rsqrt(jnp.mean(rows * rows, axis=1, keepdims=True) + rms_epsilon)
    middle[...] = rows.astype(BF)
    normed[...] = (rows * inverse * gain[...]).astype(BF)


def join_rows(x, parts, gain):
    return pl.pallas_call(
        join_kernel,
        out_shape=[jax.ShapeDtypeStruct(x.shape, BF), jax.ShapeDtypeStruct(x.shape, BF)],
        compiler_params=pltpu.CompilerParams(vmem_limit_bytes=24 << 20),
        name="join_rows",
    )(x, *parts, gain)


def rms_back_kernel(rows_in, grad_in, part0, part1, part2, gain, *outs):
    rows = rows_in[...].astype(F32)
    inverse = lax.rsqrt(jnp.mean(rows * rows, axis=1, keepdims=True) + rms_epsilon)
    normed = rows * inverse
    scaled = gain[...] * (
        part0[...].astype(F32) + part1[...].astype(F32) + part2[...].astype(F32)
    )
    result = grad_in[...].astype(F32) + inverse * (
        scaled - normed * jnp.mean(scaled * normed, axis=1, keepdims=True)
    )
    for out in outs:
        out[...] = result.astype(out.dtype)


def rms_back(rows_in, grad_in, parts, gain, kinds):
    count, width = rows_in.shape
    block = pl.BlockSpec((count // 2, width), lambda i: (i, 0))
    return pl.pallas_call(
        rms_back_kernel,
        grid=(2,),
        in_specs=[block] * 5 + [full(gain.shape)],
        out_specs=[block] * len(kinds),
        out_shape=[far((count, width), kind) for kind in kinds],
        compiler_params=params(24),
        name="rms_back",
    )(rows_in, grad_in, *parts, gain)


def hidden_grad_kernel(parts, ids, low_back, low_in, *refs):
    act, pieces, (out, low) = refs[:parts], refs[parts:-2], refs[-2:]

    @pl.when(pl.program_id(0) == 0)
    def _():
        low[...] = low_rows(low_back[...], act).astype(BF)

    weights = jnp.concatenate([w[s] for w in pieces for s in range(w.shape[0])], axis=1)
    out[...] = dot_nt(columns(act, ids), weights) + dot_tn(low[...], low_in[...])


def hidden_grad(ids, act, low_back, low_in, pieces):
    rows, depth = row_count(act), act[0].shape[1]
    width = pieces[0].shape[1]
    block = 256
    return pl.pallas_call(
        partial(hidden_grad_kernel, len(act)),
        grid=(width // block,),
        in_specs=[smem(), full(low_back.shape),
                  pl.BlockSpec((low_in.shape[0], block), lambda n: (0, n))]
        + whole(act) + [pl.BlockSpec((w.shape[0], block, w.shape[2]), lambda n: (0, n, 0)) for w in pieces],
        out_specs=[pl.BlockSpec((rows, block), lambda n: (0, n)),
                   full((low_back.shape[0], rows))],
        out_shape=[jax.ShapeDtypeStruct((rows, width), F32),
                   jax.ShapeDtypeStruct((low_back.shape[0], rows), BF)],
        compiler_params=params(40),
        cost_estimate=estimate(2 * rows * depth * width, 2 * depth * width + 8 * rows * depth),
        name="hidden_grad",
    )(ids, low_back, low_in, *act, *pieces)


def mlp_kernel(parts, count, ids, low_in, gate_out, up_out, down_in, grad, grad_low, *refs):
    act, refs = refs[:parts], refs[parts:]
    gate_pieces, up_pieces = refs[:count], refs[count:2 * count]
    hid, dgate, dup, low, lows, grad_hidden, grad_down = refs[2 * count:]

    @pl.when(pl.program_id(0) == 0)
    def _():
        low[...] = low_rows(low_in[...], act).astype(BF)
        lows[...] = jnp.zeros(lows.shape, F32)

    rows = columns(act, ids)
    extra = low[...]
    gate = dot(rows, stacked(gate_pieces)) + dot_tn(extra, gate_out[...])
    up = dot(rows, stacked(up_pieces)) + dot_tn(extra, up_out[...])
    chance = 0.5 * (1.0 + lax.erf(gate * (0.5**0.5)))
    active = gate * chance
    slope = chance + gate * (jnp.exp(-0.5 * gate * gate) * 0.3989422804014327)
    hidden = (active * up).astype(BF)
    back = grad[...]
    back_gate = (back * up * slope).astype(BF)
    back_up = (back * active).astype(BF)
    hid[...] = hidden
    dgate[...] = back_gate
    dup[...] = back_up
    lows[:RANK, :] += dot_nt(down_in[...], hidden)
    lows[RANK:, :] += dot_nt(gate_out[...], back_gate) + dot_nt(up_out[...], back_up)
    grad_hidden[:RANK, :] = dot(extra[:RANK], back_gate).astype(BF)
    grad_hidden[RANK:, :] = dot(extra[RANK:], back_up).astype(BF)
    grad_down[...] = dot(grad_low[...], hidden).astype(BF)


def mlp(ids, act, low_in, gate_out, up_out, down_in, grad, grad_low, gate_pieces, up_pieces):
    rows, depth = row_count(act), act[0].shape[1]
    width = gate_pieces[0].shape[2]
    block = 256
    ranks = low_in.shape[0]
    column = lambda height: pl.BlockSpec((height, block), lambda n: (0, n))
    return pl.pallas_call(
        partial(mlp_kernel, len(act), len(gate_pieces)),
        grid=(width // block,),
        in_specs=[smem(), full(low_in.shape), column(ranks), column(ranks),
                  column(down_in.shape[0]), column(rows), full(grad_low.shape)]
        + whole(act) + piece_specs(gate_pieces, block) + piece_specs(up_pieces, block),
        out_specs=[column(rows), column(rows), column(rows), full((ranks, rows)),
                   full((ranks + RANK, rows)), column(ranks), column(grad_low.shape[0])],
        out_shape=[jax.ShapeDtypeStruct((rows, width), BF)] * 3
        + [jax.ShapeDtypeStruct((ranks, rows), BF),
           jax.ShapeDtypeStruct((ranks + RANK, rows), F32),
           jax.ShapeDtypeStruct((ranks, width), BF),
           jax.ShapeDtypeStruct((grad_low.shape[0], width), BF)],
        compiler_params=params(48),
        cost_estimate=estimate(4 * rows * depth * width, 4 * depth * width + 8 * rows * depth),
        name="mlp",
    )(ids, low_in, gate_out, up_out, down_in, grad, grad_low, *act, *gate_pieces, *up_pieces)


def unfold_kernel(layout, ids, low_in, *refs):
    blocks, count, weights = layout
    lows, refs = refs[:blocks], refs[blocks:]
    acts, pieces, outs = refs[:blocks * count], refs[blocks * count:-blocks], refs[-blocks:]
    size = outs[0].shape[0]
    step = pl.program_id(0)
    subs = pl.num_programs(0)
    width = pieces[0].shape[1]
    extra = jnp.concatenate([low[...] for low in lows], axis=1).T.astype(BF)
    per = len(pieces) // weights
    rows = jnp.concatenate(
        [jnp.concatenate([act[...] for act in acts[i * count:(i + 1) * count]], axis=1)
         for i in range(blocks)], axis=0
    )
    for i in range(per):
        at = aligned(ids[i * subs + step] * width, width)
        weight = jnp.concatenate([pieces[k * per + i][0] for k in range(weights)], axis=1)
        product = (dot_nt(rows, weight) + dot(extra, low_in[:, at])).astype(BF)
        for j, out in enumerate(outs):
            out[:, at] = product[j * size:(j + 1) * size]


def unfold(ids, acts, low, low_in, weights, size, blocks):
    subs = weights[0][0].shape[0]
    width = low_in.shape[1]
    pieces = [piece for weight in weights for piece in weight]
    count = len(blocks)
    chosen = []
    for at in blocks:
        for act in acts:
            if isinstance(act, tuple):
                per = act[0].shape[0] // size
                chosen.append((act[at // per], at % per))
            else:
                chosen.append((act, at))
    depth = sum(act.shape[1] for act, _ in chosen) // count
    return pl.pallas_call(
        partial(unfold_kernel, (count, len(acts), len(weights))),
        grid=(subs,),
        in_specs=[smem(), full(low_in.shape)]
        + [pl.BlockSpec((low.shape[0], size), lambda s, at=at: (0, at)) for at in blocks]
        + [pl.BlockSpec((size, act.shape[1]), lambda s, at=at: (at, 0)) for act, at in chosen]
        + [pl.BlockSpec((1,) + w.shape[1:], lambda s: (s, 0, 0)) for w in pieces],
        out_specs=[full((size, width))] * count,
        out_shape=[far((size, width), BF)] * count,
        compiler_params=params(48),
        cost_estimate=estimate(
            2 * count * size * depth * width, 2 * depth * width + 4 * count * size * depth
        ),
        name="unfold",
    )(ids, low_in, *[low] * count, *in_hbm(*[act for act, _ in chosen], *pieces))


def gate_back_kernel(parts, ids, low_back, low_in, gate, nrm, inverse, hold, low_gate, low_out,
                     begin_in, begin_gate, *refs):
    act, pieces = refs[:parts], refs[parts:-6]
    dgate, dret, low, dlow, grad_in, grad_gate = refs[-6:]

    @pl.when(pl.program_id(0) == 0)
    def _():
        low[...] = low_rows(low_back[...], act).astype(BF)
        dlow[...] = jnp.zeros(dlow.shape, F32)

    weights = jnp.concatenate([w[s] for w in pieces for s in range(w.shape[0])], axis=1)
    back = dot_nt(columns(act, ids), weights) + dot_tn(low[...], low_in[...])
    level = gate[...].astype(F32)
    normed = nrm[...].astype(F32)
    chance = 1.0 / (1.0 + jnp.exp(-level))
    slope = chance * (1.0 + level * (1.0 - chance))
    back_gate = (back * normed * slope).astype(BF)
    grad = back * (level * chance)
    mean = jnp.mean(grad, axis=1, keepdims=True)
    along = jnp.mean(grad * normed, axis=1, keepdims=True)
    dgate[...] = back_gate
    dret[...] = (inverse[0, :, :1] * (grad - mean - normed * along)).astype(BF)
    grad_in[...] = begin_in[...] + dot(low[...], hold[...])
    grad_gate[...] = begin_gate[...] + dot(low_gate[...], back_gate)
    dlow[...] += dot_nt(low_out[...], back_gate)


def gate_back(ids, act, low_back, low_in, gate, nrm, inverse, hold, low_gate, low_out, pieces,
              half, begin_in, begin_gate):
    if len(act) > 1:
        act = act[len(act) // 2 * half:len(act) // 2 * (half + 1)]
    rows, depth = gate.shape[0] // 2, act[0].shape[1]
    width = gate.shape[1]
    block = VALUE_DIM
    ranks = low_back.shape[0]
    if len(act) == 1:
        acts = [pl.BlockSpec((rows, depth), lambda n: (half, 0))]
    else:
        acts = whole(act)
    column = lambda height: pl.BlockSpec((height, block), lambda n: (0, n))
    place = pl.BlockSpec((rows, block), lambda n: (half, n))
    return pl.pallas_call(
        partial(gate_back_kernel, len(act)),
        grid=(width // block,),
        in_specs=[smem(), full(low_back.shape), column(ranks), place, place,
                  pl.BlockSpec((1, rows, 128), lambda n: (n, half, 0)), place,
                  pl.BlockSpec((ranks, rows), lambda n: (low_gate.shape[0] // ranks - 1, half)),
                  column(low_out.shape[0]), column(ranks), column(ranks)]
        + acts + [pl.BlockSpec((w.shape[0], block, w.shape[2]), lambda n: (0, n, 0))
                  for w in pieces],
        out_specs=[column(rows), column(rows), full((ranks, rows)),
                   full((low_out.shape[0], rows)), column(ranks), column(ranks)],
        out_shape=[jax.ShapeDtypeStruct((rows, width), BF)] * 2
        + [jax.ShapeDtypeStruct((ranks, rows), BF),
           jax.ShapeDtypeStruct((low_out.shape[0], rows), F32),
           jax.ShapeDtypeStruct((ranks, width), F32), jax.ShapeDtypeStruct((ranks, width), F32)],
        compiler_params=params(56),
        cost_estimate=estimate(2 * rows * depth * width, 2 * depth * width + 16 * rows * width),
        name="gate_back",
    )(ids, low_back, low_in, *in_hbm(gate, nrm, inverse, hold), low_gate, low_out, begin_in,
      begin_gate, *act, *pieces)


def retention_back_kernel(spots, rates, seg_col, seg_row, cosine, sine_table, low, begin, q_out,
                          k_out, v_out, q, k, v, dret0, dret1, dq, dk, dv, dlow, grad_q, grad_k,
                          grad_v, sums):
    head = pl.program_id(0)
    rate = rates[head]
    count = spots.shape[0]
    size = q.shape[0] // count
    down, across = decay_factors(rate, size)
    column_factor = jnp.exp(rate * across)
    key_scale = 1.0 / KEY_DIM**0.5

    @pl.when(head == 0)
    def _():
        dlow[...] = begin[...]

    sums[...] = jnp.zeros(sums.shape, F32)
    for j in range(count):
        there = aligned(spots[j] * size, size)
        place = slice(j * size, (j + 1) * size)
        key, value = k[there, :], v[there, :]
        seg_there = seg_col[place, :]
        key_sum = jnp.zeros((size, KEY_DIM), F32)
        value_sum = jnp.zeros((size, VALUE_DIM), F32)
        for i in range(j, count):
            here = aligned(spots[i] * size, size)
            query = q[here, :]
            within = aligned(spots[i] % (count // 2) * size, size)
            back = jnp.where(spots[i] < count // 2, dret0[within, :], dret1[within, :])
            row_factor = jnp.exp(rate * ((i - j) * size - down))
            alive = seg_there == seg_row[:, i * size:(i + 1) * size]
            if i == j:
                alive = alive & (across >= down)
            weight = jnp.where(alive, row_factor * column_factor, 0.0)
            mixed = (dot_nt(key, query) * weight).astype(BF)
            grad = (dot_nt(value, back) * weight).astype(BF)
            value_sum = value_sum + dot(mixed, back)
            key_sum = key_sum + dot(grad, query)
            sums[i * size:(i + 1) * size, :] += dot_tn(grad, key)
        dk[there, :] = (
            key_scale * unrotated(key_sum, cosine[place, :], sine_table[place, :])
        ).astype(BF)
        dv[there, :] = value_sum.astype(BF)
    for i in range(count):
        place = slice(i * size, (i + 1) * size)
        dq[aligned(spots[i] * size, size), :] = unrotated(
            sums[place, :], cosine[place, :], sine_table[place, :]
        ).astype(BF)
    back_q, back_k, back_v = dq[...], dk[...], dv[...]
    dlow[...] += (
        dot_nt(q_out[...], back_q) + dot_nt(k_out[...], back_k) + dot_nt(v_out[...], back_v)
    )
    grad_q[...] = dot(low[:RANK, :], back_q).astype(BF)
    grad_k[...] = dot(low[RANK:2 * RANK, :], back_k).astype(BF)
    grad_v[...] = dot(low[2 * RANK:3 * RANK, :], back_v).astype(BF)


def retention_back(spots, rates, seg_col, seg_row, cosine, sine_table, low, begin, qk_out, v_out,
                   qk, v, dret0, dret1):
    rows = qk.shape[0]
    heads = v.shape[1] // VALUE_DIM
    ranks = low.shape[0]
    key = lambda height: pl.BlockSpec((height, KEY_DIM), lambda h: (0, h))
    later = lambda height: pl.BlockSpec((height, KEY_DIM), lambda h: (0, h + heads))
    value = lambda height: pl.BlockSpec((height, VALUE_DIM), lambda h: (0, h))
    keys = heads * KEY_DIM
    return pl.pallas_call(
        retention_back_kernel,
        grid=(heads,),
        in_specs=[smem(), smem(), full(seg_col.shape), full(seg_row.shape), full(cosine.shape),
                  full(cosine.shape), full(low.shape), full(begin.shape), key(ranks),
                  later(ranks), value(ranks),
                  key(rows), later(rows), value(rows), value(rows // 2), value(rows // 2)],
        out_specs=[key(rows), key(rows), value(rows), full((ranks, rows)), key(RANK), key(RANK),
                   value(RANK)],
        out_shape=[jax.ShapeDtypeStruct((rows, keys), BF), jax.ShapeDtypeStruct((rows, keys), BF),
                   jax.ShapeDtypeStruct(v.shape, BF), jax.ShapeDtypeStruct((ranks, rows), F32),
                   jax.ShapeDtypeStruct((RANK, keys), BF), jax.ShapeDtypeStruct((RANK, keys), BF),
                   jax.ShapeDtypeStruct((RANK, v.shape[1]), BF)],
        scratch_shapes=[pltpu.VMEM((rows, KEY_DIM), F32)],
        compiler_params=params(48),
        cost_estimate=estimate(2 * rows * rows * 1792 * heads, 30 << 20),
        name="retention_back",
    )(spots, rates, seg_col, seg_row,
      cosine, sine_table, low, begin, qk_out, qk_out, v_out, qk, qk, v, dret0, dret1)


def share_kernel(heights, low, *refs):
    out = refs[-1]
    at, first = 0, 0
    for height, parts in heights:
        total = jnp.zeros((height, out.shape[2]), F32)
        begin = 0
        for ref in refs[first:first + parts]:
            end = begin + ref.shape[0]
            total = total + dot(low[at:at + height, begin:end], ref[...])
            begin = end
        out[0, at:at + height, :] = total.astype(BF)
        at, first = at + height, first + parts


def share(low, span, items):
    acts = [array for _, act in items for array in act]
    heights = tuple((height, len(act)) for height, act in items)
    count = acts[0].shape[1] // span
    made = pl.pallas_call(
        partial(share_kernel, heights),
        grid=(count,),
        in_specs=[full(low.shape)]
        + [pl.BlockSpec((act.shape[0], span), lambda i: (0, i)) for act in acts],
        out_specs=pl.BlockSpec((1, low.shape[0], span), lambda i: (i, 0, 0)),
        out_shape=jax.ShapeDtypeStruct((count, low.shape[0], span), BF),
        compiler_params=params(32),
        cost_estimate=estimate(0, 0),
        name="share",
    )(low, *in_hbm(*acts))
    return made.reshape(count * low.shape[0], span)


def place_kernel(layout, arrays, order, *refs):
    packs, outs = refs[:arrays], refs[arrays:]
    pack = packs[0][0]
    if arrays == 2:
        which = order[pl.program_id(0)] >= order[pl.num_programs(0)]
        pack = jnp.where(which, packs[1][0], pack)
    span = pack.shape[1]
    for (begin, height, kind, stride), out in zip(layout, outs):
        if kind == "shares":
            for j in range(out.shape[2] // span):
                rows = pack[begin + stride * j:begin + stride * j + height]
                out[0, :, j * span:(j + 1) * span] = rows.astype(F32)
            continue
        for j in range(2):
            rows = pack[begin + stride * j:begin + stride * j + height].astype(F32)
            if kind == "halves":
                out[0, :, j * span:(j + 1) * span] = rows
            else:
                out[0, j] = rows


def place(order, arrays, layout, shares):
    entries = order.shape[0]
    size, _, span = arrays[0].shape
    shapes = []
    for _, height, kind, _ in layout:
        shapes.append({"shares": (height, shares * span),
                       "halves": (height, 2 * span)}.get(kind, (2, height, span)))

    def spec(number):
        def index(e, o):
            return (jnp.clip(o[e] - number * size, 0, size - 1), 0, 0)
        return pl.BlockSpec((1,) + arrays[0].shape[1:], index)

    order = jnp.concatenate([order, jnp.full((1,), size, jnp.int32)])
    return pl.pallas_call(
        partial(place_kernel, layout, len(arrays)),
        grid_spec=pltpu.PrefetchScalarGridSpec(
            num_scalar_prefetch=1,
            grid=(entries,),
            in_specs=[spec(number) for number in range(len(arrays))],
            out_specs=[
                pl.BlockSpec((1,) + shape, lambda e, o, n=len(shape): (e,) + (0,) * n)
                for shape in shapes
            ],
        ),
        out_shape=[jax.ShapeDtypeStruct((entries,) + shape, F32) for shape in shapes],
        compiler_params=params(32),
        cost_estimate=estimate(0, 10 << 20),
        name="place",
    )(order, *in_hbm(*arrays))


def after(x, *others):
    return lax.optimization_barrier((x,) + others)[0]


class PlainLinks:
    def __init__(self, ndp, nt):
        self.ndp, self.nt = ndp, nt
        self.rank = lax.axis_index("tensor")
        self.chunks = jnp.arange(nt, dtype=jnp.int32)
        self.spots = self.chunks
        self.row_ids = jnp.zeros((1,), jnp.int32)

    def exchange(self, x):
        return x

    def mine(self, own, other):
        return own

    def gather(self, x):
        return [lax.all_gather(x, "tensor", axis=0, tiled=True)]

    def scatter(self, rows):
        total = lax.psum_scatter(
            jnp.concatenate(rows, axis=0), "tensor", scatter_dimension=0, tiled=True
        )
        zero = jnp.zeros_like(total)
        return (total, zero, zero)

    def forward(self, shards, tokens, cotangent, line, steps):
        blocks = [
            [lax.all_gather(shard, "dp", axis=int(shard.shape[1] * self.ndp == tokens.shape[1]),
                            tiled=True)[None]]
            for shard in shards
        ]
        steps.ready(line, steps.tables(line, line)[0])
        a = self.gather(steps.norm(tokens))
        dy = self.gather(cotangent)
        projected = steps.project(a, blocks[1], blocks[0])
        mixed = steps.mix(a, *projected, blocks[2])
        *rows, low = steps.fold(mixed[0], blocks[3])
        middle, b = steps.join(tokens, self.scatter(rows))
        dhid = steps.hidden_grad(dy, blocks[4])
        return (blocks, tokens, a, cotangent, dy, projected, mixed, low, middle,
                self.gather(b), dhid)

    def group_sum(self, x):
        return lax.psum(x.astype(BF), "tensor")

    def backward(self, steps):
        steps.mlp()
        dz = self.gather(steps.dz(self.scatter(steps.unfold_mlp(256, (0, 1, 2, 3)))))
        output = steps.output(self.scatter(steps.fold_down(steps.hid)))
        early = lax.all_gather(steps.early(self.group_sum(steps.lows)), "dp")
        early = steps.place_early([early], jnp.arange(self.ndp, dtype=jnp.int32))
        steps.gate_back(dz, 0)
        steps.gate_back(dz, 1)
        steps.retention_back(*steps.dret)
        late = lax.all_gather(steps.late(self.group_sum(steps.late_lows()), dz), "dp")
        late = steps.place_late([late], jnp.arange(self.ndp, dtype=jnp.int32))
        parts = self.scatter(steps.unfold_attn(256, (0, 1, 2, 3)))
        dx, _ = steps.dx(parts)
        return output, dx, early, late


class PairedLinks:
    def __init__(self, ndp, nt):
        self.ndp, self.nt = ndp, nt
        d, t = lax.axis_index("dp"), lax.axis_index("tensor")
        c, p, m = d % 2, t // 2, t % 2
        self.home = c == p
        self.rank = 2 * c + m
        flips = jnp.array([0, 2, 1, 3], jnp.int32)
        self.chunks = self.rank ^ flips
        order = jnp.arange(4, dtype=jnp.int32) ^ self.rank
        self.spots = (order % 2) * 2 + order // 2
        g = d // 2
        self.row_ids = ((2 * (g ^ jnp.arange(4, dtype=jnp.int32))[:, None]
                         + jnp.arange(2, dtype=jnp.int32)[None, :]) ^ c).reshape(-1)
        self.last = {}
        self.last_round = ()
        self.slow = ()

    def pairs(self, place):
        listed = []
        for d in range(self.ndp):
            for t in range(self.nt):
                to = place(d, t)
                if to is not None:
                    listed.append((d * self.nt + t, to[0] * self.nt + to[1]))
        return listed

    def move(self, x, place, chain=None):
        if chain in self.last:
            x = after(x, *self.last[chain])
        moved = lax.ppermute(x, ("dp", "tensor"), self.pairs(place))
        if chain is not None:
            self.last[chain] = (moved,)
        return moved

    def send(self, moves):
        return [lax.ppermute(x, ("dp", "tensor"), self.pairs(place)) for x, place in moves]

    def round(self, moves, work=None, inputs=(), later=(), slow=(), feed=0):
        every = list(moves) + list(slow)
        values = [x for x, _ in every]
        flat, form = jax.tree.flatten((values, inputs))
        last, _ = jax.tree.flatten(self.last_round)
        if last:
            flat = lax.optimization_barrier((*flat, *last))[:len(flat)]
        values, inputs = jax.tree.unflatten(form, flat)
        moved = self.send([(x, place) for x, (_, place) in zip(values, every)])
        moved, slowly = moved[:len(moves)], moved[len(moves):]
        second = []
        if later:
            count, make = later
            moves = make(moved[:count])
            values = [x for x, _ in moves]
            values = lax.optimization_barrier((*values, *moved[:count]))[:len(values)]
            second = self.send([(x, place) for x, (_, place) in zip(values, moves)])
        made = work(*moved[:feed], *inputs) if work is not None else ()
        self.last_round = (moved, second, made, self.slow)
        self.slow = slowly
        return moved + slowly, second, made

    def core(self, x):
        return self.move(x, lambda d, t: (d ^ 1, t))

    def pair(self, x):
        return self.move(x, lambda d, t: (d, t ^ 1), "pair")

    def mine(self, own, other):
        return jnp.where(self.home, own, other)

    def exchange(self, x):
        moved = self.move(
            x, lambda d, t: (d ^ 1, t ^ 2) if d % 2 != t // 2 else None, "middle"
        )
        return jnp.where(self.home, x, moved)

    def gather(self, x):
        across = self.pair(x)
        return [x, self.core(x), across, self.core(across)]

    def forward(self, shards, tokens, cotangent, line, steps):
        by_one = lambda d, t: (d ^ 2, t)
        by_two = lambda d, t: (d ^ 4, t)
        core = lambda d, t: (d ^ 1, t)
        pair = lambda d, t: (d, t ^ 1)
        swap = lambda d, t: (d ^ 1, t ^ 2) if d % 2 != t // 2 else None
        seat = lambda d, t: (d, t ^ 2) if d % 2 == t // 2 else None
        blocks = [[None] * 4 for _ in shards]
        doubled = [jnp.stack([shards[0], self.core(shards[0])])]

        def over(i):
            return (doubled[i], seat)

        def arrived(i, moved):
            blocks[i][0] = self.mine(doubled[i], moved)

        hops = {
            "x": lambda i: (blocks[i][0], by_one),
            "y": lambda i: (blocks[i][0], by_two),
            "xy": lambda i: (blocks[i][1], by_two),
            "yx": lambda i: (blocks[i][2], by_one),
        }
        place_of = {"x": 1, "y": 2, "xy": 3, "yx": 3}

        def go(first, second, others, work=None, inputs=()):
            def later(moved):
                for (i, way), block in zip(first, moved):
                    blocks[i][place_of[way]] = block
                return [hops[way](i) for i, way in second]

            moved, seconds, made = self.round(
                [hops[way](i) for i, way in first] + list(others), work, inputs,
                (len(first), later)
            )
            for (i, way), block in zip(second, seconds):
                blocks[i][place_of[way]] = block
            return moved[len(first):], made

        def double(rest):
            return [jnp.stack([shard, self.core(shard)]) for shard in rest]

        other = self.core(line)
        (moved,), made = go([], [], [over(0)], double, (shards[1:],))
        doubled += made
        arrived(0, moved)
        (moved,), (home_table, sent_table) = go(
            [(0, "x"), (0, "y")], [], [over(1)], steps.tables, (line, other)
        )
        arrived(1, moved)
        (x, table, moved), _ = go([(1, "x"), (0, "xy")], [(1, "y")],
                                  [(tokens, swap), (sent_table, seat), over(2)])
        arrived(2, moved)
        x = self.mine(tokens, x)
        steps.ready(other, self.mine(home_table, table))
        a = steps.norm(x)
        (across, moved, grad), _ = go([(2, "x"), (2, "y")], [(1, "yx"), (2, "xy")],
                                      [(a, pair), over(3), (cotangent, swap)])
        arrived(3, moved)
        grad = self.mine(cotangent, grad)
        def attend(near, beyond, own, across, *weights):
            a = [own, near, across, beyond]
            return a, steps.project(a, *weights[::-1])

        moves = [(a, core), (across, core), hops["x"](3), hops["y"](3), over(4)]
        moved, _, (a, projected) = self.round(
            moves, attend, (a, across, *blocks[:2]), feed=2
        )
        _, _, blocks[3][1], blocks[3][2], moved = moved
        arrived(4, moved)
        half = grad.shape[0] // 2
        (moved, across0), mixed = go(
            [(4, "x"), (3, "xy")], [], [over(5), (grad[:half], pair)], steps.mix,
            (a, *projected, blocks[2])
        )
        arrived(5, moved)
        (moved, across1), folded = go(
            [(5, "x"), (4, "y")], [], [over(6), (grad[half:], pair)], steps.fold,
            (mixed[0], blocks[3])
        )
        across = jnp.concatenate([across0, across1])
        arrived(6, moved)
        own, near, far, beyond, low = folded
        moves = [(near, core), (beyond, core), hops["yx"](4), hops["y"](5)]
        moved, (far,), _ = self.round(
            moves, later=(2, lambda moved: [(self.add(far, moved[1]), pair)])
        )
        near, _, blocks[4][3], blocks[5][2] = moved
        middle, b = steps.join(x, (own, near, far))
        (far, near_grad, beyond_grad), _ = go([(6, "x"), (6, "y")], [],
                                              [(b, pair), (grad, core), (across, core)])
        dy = [grad, near_grad, across, beyond_grad]
        (near, beyond), dhid = go([(5, "yx"), (6, "xy")], [], [(b, core), (far, core)],
                                  steps.hidden_grad, (dy, blocks[4]))
        b = [b, near, far, beyond]
        return blocks, x, a, grad, dy, projected, mixed, low, middle, b, dhid

    def add(self, one, two):
        return (one.astype(F32) + two.astype(F32)).astype(BF)

    def core_sum(self, x, other):
        size = x.shape[1] // 4
        other = other.astype(F32)
        return (x + jnp.concatenate(
            [other[:, i * size:(i + 1) * size] for i in (1, 0, 3, 2)], axis=1
        )).astype(BF)

    def pair_sum(self, x, other):
        size = x.shape[1] // 2
        other = jnp.concatenate([other[:, size:], other[:, :size]], axis=1)
        return (x.astype(F32) + other.astype(F32)).astype(BF)

    def both_halves(self, halves, one, two):
        return jnp.concatenate(
            [jnp.concatenate([halves[0], one]),
             jnp.concatenate([halves[1][:1], two[:1], halves[1][1:], two[1:]])], axis=1
        )

    def backward(self, steps):
        pair = lambda d, t: (d, t ^ 1)
        swap = lambda d, t: (d ^ 1, t ^ 2) if d % 2 != t // 2 else None
        by_one = lambda d, t: (d ^ 2, t)
        by_two = lambda d, t: (d ^ 4, t)
        core = lambda d, t: (d ^ 1, t)

        self.last_round = ()
        steps.mlp()
        (lows,), _, (near, far, beyond) = self.round(
            [(steps.lows.astype(BF), core)],
            lambda dup: steps.unfold_mlp(256, (1, 2, 3), dup), (steps.dup,)
        )
        lows = self.core_sum(steps.lows, lows)
        (beyond, near, other), _, _ = self.round([(beyond, core), (near, core), (lows, pair)])
        far = self.add(far, beyond)
        half = far.shape[0] // 2
        lows = self.pair_sum(lows, other)
        (far,), _, ((own,), folded, early) = self.round(
            [(far, pair)],
            lambda dup, hid, lows: (steps.unfold_mlp(256, (0,), dup), steps.fold_down(hid),
                                    steps.early(lows)),
            (steps.dup, steps.hid, lows)
        )
        own_out, near_out, far_out, beyond_out = folded
        dz = steps.dz((own, near, far))


        def beside(beyond, dz_near, far, dz):
            return self.add(far, beyond), steps.gate_back([dz, dz_near, dz, dz], 0)

        (_, dz_near, across, moved, near_out), _, (far_out, dret0) = self.round(
            [(beyond_out, core), (dz, core), (dz, pair), (early, swap), (near_out, core)],
            beside, (far_out, dz), feed=2
        )
        early = self.mine(early, moved)
        size = early.shape[0] // 2
        early = [early[:size][None], early[size:][None]]
        (dz_beyond,), _, _ = self.round([(across, core)])
        (one, two, far_out), _, dret1 = self.round(
            [(early[0], by_one), (early[1], by_two)],
            lambda across, beyond: steps.gate_back([across, across, across, beyond], 1),
            (across, dz_beyond), slow=[(far_out, pair)]
        )
        early = [jnp.concatenate([early[0], one]), jnp.concatenate([early[1], two])]
        (one, two), _, dpv = self.round(
            [(early[0], by_two), (early[1], by_one)], steps.retention_back, (dret0, dret1)
        )
        dz = [dz, dz_near, across, dz_beyond]
        early = early, one, two

        (dlow,), _, output = self.round(
            [(steps.late_lows().astype(BF), core)], lambda *parts: steps.output(parts),
            (own_out, near_out, far_out)
        )
        dlow = self.core_sum(steps.late_lows(), dlow)
        (other, moved_out), _, ((near, far, beyond), early) = self.round(
            [(dlow, pair), (output, swap)],
            lambda dpv, early: (steps.unfold_attn(256, (1, 2, 3), dpv), self.both_halves(*early)),
            (dpv, early)
        )
        (beyond, near), _, late = self.round(
            [(beyond, core), (near, core)],
            lambda dlow, other: steps.late(self.pair_sum(dlow, other), dz), (dlow, other)
        )
        (moved,), _, ((own,), far) = self.round(
            [(late, swap)],
            lambda dpv, far, beyond: (steps.unfold_attn(256, (0,), dpv), self.add(far, beyond)),
            (dpv, far, beyond)
        )
        late = self.mine(late, moved)
        size = late.shape[0] // 2
        late = [late[:size][None], late[size:][None]]
        (one, two, far0), _, _ = self.round(
            [(late[0], by_one), (late[1], by_two), (far[:half], pair)]
        )
        late = [jnp.concatenate([late[0], one]), jnp.concatenate([late[1], two])]
        (one, two, far1), _, _ = self.round(
            [(late[0], by_two), (late[1], by_one), (far[half:], pair)]
        )
        dx, low = steps.dx((own, near, jnp.concatenate([far0, far1])))
        late = self.both_halves(late, one, two)
        apart = jnp.arange(self.ndp, dtype=jnp.int32) ^ lax.axis_index("dp")

        def put(early_other, other, early, late):
            at = apart // 2 + 4 * (apart % 2)
            early = steps.place_early([early, early_other], at)
            return early, steps.place_late([late, other], at)

        (_, _, moved), _, (early, late) = self.round(
            [(early, core), (late, core), (low, swap)], put, (early, late), feed=2
        )
        moved, early, late = lax.optimization_barrier((moved, early, late))
        return (self.mine(output, moved_out),
                self.mine(dx, moved.astype(F32)), early, late)


def rotation_tables(seq_length, half_dim):
    positions = jnp.arange(seq_length, dtype=jnp.float32)
    frequency = jnp.exp(-jnp.log(10000.0) * jnp.arange(half_dim, dtype=jnp.float32) / half_dim)
    angles = positions[:, None] * frequency[None, :]
    return (jnp.cos(angles), jnp.sin(angles))


def shards(
    ndp,
    nt,
    tokens,
    cotangent,
    adapter_ids,
    segments,
    norm_attn,
    norm_mlp,
    weight_query,
    weight_key,
    weight_value,
    weight_gate,
    weight_out,
    weight_mlp_gate,
    weight_mlp_up,
    weight_mlp_down,
    adapt_attn_in,
    adapt_query_key,
    adapt_value_gate,
    adapt_out_in,
    adapt_out_back,
    adapt_mlp_in,
    adapt_mlp_hidden,
    adapt_down_in,
    adapt_down_back,
):
    links = PairedLinks(ndp, nt) if (ndp, nt) == (8, 4) else PlainLinks(ndp, nt)
    rank, chunks, spots, ids = links.rank, links.chunks, links.spots, links.row_ids
    adapters = adapt_attn_in.shape[0]
    depth = tokens.shape[2]
    seq_length = segments.shape[1]
    gain_attn, gain_mlp = norm_attn[None], norm_mlp[None]

    def pick(table, which):
        return lax.dynamic_index_in_dim(table, which, 0, keepdims=False)

    def packed(which):
        qk, vg = pick(adapt_query_key, which), pick(adapt_value_gate, which)
        return jnp.concatenate(
            [jnp.concatenate([qk[0], qk[1]], axis=1), vg[0], vg[1],
             pick(adapt_mlp_hidden, which).reshape(2 * RANK, -1),
             pick(adapt_out_in, which).T, pick(adapt_down_in, which).T], axis=0
        )

    own_id = adapter_ids[0, 0]
    own_line = jnp.concatenate([segments, jnp.broadcast_to(adapter_ids, (1, 128))], axis=1)
    wide = weight_gate.shape[1]
    keys = adapt_query_key.shape[3]
    heads_local = wide // VALUE_DIM
    head_ids = (rank * heads_local + jnp.arange(heads_local, dtype=jnp.int32)).astype(F32)
    rates = jnp.log(1.0 - jnp.exp2(-5.0 - head_ids))
    cosine, sine_table = rotation_tables(seq_length, HALF)

    class Steps:
        def tables(self, line, other):
            return packed(line[0, seq_length]), packed(other[0, seq_length])

        def ready(self, other, table):
            line = links.mine(own_line, other)
            self.work_id = work_id = line[0, seq_length]
            self.seg_row = line[:, :seq_length]
            self.seg_col = self.seg_row.reshape(seq_length, 1)
            blank = jnp.zeros((RANK, wide), BF)
            left = jnp.arange(wide)[None, :] < keys
            zero = jnp.zeros((), BF)
            self.qk_out = jnp.concatenate([jnp.where(left, table[:RANK], zero),
                                           jnp.where(left, zero, table[:RANK]), blank, blank])
            self.v_out = jnp.concatenate([blank, blank, table[RANK:2 * RANK], blank])
            self.g_out = jnp.concatenate([blank, blank, blank, table[2 * RANK:3 * RANK]])
            self.mg_out = jnp.concatenate([table[3 * RANK:4 * RANK], blank])
            self.mu_out = jnp.concatenate([blank, table[4 * RANK:5 * RANK]])
            self.out_in = table[5 * RANK:6 * RANK]
            self.down_in = table[6 * RANK:7 * RANK]
            self.attn_in = pick(adapt_attn_in, work_id).T
            self.out_back = pick(adapt_out_back, work_id)
            self.mlp_in = pick(adapt_mlp_in, work_id).T
            self.down_back = pick(adapt_down_back, work_id)

        def norm(self, x):
            return norm_rows(x, gain_attn)

        def project(self, a, w_qk, w_v):
            return project(
                ids, chunks, a, self.attn_in, jnp.concatenate([self.qk_out, self.v_out], axis=1),
                (w_qk, w_v), (cosine, sine_table)
            )

        def mix(self, a, qk, v, low, w_g):
            gate, = project(ids, chunks, a, low, self.g_out, (w_g,), ())
            return (*retention(spots, rates, self.seg_col, self.seg_row, qk, v, gate), gate)

        def fold(self, o, w_o):
            return fold(ids, o, self.out_in, self.out_back, w_o)

        def join(self, x, parts):
            return join_rows(x, parts, gain_mlp)

        def hidden_grad(self, dy, w_d):
            return hidden_grad(ids, dy, self.down_back, self.down_in, w_d)

    steps = Steps()
    ((w_v, w_qk, w_g, w_o, w_d, w_mg, w_mu), x, a, grad, dy, (qk, v, low_a),
     (o, nrm, inverse, gate), low_o, middle, b, (dhid, low_dy)) = links.forward(
        [weight_value, jnp.concatenate([weight_query, weight_key], axis=1), weight_gate,
         weight_out, weight_mlp_down, weight_mlp_gate, weight_mlp_up],
        tokens[0], cotangent[0], own_line, steps,
    )
    seg_row, seg_col, work_id = steps.seg_row, steps.seg_col, steps.work_id
    qk_out, v_out, g_out, mg_out, mu_out = (
        steps.qk_out, steps.v_out, steps.g_out, steps.mg_out, steps.mu_out
    )
    attn_in, out_in, out_back = steps.attn_in, steps.out_in, steps.out_back
    mlp_in, down_in, down_back = steps.mlp_in, steps.down_in, steps.down_back

    span = depth // nt
    halves = lambda y: jnp.concatenate([y[:, :wide // 2], y[:, wide // 2:]])

    class Back:
        early_height = 3 * RANK
        late_height = 5 * RANK

        def mlp(self):
            (self.hid, self.dgate, self.dup, _, self.lows, self.grad_hidden,
             self.grad_down) = mlp(
                ids, b, mlp_in, mg_out, mu_out, down_in, dhid, low_dy, w_mg, w_mu
            )

        def unfold_mlp(self, size, blocks, dup=None):
            dup = self.dup if dup is None else dup
            return unfold(ids, (self.dgate, dup), self.lows[RANK:], mlp_in, (w_mg, w_mu),
                          size, blocks)

        def dz(self, parts):
            self.dmid, = rms_back(middle, grad, parts, gain_mlp, (BF,))
            return self.dmid

        def fold_down(self, hid):
            return fold(ids, hid, down_in, down_back, w_d)[:4]

        def output(self, parts):
            return (middle.astype(F32) + (
                parts[0].astype(F32) + parts[1].astype(F32) + parts[2].astype(F32)
            )).astype(BF)

        def early(self, lows):
            mark = jnp.full((RANK, span), work_id, F32).astype(BF)
            return jnp.concatenate(
                [share(lows, span, ((RANK, dy), (2 * RANK, b))),
                 halves(jnp.concatenate([self.grad_hidden, self.grad_down])), mark]
            )

        def gate_back(self, dz, half):
            if half == 0:
                self.grad_out_in = self.grad_gate = jnp.zeros((RANK, wide), F32)
                self.dpg, self.dret, self.low_parts = (), (), ()
            dpg, dret, _, dlow, self.grad_out_in, self.grad_gate = gate_back(
                ids, dz, out_back, out_in, gate, nrm, inverse, o, low_a, g_out, w_o, half,
                self.grad_out_in, self.grad_gate
            )
            self.dpg, self.dret = self.dpg + (dpg,), self.dret + (dret,)
            self.low_parts = self.low_parts + (dlow,)
            return dret

        def late_lows(self):
            return jnp.concatenate([self.dlow, low_o])

        def retention_back(self, *dret):
            (self.dpq, self.dpk, self.dpv, self.dlow, self.grad_q, self.grad_k,
             self.grad_v) = retention_back(
                spots, rates, seg_col, seg_row, cosine, sine_table, low_a,
                jnp.concatenate(self.low_parts, axis=1), qk_out, v_out, qk, v, *dret
            )
            return self.dpv

        def late(self, lows, dz):
            return jnp.concatenate(
                [share(lows, span, ((4 * RANK, a), (RANK, dz))),
                 halves(jnp.concatenate(
                     [jnp.concatenate([self.grad_q, self.grad_k], axis=1), self.grad_v,
                      self.grad_gate.astype(BF), self.grad_out_in.astype(BF)]
                 ))]
            )

        def unfold_attn(self, size, blocks, dpv=None):
            dpv = self.dpv if dpv is None else dpv
            return unfold(ids, (self.dpq, self.dpk, dpv, self.dpg), self.dlow, attn_in,
                          (w_qk, w_v, w_g), size, blocks)

        def dx(self, parts):
            return rms_back(x, self.dmid, parts, gain_attn, (F32, BF))

        def place_early(self, arrays, at):
            sequences = sum(array.shape[0] for array in arrays)
            shares = nt * self.early_height
            marks = [array[:, shares + 6 * RANK, 0] for array in arrays]
            all_ids = jnp.concatenate(marks).astype(jnp.int32)[at]
            numbers = jnp.arange(adapters, dtype=jnp.int32)
            chosen = numbers[:, None] == all_ids[None, :]
            if sequences == adapters:
                self.order = jnp.sum(jnp.where(chosen, numbers[None, :], 0), axis=1)
                self.total = None
            else:
                self.order = numbers
                self.total = lambda y: jnp.einsum(
                    "es,sij->eij", chosen.astype(BF), y, preferred_element_type=F32
                )
                arrays, at = [self.total(arrays[0])], numbers
            pitch = self.early_height
            return place(
                at[self.order], arrays,
                ((0, RANK, "shares", pitch), (RANK, 2 * RANK, "shares", pitch),
                 (shares, 2 * RANK, "halves", 3 * RANK),
                 (shares + 2 * RANK, RANK, "halves", 3 * RANK)), nt
            )

        def place_late(self, arrays, at):
            if self.total is not None:
                arrays, at = [self.total(arrays[0])], self.order
            pitch = self.late_height
            shares = nt * pitch
            return place(
                at[self.order], arrays,
                ((0, 4 * RANK, "shares", pitch), (4 * RANK, RANK, "shares", pitch),
                 (shares, RANK, "two", 4 * RANK), (shares + RANK, 2 * RANK, "halves", 4 * RANK),
                 (shares + 3 * RANK, RANK, "halves", 4 * RANK)), nt
            )

    output, input_grad, early, late = links.backward(Back())
    down_back_out, mlp_out, hidden_out, down_out = early
    attn_out, out_back_out, qk_grads, vg_grads, out_out = late
    return (
        output[None],
        input_grad[None],
        jnp.swapaxes(attn_out, 1, 2),
        qk_grads,
        vg_grads.reshape(adapters, 2, RANK, wide),
        jnp.swapaxes(out_out, 1, 2),
        out_back_out,
        jnp.swapaxes(mlp_out, 1, 2),
        hidden_out.reshape(adapters, 2, RANK, wide),
        jnp.swapaxes(down_out, 1, 2),
        down_back_out,
    )


def solution(mesh):
    in_specs = (
        P("dp", "tensor", None),
        P("dp", "tensor", None),
        P("dp", None),
        P("dp", None),
        P(),
        P(),
        P("dp", "tensor"),
        P("dp", "tensor"),
        P("dp", "tensor"),
        P("dp", "tensor"),
        P("tensor", "dp"),
        P("dp", "tensor"),
        P("dp", "tensor"),
        P("tensor", "dp"),
        P(),
        P(None, None, None, "tensor"),
        P(None, None, None, "tensor"),
        P(None, "tensor", None),
        P(),
        P(),
        P(None, None, None, "tensor"),
        P(None, "tensor", None),
        P(),
    )
    out_specs = (
        P("dp", "tensor", None),
        P("dp", "tensor", None),
        P(),
        P(None, None, None, "tensor"),
        P(None, None, None, "tensor"),
        P(None, "tensor", None),
        P(),
        P(),
        P(None, None, None, "tensor"),
        P(None, "tensor", None),
        P(),
    )
    local = partial(shards, mesh.shape["dp"], mesh.shape["tensor"])
    return jax.shard_map(local, mesh=mesh, in_specs=in_specs, out_specs=out_specs, check_vma=False)
```

```python
from functools import partial

import jax
import jax.numpy as jnp
from jax import lax
from jax.experimental import pallas as pl
from jax.experimental.pallas import tpu as pltpu
from jax.sharding import PartitionSpec as P

KEY_DIM = 256
VALUE_DIM = 512
RANK = 16
HALF = KEY_DIM // 2

rms_epsilon = 1e-06
group_floor = 1.0
BF = jnp.bfloat16
F32 = jnp.float32


def dot(a, b):
    return jnp.dot(a, b, preferred_element_type=F32)


def dot_nt(a, b):
    return lax.dot_general(a, b, (((1,), (1,)), ((), ())), preferred_element_type=F32)


def dot_tn(a, b):
    return lax.dot_general(a, b, (((0,), (0,)), ((), ())), preferred_element_type=F32)


def aligned(start, size):
    return pl.ds(pl.multiple_of(start, size), size)


def params(mib):
    return pltpu.CompilerParams(
        vmem_limit_bytes=mib << 20, dimension_semantics=("arbitrary",)
    )


def estimate(flops, moved):
    return pl.CostEstimate(flops=1, bytes_accessed=1, transcendentals=0)


def full(shape):
    return pl.BlockSpec(shape, lambda *_: (0,) * len(shape))


def in_hbm(*arrays):
    return [pltpu.with_memory_space_constraint(array, pltpu.HBM) for array in arrays]


def far(shape, kind):
    return pltpu.HBM(shape, kind)


def smem():
    return pl.BlockSpec(memory_space=pltpu.SMEM)


def columns(refs, ids, begin=0, end=None):
    count = ids.shape[0]
    width = refs[0].shape[1] // count
    if count == 1:
        return all_rows(refs)
    chosen = range(begin, count if end is None else end)
    return jnp.concatenate(
        [
            jnp.concatenate([ref[:, aligned(ids[i] * width, width)] for i in chosen], axis=1)
            for ref in refs
        ],
        axis=0,
    )


def all_rows(refs):
    return refs[0][...] if len(refs) == 1 else jnp.concatenate([ref[...] for ref in refs], axis=0)


def low_rows(low_in, refs):
    return jnp.concatenate([dot_nt(low_in, ref[...]) for ref in refs], axis=1)


def whole(arrays):
    return [full(array.shape) for array in arrays]


def row_count(arrays):
    return sum(array.shape[0] for array in arrays)


def stacked(refs):
    return jnp.concatenate([w[s] for w in refs for s in range(w.shape[0])], axis=0)


def rotated(values, cosine, sine_table):
    first = values[:, :HALF]
    second = values[:, HALF:]
    return jnp.concatenate(
        [first * cosine - second * sine_table, second * cosine + first * sine_table], axis=1
    )


def unrotated(values, cosine, sine_table):
    first = values[:, :HALF]
    second = values[:, HALF:]
    return jnp.concatenate(
        [first * cosine + second * sine_table, second * cosine - first * sine_table], axis=1
    )


def norm_kernel(x, gain, out):
    rows = x[...].astype(F32)
    inverse = lax.rsqrt(jnp.mean(rows * rows, axis=1, keepdims=True) + rms_epsilon)
    out[...] = (rows * inverse * gain[...]).astype(BF)


def norm_rows(x, gain):
    return pl.pallas_call(
        norm_kernel,
        out_shape=far(x.shape, BF),
        compiler_params=pltpu.CompilerParams(vmem_limit_bytes=24 << 20),
        name="norm_rows",
    )(x, gain)


def piece_specs(pieces, width):
    return [
        pl.BlockSpec((w.shape[0], w.shape[1], width), lambda n: (0, 0, n)) for w in pieces
    ]


def project_kernel(layout, ids, chunks, low_in, low_out, *refs):
    parts, count, lengths, turn = layout
    if turn:
        (cosine, sine_table), refs = refs[:2], refs[2:]
    act, refs = refs[:parts], refs[parts:]
    groups = len(lengths)
    pieces, outs = refs[:groups * count], refs[groups * count:]
    if turn:
        low = outs[-1]

        @pl.when(pl.program_id(0) == 0)
        def _():
            low[...] = low_rows(low_in[...], act).astype(BF)
    else:
        low = low_in
    n = pl.program_id(0)
    begin = 0
    for i, length in enumerate(lengths):

        @pl.when((n >= begin) & (n < begin + length))
        def _(i=i, length=length):
            made = dot(columns(act, ids), stacked(pieces[i * count:(i + 1) * count]))
            made = made + dot_tn(low[...], low_out[...])
            if i > 0 or not turn:
                outs[i][...] = made.astype(BF)
                return
            scale = jnp.where(n >= length // 2, 1.0 / KEY_DIM**0.5, 1.0)
            size = made.shape[0] // chunks.shape[0]
            for j in range(chunks.shape[0]):
                at = aligned(chunks[j] * size, size)
                rows = slice(j * size, (j + 1) * size)
                turned = rotated(made[rows], cosine[at, :], sine_table[at, :])
                outs[i][rows, :] = (scale * turned).astype(BF)

        begin += length


def project(ids, chunks, act, low_in, low_out, weights, turn):
    rows, depth = row_count(act), act[0].shape[1]
    block = KEY_DIM
    lengths = tuple(w[0].shape[2] // block for w in weights)
    begins = [sum(lengths[:i]) for i in range(len(lengths))]

    def at(group):
        return lambda n: jnp.clip(n - begins[group], 0, lengths[group] - 1)

    pieces = [
        pl.BlockSpec((w.shape[0], w.shape[1], block), lambda n, at=at(i): (0, 0, at(n)))
        for i, weight in enumerate(weights) for w in weight
    ]
    outs = [pl.BlockSpec((rows, block), lambda n, at=at(i): (0, at(n))) for i in range(len(weights))]
    shapes = [far((rows, length * block), BF) for length in lengths]
    ranks = low_in.shape[0]
    if turn:
        outs.append(full((ranks, rows)))
        shapes.append(jax.ShapeDtypeStruct((ranks, rows), BF))
    return pl.pallas_call(
        partial(project_kernel, (len(act), len(weights[0]), lengths, bool(turn))),
        grid=(sum(lengths),),
        in_specs=[smem(), smem(), full(low_in.shape),
                  pl.BlockSpec((ranks, block), lambda n: (0, n))]
        + whole(turn) + whole(act) + pieces,
        out_specs=outs,
        out_shape=shapes,
        compiler_params=params(48),
        cost_estimate=estimate(0, 0),
        name="project",
    )(ids, chunks, low_in, low_out, *turn, *in_hbm(*act, *[w for x in weights for w in x]))


def decay_factors(rate, size):
    down = lax.broadcasted_iota(jnp.int32, (size, 1), 0).astype(F32)
    across = lax.broadcasted_iota(jnp.int32, (1, size), 1).astype(F32)
    return down, across


def retention_kernel(spots, rates, seg_col, seg_row, q, k, v, gate, out, nrm, inverse):
    rate = rates[pl.program_id(0)]
    count = spots.shape[0]
    size = q.shape[0] // count
    down, across = decay_factors(rate, size)
    row_factor = jnp.exp(rate * down)
    for i in range(count):
        here = aligned(spots[i] * size, size)
        query = q[here, :]
        seg_here = seg_col[i * size:(i + 1) * size, :]
        total = jnp.zeros((size, v.shape[1]), F32)
        for j in range(i + 1):
            there = aligned(spots[j] * size, size)
            column_factor = jnp.exp(rate * ((i - j) * size - across))
            alive = seg_here == seg_row[:, j * size:(j + 1) * size]
            if i == j:
                alive = alive & (down >= across)
            scores = dot_nt(query, k[there, :])
            mixed = jnp.where(alive, scores * row_factor * column_factor, 0.0).astype(BF)
            total = total + dot(mixed, v[there, :])
        centered = total - jnp.mean(total, axis=1, keepdims=True)
        scale = lax.rsqrt(jnp.mean(centered * centered, axis=1, keepdims=True) + group_floor)
        normed = centered * scale
        level = gate[here, :].astype(F32)
        out[here, :] = (level / (1.0 + jnp.exp(-level)) * normed).astype(BF)
        nrm[here, :] = normed.astype(nrm.dtype)
        inverse[0, here, :] = jnp.broadcast_to(scale, (size, 128))


def retention(spots, rates, seg_col, seg_row, qk, v, gate):
    rows = qk.shape[0]
    heads = v.shape[1] // VALUE_DIM
    return pl.pallas_call(
        retention_kernel,
        grid=(heads,),
        in_specs=[smem(), smem(), full(seg_col.shape), full(seg_row.shape),
                  pl.BlockSpec((rows, KEY_DIM), lambda h: (0, h)),
                  pl.BlockSpec((rows, KEY_DIM), lambda h: (0, h + heads)),
                  pl.BlockSpec((rows, VALUE_DIM), lambda h: (0, h)),
                  pl.BlockSpec((rows, VALUE_DIM), lambda h: (0, h))],
        out_specs=[pl.BlockSpec((rows, VALUE_DIM), lambda h: (0, h)),
                   pl.BlockSpec((rows, VALUE_DIM), lambda h: (0, h)),
                   pl.BlockSpec((1, rows, 128), lambda h: (h, 0, 0))],
        out_shape=[far(v.shape, BF), far(v.shape, BF),
                   far((heads, rows, 128), F32)],
        compiler_params=params(40),
        cost_estimate=estimate(2 * rows * rows * 768 * heads, 30 << 20),
        name="retention",
    )(spots, rates, seg_col, seg_row, qk, qk, *in_hbm(v, gate))


def fold_kernel(ids, act, low_in, low_out, *refs):
    pieces, (outs, low) = refs[:-5], (refs[-5:-1], refs[-1])
    step = pl.program_id(0)
    subs = pl.num_programs(0)
    width = pieces[0].shape[2]
    size = outs[0].shape[0]

    @pl.when(step == 0)
    def _():
        low[...] = dot_nt(low_in[...], act[...])

    extra = low[...].astype(BF)
    rows = act[...]
    for i, piece in enumerate(pieces):
        at = aligned(ids[i * subs + step] * width, width)
        product = (dot(rows, piece[0]) + dot_tn(extra, low_out[:, at])).astype(BF)
        for j, out in enumerate(outs):
            out[:, at] = product[j * size:(j + 1) * size]


def fold(ids, act, low_in, low_out, pieces):
    rows, depth = act.shape
    subs = pieces[0].shape[0]
    width = low_out.shape[1]
    return pl.pallas_call(
        fold_kernel,
        grid=(subs,),
        in_specs=[smem(), full(act.shape), full(low_in.shape), full(low_out.shape)]
        + [pl.BlockSpec((1,) + w.shape[1:], lambda s: (s, 0, 0)) for w in pieces],
        out_specs=[full((rows // 4, width))] * 4 + [full((low_in.shape[0], rows))],
        out_shape=[far((rows // 4, width), BF)] * 4
        + [jax.ShapeDtypeStruct((low_in.shape[0], rows), F32)],
        compiler_params=params(48),
        cost_estimate=estimate(2 * rows * depth * width, 2 * depth * width + 4 * rows * depth),
        name="fold",
    )(ids, act, low_in, low_out, *pieces)


def join_kernel(x, part0, part1, part2, gain, middle, normed):
    rows = x[...].astype(F32) + (
        part0[...].astype(F32) + part1[...].astype(F32) + part2[...].astype(F32)
    )
    inverse = lax.rsqrt(jnp.mean(rows * rows, axis=1, keepdims=True) + rms_epsilon)
    middle[...] = rows.astype(BF)
    normed[...] = (rows * inverse * gain[...]).astype(BF)


def join_rows(x, parts, gain):
    return pl.pallas_call(
        join_kernel,
        out_shape=[jax.ShapeDtypeStruct(x.shape, BF), jax.ShapeDtypeStruct(x.shape, BF)],
        compiler_params=pltpu.CompilerParams(vmem_limit_bytes=24 << 20),
        name="join_rows",
    )(x, *parts, gain)


def rms_back_kernel(rows_in, grad_in, part0, part1, part2, gain, *outs):
    rows = rows_in[...].astype(F32)
    inverse = lax.rsqrt(jnp.mean(rows * rows, axis=1, keepdims=True) + rms_epsilon)
    normed = rows * inverse
    scaled = gain[...] * (
        part0[...].astype(F32) + part1[...].astype(F32) + part2[...].astype(F32)
    )
    result = grad_in[...].astype(F32) + inverse * (
        scaled - normed * jnp.mean(scaled * normed, axis=1, keepdims=True)
    )
    for out in outs:
        out[...] = result.astype(out.dtype)


def rms_back(rows_in, grad_in, parts, gain, kinds):
    count, width = rows_in.shape
    block = pl.BlockSpec((count // 2, width), lambda i: (i, 0))
    return pl.pallas_call(
        rms_back_kernel,
        grid=(2,),
        in_specs=[block] * 5 + [full(gain.shape)],
        out_specs=[block] * len(kinds),
        out_shape=[far((count, width), kind) for kind in kinds],
        compiler_params=params(24),
        name="rms_back",
    )(rows_in, grad_in, *parts, gain)


def hidden_grad_kernel(parts, ids, low_back, low_in, *refs):
    act, pieces, (out, low) = refs[:parts], refs[parts:-2], refs[-2:]

    @pl.when(pl.program_id(0) == 0)
    def _():
        low[...] = low_rows(low_back[...], act).astype(BF)

    weights = jnp.concatenate([w[s] for w in pieces for s in range(w.shape[0])], axis=1)
    out[...] = (dot_nt(columns(act, ids), weights) + dot_tn(low[...], low_in[...])).astype(BF)


def hidden_grad(ids, act, low_back, low_in, pieces):
    rows, depth = row_count(act), act[0].shape[1]
    width = pieces[0].shape[1]
    block = 256
    return pl.pallas_call(
        partial(hidden_grad_kernel, len(act)),
        grid=(width // block,),
        in_specs=[smem(), full(low_back.shape),
                  pl.BlockSpec((low_in.shape[0], block), lambda n: (0, n))]
        + whole(act) + [pl.BlockSpec((w.shape[0], block, w.shape[2]), lambda n: (0, n, 0)) for w in pieces],
        out_specs=[pl.BlockSpec((rows, block), lambda n: (0, n)),
                   full((low_back.shape[0], rows))],
        out_shape=[far((rows, width), BF),
                   jax.ShapeDtypeStruct((low_back.shape[0], rows), BF)],
        compiler_params=params(40),
        cost_estimate=estimate(2 * rows * depth * width, 2 * depth * width + 8 * rows * depth),
        name="hidden_grad",
    )(ids, low_back, low_in, *act, *pieces)


def mlp_begin_kernel(parts, count, ids, low_in, *refs):
    act, refs = refs[:parts], refs[parts:]
    gate_pieces, up_pieces = refs[:count], refs[count:2 * count]
    gate, up, low = refs[2 * count:]

    @pl.when(pl.program_id(0) == 0)
    def _():
        low[...] = low_rows(low_in[...], act).astype(BF)

    rows = columns(act, ids, 0, sum(w.shape[0] for w in gate_pieces))
    gate[...] = dot(rows, stacked(gate_pieces))
    up[...] = dot(rows, stacked(up_pieces))


def mlp_begin(ids, act, low_in, gate_pieces, up_pieces):
    rows, depth = row_count(act), act[0].shape[1]
    width = gate_pieces[0].shape[2]
    block = 256
    ranks = low_in.shape[0]
    column = pl.BlockSpec((rows, block), lambda n: (0, n))
    return pl.pallas_call(
        partial(mlp_begin_kernel, len(act), len(gate_pieces)),
        grid=(width // block,),
        in_specs=[smem(), full(low_in.shape)] + whole(act) + piece_specs(gate_pieces, block)
        + piece_specs(up_pieces, block),
        out_specs=[column, column, full((ranks, rows))],
        out_shape=[far((rows, width), F32)] * 2 + [jax.ShapeDtypeStruct((ranks, rows), BF)],
        compiler_params=params(48),
        cost_estimate=estimate(0, 0),
        name="mlp_begin",
    )(ids, low_in, *act, *gate_pieces, *up_pieces)


def mlp_kernel(parts, count, ids, gate_in, up_in, low, gate_out, up_out, down_in, grad, grad_low,
               *refs):
    act, refs = refs[:parts], refs[parts:]
    gate_pieces, up_pieces = refs[:count], refs[count:2 * count]
    hid, dgate, dup, lows, grad_hidden, grad_down = refs[2 * count:]

    @pl.when(pl.program_id(0) == 0)
    def _():
        lows[...] = jnp.zeros(lows.shape, F32)

    extra = low[...]
    gate = gate_in[...] + dot_tn(extra, gate_out[...])
    up = up_in[...] + dot_tn(extra, up_out[...])
    if count:
        last = sum(w.shape[0] for w in gate_pieces)
        rows = columns(act, ids, ids.shape[0] - last)
        gate = gate + dot(rows, stacked(gate_pieces))
        up = up + dot(rows, stacked(up_pieces))
    chance = 0.5 * (1.0 + lax.erf(gate * (0.5**0.5)))
    active = gate * chance
    slope = chance + gate * (jnp.exp(-0.5 * gate * gate) * 0.3989422804014327)
    hidden = (active * up).astype(BF)
    back = grad[...].astype(F32)
    back_gate = (back * up * slope).astype(BF)
    back_up = (back * active).astype(BF)
    hid[...] = hidden
    dgate[...] = back_gate
    dup[...] = back_up
    lows[:RANK, :] += dot_nt(down_in[...], hidden)
    lows[RANK:, :] += dot_nt(gate_out[...], back_gate) + dot_nt(up_out[...], back_up)
    grad_hidden[:RANK, :] = dot(extra[:RANK], back_gate).astype(BF)
    grad_hidden[RANK:, :] = dot(extra[RANK:], back_up).astype(BF)
    grad_down[...] = dot(grad_low[...], hidden).astype(BF)


def mlp(ids, begun, act, gate_out, up_out, down_in, grad, grad_low, gate_pieces, up_pieces):
    gate_in, up_in, low = begun
    rows, width = gate_in.shape
    block = 256
    ranks = low.shape[0]
    column = lambda height: pl.BlockSpec((height, block), lambda n: (0, n))
    return pl.pallas_call(
        partial(mlp_kernel, len(act), len(gate_pieces)),
        grid=(width // block,),
        in_specs=[smem(), column(rows), column(rows), full(low.shape), column(ranks),
                  column(ranks), column(down_in.shape[0]), column(rows), full(grad_low.shape)]
        + whole(act) + piece_specs(gate_pieces, block) + piece_specs(up_pieces, block),
        out_specs=[column(rows), column(rows), column(rows), full((ranks + RANK, rows)),
                   column(ranks), column(grad_low.shape[0])],
        out_shape=[jax.ShapeDtypeStruct((rows, width), BF)] * 3
        + [jax.ShapeDtypeStruct((ranks + RANK, rows), F32),
           jax.ShapeDtypeStruct((ranks, width), BF),
           jax.ShapeDtypeStruct((grad_low.shape[0], width), BF)],
        compiler_params=params(48),
        cost_estimate=estimate(0, 0),
        name="mlp",
    )(ids, gate_in, up_in, low, gate_out, up_out, down_in, grad, grad_low, *act, *gate_pieces,
      *up_pieces)


def unfold_kernel(layout, ids, low_in, *refs):
    blocks, count, weights = layout
    lows, refs = refs[:blocks], refs[blocks:]
    acts, pieces, outs = refs[:blocks * count], refs[blocks * count:-blocks], refs[-blocks:]
    size = outs[0].shape[0]
    step = pl.program_id(0)
    subs = pl.num_programs(0)
    width = pieces[0].shape[1]
    extra = jnp.concatenate([low[...] for low in lows], axis=1).T.astype(BF)
    per = len(pieces) // weights
    rows = jnp.concatenate(
        [jnp.concatenate([act[...] for act in acts[i * count:(i + 1) * count]], axis=1)
         for i in range(blocks)], axis=0
    )
    for i in range(per):
        at = aligned(ids[i * subs + step] * width, width)
        weight = jnp.concatenate([pieces[k * per + i][0] for k in range(weights)], axis=1)
        product = (dot_nt(rows, weight) + dot(extra, low_in[:, at])).astype(BF)
        for j, out in enumerate(outs):
            out[:, at] = product[j * size:(j + 1) * size]


def unfold(ids, acts, low, low_in, weights, size, blocks):
    subs = weights[0][0].shape[0]
    width = low_in.shape[1]
    pieces = [piece for weight in weights for piece in weight]
    count = len(blocks)
    chosen = []
    for at in blocks:
        for act in acts:
            if isinstance(act, tuple):
                per = act[0].shape[0] // size
                chosen.append((act[at // per], at % per))
            else:
                chosen.append((act, at))
    depth = sum(act.shape[1] for act, _ in chosen) // count
    return pl.pallas_call(
        partial(unfold_kernel, (count, len(acts), len(weights))),
        grid=(subs,),
        in_specs=[smem(), full(low_in.shape)]
        + [pl.BlockSpec((low.shape[0], size), lambda s, at=at: (0, at)) for at in blocks]
        + [pl.BlockSpec((size, act.shape[1]), lambda s, at=at: (at, 0)) for act, at in chosen]
        + [pl.BlockSpec((1,) + w.shape[1:], lambda s: (s, 0, 0)) for w in pieces],
        out_specs=[full((size, width))] * count,
        out_shape=[far((size, width), BF)] * count,
        compiler_params=params(48),
        cost_estimate=estimate(
            2 * count * size * depth * width, 2 * depth * width + 4 * count * size * depth
        ),
        name="unfold",
    )(ids, low_in, *[low] * count, *in_hbm(*[act for act, _ in chosen], *pieces))


def gate_back_kernel(parts, ids, low_back, low_in, gate, nrm, inverse, hold, low_gate, low_out,
                     begin_in, begin_gate, *refs):
    act, pieces = refs[:parts], refs[parts:-6]
    dgate, dret, low, dlow, grad_in, grad_gate = refs[-6:]

    @pl.when(pl.program_id(0) == 0)
    def _():
        low[...] = low_rows(low_back[...], act).astype(BF)
        dlow[...] = jnp.zeros(dlow.shape, F32)

    weights = jnp.concatenate([w[s] for w in pieces for s in range(w.shape[0])], axis=1)
    back = dot_nt(columns(act, ids), weights) + dot_tn(low[...], low_in[...])
    level = gate[...].astype(F32)
    normed = nrm[...].astype(F32)
    chance = 1.0 / (1.0 + jnp.exp(-level))
    slope = chance * (1.0 + level * (1.0 - chance))
    back_gate = (back * normed * slope).astype(BF)
    grad = back * (level * chance)
    mean = jnp.mean(grad, axis=1, keepdims=True)
    along = jnp.mean(grad * normed, axis=1, keepdims=True)
    dgate[...] = back_gate
    dret[...] = (inverse[0, :, :1] * (grad - mean - normed * along)).astype(BF)
    grad_in[...] = begin_in[...] + dot(low[...], hold[...])
    grad_gate[...] = begin_gate[...] + dot(low_gate[...], back_gate)
    dlow[...] += dot_nt(low_out[...], back_gate)


def gate_back(ids, act, low_back, low_in, gate, nrm, inverse, hold, low_gate, low_out, pieces,
              half, begin_in, begin_gate):
    if len(act) > 1:
        act = act[len(act) // 2 * half:len(act) // 2 * (half + 1)]
    rows, depth = gate.shape[0] // 2, act[0].shape[1]
    width = gate.shape[1]
    block = VALUE_DIM
    ranks = low_back.shape[0]
    if len(act) == 1:
        acts = [pl.BlockSpec((rows, depth), lambda n: (half, 0))]
    else:
        acts = whole(act)
    column = lambda height: pl.BlockSpec((height, block), lambda n: (0, n))
    place = pl.BlockSpec((rows, block), lambda n: (half, n))
    return pl.pallas_call(
        partial(gate_back_kernel, len(act)),
        grid=(width // block,),
        in_specs=[smem(), full(low_back.shape), column(ranks), place, place,
                  pl.BlockSpec((1, rows, 128), lambda n: (n, half, 0)), place,
                  pl.BlockSpec((ranks, rows), lambda n: (low_gate.shape[0] // ranks - 1, half)),
                  column(low_out.shape[0]), column(ranks), column(ranks)]
        + acts + [pl.BlockSpec((w.shape[0], block, w.shape[2]), lambda n: (0, n, 0))
                  for w in pieces],
        out_specs=[column(rows), column(rows), full((ranks, rows)),
                   full((low_out.shape[0], rows)), column(ranks), column(ranks)],
        out_shape=[jax.ShapeDtypeStruct((rows, width), BF)] * 2
        + [jax.ShapeDtypeStruct((ranks, rows), BF),
           jax.ShapeDtypeStruct((low_out.shape[0], rows), F32),
           jax.ShapeDtypeStruct((ranks, width), F32), jax.ShapeDtypeStruct((ranks, width), F32)],
        compiler_params=params(56),
        cost_estimate=estimate(2 * rows * depth * width, 2 * depth * width + 16 * rows * width),
        name="gate_back",
    )(ids, low_back, low_in, *in_hbm(gate, nrm, inverse, hold), low_gate, low_out, begin_in,
      begin_gate, *act, *pieces)


def retention_back_kernel(spots, rates, seg_col, seg_row, cosine, sine_table, low, begin, q_out,
                          k_out, v_out, q, k, v, dret0, dret1, dq, dk, dv, dlow, grad_q, grad_k,
                          grad_v, sums):
    head = pl.program_id(0)
    rate = rates[head]
    count = spots.shape[0]
    size = q.shape[0] // count
    down, across = decay_factors(rate, size)
    column_factor = jnp.exp(rate * across)
    key_scale = 1.0 / KEY_DIM**0.5

    @pl.when(head == 0)
    def _():
        dlow[...] = begin[...]

    sums[...] = jnp.zeros(sums.shape, F32)
    for j in range(count):
        there = aligned(spots[j] * size, size)
        place = slice(j * size, (j + 1) * size)
        key, value = k[there, :], v[there, :]
        seg_there = seg_col[place, :]
        key_sum = jnp.zeros((size, KEY_DIM), F32)
        value_sum = jnp.zeros((size, VALUE_DIM), F32)
        for i in range(j, count):
            here = aligned(spots[i] * size, size)
            query = q[here, :]
            within = aligned(spots[i] % (count // 2) * size, size)
            back = jnp.where(spots[i] < count // 2, dret0[within, :], dret1[within, :])
            row_factor = jnp.exp(rate * ((i - j) * size - down))
            alive = seg_there == seg_row[:, i * size:(i + 1) * size]
            if i == j:
                alive = alive & (across >= down)
            weight = jnp.where(alive, row_factor * column_factor, 0.0)
            mixed = (dot_nt(key, query) * weight).astype(BF)
            grad = (dot_nt(value, back) * weight).astype(BF)
            value_sum = value_sum + dot(mixed, back)
            key_sum = key_sum + dot(grad, query)
            sums[i * size:(i + 1) * size, :] += dot_tn(grad, key)
        dk[there, :] = (
            key_scale * unrotated(key_sum, cosine[place, :], sine_table[place, :])
        ).astype(BF)
        dv[there, :] = value_sum.astype(BF)
    for i in range(count):
        place = slice(i * size, (i + 1) * size)
        dq[aligned(spots[i] * size, size), :] = unrotated(
            sums[place, :], cosine[place, :], sine_table[place, :]
        ).astype(BF)
    back_q, back_k, back_v = dq[...], dk[...], dv[...]
    dlow[...] += (
        dot_nt(q_out[...], back_q) + dot_nt(k_out[...], back_k) + dot_nt(v_out[...], back_v)
    )
    grad_q[...] = dot(low[:RANK, :], back_q).astype(BF)
    grad_k[...] = dot(low[RANK:2 * RANK, :], back_k).astype(BF)
    grad_v[...] = dot(low[2 * RANK:3 * RANK, :], back_v).astype(BF)


def retention_back(spots, rates, seg_col, seg_row, cosine, sine_table, low, begin, qk_out, v_out,
                   qk, v, dret0, dret1):
    rows = qk.shape[0]
    heads = v.shape[1] // VALUE_DIM
    ranks = low.shape[0]
    key = lambda height: pl.BlockSpec((height, KEY_DIM), lambda h: (0, h))
    later = lambda height: pl.BlockSpec((height, KEY_DIM), lambda h: (0, h + heads))
    value = lambda height: pl.BlockSpec((height, VALUE_DIM), lambda h: (0, h))
    keys = heads * KEY_DIM
    return pl.pallas_call(
        retention_back_kernel,
        grid=(heads,),
        in_specs=[smem(), smem(), full(seg_col.shape), full(seg_row.shape), full(cosine.shape),
                  full(cosine.shape), full(low.shape), full(begin.shape), key(ranks),
                  later(ranks), value(ranks),
                  key(rows), later(rows), value(rows), value(rows // 2), value(rows // 2)],
        out_specs=[key(rows), key(rows), value(rows), full((ranks, rows)), key(RANK), key(RANK),
                   value(RANK)],
        out_shape=[jax.ShapeDtypeStruct((rows, keys), BF), jax.ShapeDtypeStruct((rows, keys), BF),
                   jax.ShapeDtypeStruct(v.shape, BF), jax.ShapeDtypeStruct((ranks, rows), F32),
                   jax.ShapeDtypeStruct((RANK, keys), BF), jax.ShapeDtypeStruct((RANK, keys), BF),
                   jax.ShapeDtypeStruct((RANK, v.shape[1]), BF)],
        scratch_shapes=[pltpu.VMEM((rows, KEY_DIM), F32)],
        compiler_params=params(48),
        cost_estimate=estimate(2 * rows * rows * 1792 * heads, 30 << 20),
        name="retention_back",
    )(spots, rates, seg_col, seg_row,
      cosine, sine_table, low, begin, qk_out, qk_out, v_out, qk, qk, v, dret0, dret1)


def share_kernel(heights, low, *refs):
    out = refs[-1]
    at, first = 0, 0
    for height, parts in heights:
        total = jnp.zeros((height, out.shape[2]), F32)
        begin = 0
        for ref in refs[first:first + parts]:
            end = begin + ref.shape[0]
            total = total + dot(low[at:at + height, begin:end], ref[...])
            begin = end
        out[0, at:at + height, :] = total.astype(BF)
        at, first = at + height, first + parts


def share(low, span, items):
    acts = [array for _, act in items for array in act]
    heights = tuple((height, len(act)) for height, act in items)
    count = acts[0].shape[1] // span
    made = pl.pallas_call(
        partial(share_kernel, heights),
        grid=(count,),
        in_specs=[full(low.shape)]
        + [pl.BlockSpec((act.shape[0], span), lambda i: (0, i)) for act in acts],
        out_specs=pl.BlockSpec((1, low.shape[0], span), lambda i: (i, 0, 0)),
        out_shape=jax.ShapeDtypeStruct((count, low.shape[0], span), BF),
        compiler_params=params(32),
        cost_estimate=estimate(0, 0),
        name="share",
    )(low, *in_hbm(*acts))
    return made.reshape(count * low.shape[0], span)


def place_kernel(layout, arrays, order, *refs):
    packs, outs = refs[:arrays], refs[arrays:]
    pack = packs[0][0]
    if arrays == 2:
        which = order[pl.program_id(0)] >= order[pl.num_programs(0)]
        pack = jnp.where(which, packs[1][0], pack)
    span = pack.shape[1]
    for (begin, height, kind, stride), out in zip(layout, outs):
        if kind == "shares":
            for j in range(out.shape[2] // span):
                rows = pack[begin + stride * j:begin + stride * j + height]
                out[0, :, j * span:(j + 1) * span] = rows.astype(F32)
            continue
        for j in range(2):
            rows = pack[begin + stride * j:begin + stride * j + height].astype(F32)
            if kind == "halves":
                out[0, :, j * span:(j + 1) * span] = rows
            else:
                out[0, j] = rows


def place(order, arrays, layout, shares):
    entries = order.shape[0]
    size, _, span = arrays[0].shape
    shapes = []
    for _, height, kind, _ in layout:
        shapes.append({"shares": (height, shares * span),
                       "halves": (height, 2 * span)}.get(kind, (2, height, span)))

    def spec(number):
        def index(e, o):
            return (jnp.clip(o[e] - number * size, 0, size - 1), 0, 0)
        return pl.BlockSpec((1,) + arrays[0].shape[1:], index)

    order = jnp.concatenate([order, jnp.full((1,), size, jnp.int32)])
    return pl.pallas_call(
        partial(place_kernel, layout, len(arrays)),
        grid_spec=pltpu.PrefetchScalarGridSpec(
            num_scalar_prefetch=1,
            grid=(entries,),
            in_specs=[spec(number) for number in range(len(arrays))],
            out_specs=[
                pl.BlockSpec((1,) + shape, lambda e, o, n=len(shape): (e,) + (0,) * n)
                for shape in shapes
            ],
        ),
        out_shape=[jax.ShapeDtypeStruct((entries,) + shape, F32) for shape in shapes],
        compiler_params=params(32),
        cost_estimate=estimate(0, 10 << 20),
        name="place",
    )(order, *in_hbm(*arrays))


def after(x, *others):
    return lax.optimization_barrier((x,) + others)[0]


class PlainLinks:
    def __init__(self, ndp, nt):
        self.ndp, self.nt = ndp, nt
        self.rank = lax.axis_index("tensor")
        self.chunks = jnp.arange(nt, dtype=jnp.int32)
        self.spots = self.chunks
        self.row_ids = jnp.zeros((1,), jnp.int32)

    def exchange(self, x):
        return x

    def mine(self, own, other):
        return own

    def gather(self, x):
        return [lax.all_gather(x, "tensor", axis=0, tiled=True)]

    def scatter(self, rows):
        total = lax.psum_scatter(
            jnp.concatenate(rows, axis=0), "tensor", scatter_dimension=0, tiled=True
        )
        zero = jnp.zeros_like(total)
        return (total, zero, zero)

    def forward(self, shards, tokens, cotangent, line, steps):
        steps.rotation()
        blocks = [
            [lax.all_gather(shard, "dp", axis=int(shard.shape[1] * self.ndp == tokens.shape[1]),
                            tiled=True)[None]]
            for shard in shards
        ]
        steps.ready(line, steps.tables(line, line)[0])
        a = self.gather(steps.norm(tokens))
        dy = self.gather(cotangent)
        projected = steps.project(a, blocks[1], blocks[0])
        mixed = steps.mix(a, *projected, blocks[2])
        *rows, low = steps.fold(mixed[0], blocks[3])
        middle, b = steps.join(tokens, self.scatter(rows))
        b = self.gather(b)
        begun = steps.mlp_begin(b, blocks[5], blocks[6])
        dhid = (*steps.hidden_grad(dy, blocks[4]), begun, ([], []))
        return blocks, tokens, a, cotangent, dy, projected, mixed, low, middle, b, dhid

    def group_sum(self, x):
        return lax.psum(x.astype(BF), "tensor")

    def backward(self, steps):
        steps.mlp()
        dz = self.gather(steps.dz(self.scatter(steps.unfold_mlp(256, (0, 1, 2, 3)))))
        output = steps.output(self.scatter(steps.fold_down(steps.hid)))
        lows = self.group_sum(steps.early_lows())
        early = lax.all_gather(steps.early(lows), "dp")
        early = steps.place_early([early], jnp.arange(self.ndp, dtype=jnp.int32))
        steps.gate_back(dz, 0)
        steps.gate_back(dz, 1)
        steps.retention_back(*steps.dret)
        late = jnp.concatenate(
            [steps.late_shares(self.group_sum(steps.dlow)), steps.late_rest(lows, dz)]
        )
        late = lax.all_gather(late, "dp")
        late = steps.place_late([late], jnp.arange(self.ndp, dtype=jnp.int32))
        parts = self.scatter(steps.unfold_attn(256, (0, 1, 2, 3)))
        dx, _ = steps.dx(parts)
        return output, dx, early, late


class PairedLinks:
    def __init__(self, ndp, nt):
        self.ndp, self.nt = ndp, nt
        d, t = lax.axis_index("dp"), lax.axis_index("tensor")
        c, p, m = d % 2, t // 2, t % 2
        self.home = c == p
        self.rank = 2 * c + m
        flips = jnp.array([0, 2, 1, 3], jnp.int32)
        self.chunks = self.rank ^ flips
        order = jnp.arange(4, dtype=jnp.int32) ^ self.rank
        self.spots = (order % 2) * 2 + order // 2
        g = d // 2
        self.row_ids = ((2 * (g ^ jnp.arange(4, dtype=jnp.int32))[:, None]
                         + jnp.arange(2, dtype=jnp.int32)[None, :]) ^ c).reshape(-1)
        self.last = {}
        self.last_round = ()
        self.slow = ()

    def pairs(self, place):
        listed = []
        for d in range(self.ndp):
            for t in range(self.nt):
                to = place(d, t)
                if to is not None:
                    listed.append((d * self.nt + t, to[0] * self.nt + to[1]))
        return listed

    def move(self, x, place, chain=None):
        if chain in self.last:
            x = after(x, *self.last[chain])
        moved = lax.ppermute(x, ("dp", "tensor"), self.pairs(place))
        if chain is not None:
            self.last[chain] = (moved,)
        return moved

    def send(self, moves):
        return [lax.ppermute(x, ("dp", "tensor"), self.pairs(place)) for x, place in moves]

    def round(self, moves, work=None, inputs=(), later=(), slow=(), feed=0):
        every = list(moves) + list(slow)
        values = [x for x, _ in every]
        flat, form = jax.tree.flatten((values, inputs))
        last, _ = jax.tree.flatten(self.last_round)
        if last:
            flat = lax.optimization_barrier((*flat, *last))[:len(flat)]
        values, inputs = jax.tree.unflatten(form, flat)
        moved = self.send([(x, place) for x, (_, place) in zip(values, every)])
        moved, slowly = moved[:len(moves)], moved[len(moves):]
        second = []
        if later:
            count, make = later
            moves = make(moved[:count])
            values = [x for x, _ in moves]
            values = lax.optimization_barrier((*values, *moved[:count]))[:len(values)]
            second = self.send([(x, place) for x, (_, place) in zip(values, moves)])
        made = work(*moved[:feed], *inputs) if work is not None else ()
        self.last_round = (moved, second, made, self.slow)
        self.slow = slowly
        return moved + slowly, second, made

    def core(self, x):
        return self.move(x, lambda d, t: (d ^ 1, t))

    def pair(self, x):
        return self.move(x, lambda d, t: (d, t ^ 1), "pair")

    def mine(self, own, other):
        return jnp.where(self.home, own, other)

    def exchange(self, x):
        moved = self.move(
            x, lambda d, t: (d ^ 1, t ^ 2) if d % 2 != t // 2 else None, "middle"
        )
        return jnp.where(self.home, x, moved)

    def gather(self, x):
        across = self.pair(x)
        return [x, self.core(x), across, self.core(across)]

    def forward(self, shards, tokens, cotangent, line, steps):
        by_one = lambda d, t: (d ^ 2, t)
        by_two = lambda d, t: (d ^ 4, t)
        core = lambda d, t: (d ^ 1, t)
        pair = lambda d, t: (d, t ^ 1)
        swap = lambda d, t: (d ^ 1, t ^ 2) if d % 2 != t // 2 else None
        seat = lambda d, t: (d, t ^ 2) if d % 2 == t // 2 else None
        blocks = [[None] * 4 for _ in shards]
        doubled = [jnp.stack([shards[0], self.core(shards[0])])]

        def over(i):
            return (doubled[i], seat)

        def arrived(i, moved):
            blocks[i][0] = self.mine(doubled[i], moved)

        hops = {
            "x": lambda i: (blocks[i][0], by_one),
            "y": lambda i: (blocks[i][0], by_two),
            "xy": lambda i: (blocks[i][1], by_two),
            "yx": lambda i: (blocks[i][2], by_one),
        }
        place_of = {"x": 1, "y": 2, "xy": 3, "yx": 3}

        def go(first, second, others, work=None, inputs=()):
            def later(moved):
                for (i, way), block in zip(first, moved):
                    blocks[i][place_of[way]] = block
                return [hops[way](i) for i, way in second]

            moved, seconds, made = self.round(
                [hops[way](i) for i, way in first] + list(others), work, inputs,
                (len(first), later)
            )
            for (i, way), block in zip(second, seconds):
                blocks[i][place_of[way]] = block
            return moved[len(first):], made

        def double(rest):
            return [jnp.stack([shard, self.core(shard)]) for shard in rest]

        other = self.core(line)
        def begin(rest):
            return double(rest), steps.rotation()

        (moved,), (made, turn) = go([], [], [over(0)], begin, (shards[1:],))
        steps.turn = turn
        doubled += made
        arrived(0, moved)
        (moved,), (home_table, sent_table) = go(
            [(0, "x"), (0, "y")], [], [over(1)], steps.tables, (line, other)
        )
        arrived(1, moved)
        (x, table, moved), _ = go([(1, "x"), (0, "xy")], [(1, "y")],
                                  [(tokens, swap), (sent_table, seat), over(2)])
        arrived(2, moved)
        x = self.mine(tokens, x)
        steps.ready(other, self.mine(home_table, table))
        a = steps.norm(x)
        (across, moved, grad), _ = go([(2, "x"), (2, "y")], [(1, "yx"), (2, "xy")],
                                      [(a, pair), over(3), (cotangent, swap)])
        arrived(3, moved)
        grad = self.mine(cotangent, grad)
        def attend(near, beyond, own, across, *weights):
            a = [own, near, across, beyond]
            return a, steps.project(a, *weights[::-1])

        moves = [(a, core), (across, core), hops["x"](3), hops["y"](3), over(4)]
        moved, _, (a, projected) = self.round(
            moves, attend, (a, across, *blocks[:2]), feed=2
        )
        _, _, blocks[3][1], blocks[3][2], moved = moved
        arrived(4, moved)
        half = grad.shape[0] // 2
        (moved, across0), mixed = go(
            [(4, "x"), (3, "xy")], [], [over(5), (grad[:half], pair)], steps.mix,
            (a, *projected, blocks[2])
        )
        arrived(5, moved)
        (moved, across1), folded = go(
            [(5, "x"), (4, "y")], [], [over(6), (grad[half:], pair)], steps.fold,
            (mixed[0], blocks[3])
        )
        across = jnp.concatenate([across0, across1])
        arrived(6, moved)
        own, near, far, beyond, low = folded
        moves = [(near, core), (beyond, core), hops["yx"](4), hops["y"](5)]
        moved, (far,), _ = self.round(
            moves, later=(2, lambda moved: [(self.add(far, moved[1]), pair)])
        )
        near, _, blocks[4][3], blocks[5][2] = moved
        middle, b = steps.join(x, (own, near, far))
        (far, near_grad, beyond_grad), _ = go([(6, "x"), (6, "y")], [],
                                              [(b, pair), (grad, core), (across, core)])
        dy = [grad, near_grad, across, beyond_grad]

        def beside(near, beyond, own, across, dy, w_d, *weights):
            rows = [own, near, across, beyond]
            return steps.hidden_grad(dy, w_d), rows, steps.mlp_begin(rows, *weights)

        moves = [(b, core), (far, core), hops["yx"](5), hops["xy"](6)]
        moved, _, (dhid, b, begun) = self.round(
            moves, beside, (b, far, dy, blocks[4], blocks[5][:3], blocks[6][:3]), feed=2
        )
        blocks[5][3], blocks[6][3] = moved[2:]
        dhid = (*dhid, begun, (blocks[5][3:], blocks[6][3:]))
        return blocks, x, a, grad, dy, projected, mixed, low, middle, b, dhid

    def add(self, one, two):
        return (one.astype(F32) + two.astype(F32)).astype(BF)

    def core_sum(self, x, other):
        size = x.shape[1] // 4
        other = other.astype(F32)
        return (x + jnp.concatenate(
            [other[:, i * size:(i + 1) * size] for i in (1, 0, 3, 2)], axis=1
        )).astype(BF)

    def pair_sum(self, x, other):
        size = x.shape[1] // 2
        other = jnp.concatenate([other[:, size:], other[:, :size]], axis=1)
        return (x.astype(F32) + other.astype(F32)).astype(BF)

    def both_halves(self, halves, one, two):
        return jnp.concatenate(
            [jnp.concatenate([halves[0], one]),
             jnp.concatenate([halves[1][:1], two[:1], halves[1][1:], two[1:]])], axis=1
        )

    def backward(self, steps):
        pair = lambda d, t: (d, t ^ 1)
        swap = lambda d, t: (d ^ 1, t ^ 2) if d % 2 != t // 2 else None
        by_one = lambda d, t: (d ^ 2, t)
        by_two = lambda d, t: (d ^ 4, t)
        core = lambda d, t: (d ^ 1, t)

        self.last_round = ()
        steps.mlp()
        (lows,), _, (near, far, beyond) = self.round(
            [(steps.early_lows().astype(BF), core)],
            lambda dup: steps.unfold_mlp(256, (1, 2, 3), dup), (steps.dup,)
        )
        lows = self.core_sum(steps.early_lows(), lows)
        (beyond, near, other), _, _ = self.round([(beyond, core), (near, core), (lows, pair)])
        far = self.add(far, beyond)
        half = far.shape[0] // 2
        lows = self.pair_sum(lows, other)
        (far,), _, ((own,), folded, early) = self.round(
            [(far, pair)],
            lambda dup, hid, lows: (steps.unfold_mlp(256, (0,), dup), steps.fold_down(hid),
                                    steps.early(lows)),
            (steps.dup, steps.hid, lows)
        )
        own_out, near_out, far_out, beyond_out = folded
        dz = steps.dz((own, near, far))


        def beside(beyond, dz_near, far, dz):
            return self.add(far, beyond), steps.gate_back([dz, dz_near, dz, dz], 0)

        (_, dz_near, across, near_out), _, (far_out, dret0) = self.round(
            [(beyond_out, core), (dz, core), (dz, pair), (near_out, core)],
            beside, (far_out, dz), feed=2
        )
        (dz_beyond,), _, _ = self.round([(across, core)])
        (moved, far_out), _, dret1 = self.round(
            [(early, swap)],
            lambda across, beyond: steps.gate_back([across, across, across, beyond], 1),
            (across, dz_beyond), slow=[(far_out, pair)]
        )
        early = self.mine(early, moved)
        size = early.shape[0] // 2
        early = [early[:size][None], early[size:][None]]
        (one, two), _, dpv = self.round(
            [(early[0], by_one), (early[1], by_two)], steps.retention_back, (dret0, dret1)
        )
        early = [jnp.concatenate([early[0], one]), jnp.concatenate([early[1], two])]
        dz = [dz, dz_near, across, dz_beyond]

        (dlow,), _, output = self.round(
            [(steps.dlow.astype(BF), core)], lambda *parts: steps.output(parts),
            (own_out, near_out, far_out)
        )
        dlow = self.core_sum(steps.dlow, dlow)
        (other, moved_out, one, two), _, ((own, near, far, beyond), rest) = self.round(
            [(dlow, pair), (output, swap), (early[0], by_two), (early[1], by_one)],
            lambda dpv, lows: (steps.unfold_attn(256, (0, 1, 2, 3), dpv),
                               steps.late_rest(lows, dz)),
            (dpv, lows)
        )
        (beyond, near, moved), _, shares = self.round(
            [(beyond, core), (near, core), (rest, swap)],
            lambda dlow, other: steps.late_shares(self.pair_sum(dlow, other)), (dlow, other)
        )
        rest = self.mine(rest, moved)
        (moved,), _, (far, early) = self.round(
            [(shares, swap)],
            lambda far, beyond, *early: (self.add(far, beyond), self.both_halves(*early)),
            (far, beyond, early, one, two)
        )
        late = [self.mine(shares, moved)[None], rest[None]]
        (one, two, far0), _, _ = self.round(
            [(late[0], by_one), (late[1], by_two), (far[:half], pair)]
        )
        late = [jnp.concatenate([late[0], one]), jnp.concatenate([late[1], two])]
        (one, two, far1), _, _ = self.round(
            [(late[0], by_two), (late[1], by_one), (far[half:], pair)]
        )
        dx, low = steps.dx((own, near, jnp.concatenate([far0, far1])))
        late = self.both_halves(late, one, two)
        apart = jnp.arange(self.ndp, dtype=jnp.int32) ^ lax.axis_index("dp")

        def put(early_other, other, early, late):
            at = apart // 2 + 4 * (apart % 2)
            early = steps.place_early([early, early_other], at)
            return early, steps.place_late([late, other], at)

        (_, _, moved), _, (early, late) = self.round(
            [(early, core), (late, core), (low, swap)], put, (early, late), feed=2
        )
        moved, early, late = lax.optimization_barrier((moved, early, late))
        return (self.mine(output, moved_out),
                self.mine(dx, moved.astype(F32)), early, late)


def rotation_tables(seq_length, half_dim):
    positions = jnp.arange(seq_length, dtype=jnp.float32)
    frequency = jnp.exp(-jnp.log(10000.0) * jnp.arange(half_dim, dtype=jnp.float32) / half_dim)
    angles = positions[:, None] * frequency[None, :]
    return (jnp.cos(angles), jnp.sin(angles))


def shards(
    ndp,
    nt,
    tokens,
    cotangent,
    adapter_ids,
    segments,
    norm_attn,
    norm_mlp,
    weight_query,
    weight_key,
    weight_value,
    weight_gate,
    weight_out,
    weight_mlp_gate,
    weight_mlp_up,
    weight_mlp_down,
    adapt_attn_in,
    adapt_query_key,
    adapt_value_gate,
    adapt_out_in,
    adapt_out_back,
    adapt_mlp_in,
    adapt_mlp_hidden,
    adapt_down_in,
    adapt_down_back,
):
    links = PairedLinks(ndp, nt) if (ndp, nt) == (8, 4) else PlainLinks(ndp, nt)
    rank, chunks, spots, ids = links.rank, links.chunks, links.spots, links.row_ids
    adapters = adapt_attn_in.shape[0]
    depth = tokens.shape[2]
    seq_length = segments.shape[1]
    gain_attn, gain_mlp = norm_attn[None], norm_mlp[None]

    def pick(table, which):
        return lax.dynamic_index_in_dim(table, which, 0, keepdims=False)

    def packed(which):
        qk, vg = pick(adapt_query_key, which), pick(adapt_value_gate, which)
        return jnp.concatenate(
            [jnp.concatenate([qk[0], qk[1]], axis=1), vg[0], vg[1],
             pick(adapt_mlp_hidden, which).reshape(2 * RANK, -1),
             pick(adapt_out_in, which).T, pick(adapt_down_in, which).T], axis=0
        )

    own_id = adapter_ids[0, 0]
    own_line = jnp.concatenate([segments, jnp.broadcast_to(adapter_ids, (1, 128))], axis=1)
    wide = weight_gate.shape[1]
    keys = adapt_query_key.shape[3]
    heads_local = wide // VALUE_DIM
    head_ids = (rank * heads_local + jnp.arange(heads_local, dtype=jnp.int32)).astype(F32)
    rates = jnp.log(1.0 - jnp.exp2(-5.0 - head_ids))
    class Steps:
        def tables(self, line, other):
            return packed(line[0, seq_length]), packed(other[0, seq_length])

        def ready(self, other, table):
            line = links.mine(own_line, other)
            self.work_id = work_id = line[0, seq_length]
            self.seg_row = line[:, :seq_length]
            self.seg_col = self.seg_row.reshape(seq_length, 1)
            blank = jnp.zeros((RANK, wide), BF)
            left = jnp.arange(wide)[None, :] < keys
            zero = jnp.zeros((), BF)
            self.qk_out = jnp.concatenate([jnp.where(left, table[:RANK], zero),
                                           jnp.where(left, zero, table[:RANK]), blank, blank])
            self.v_out = jnp.concatenate([blank, blank, table[RANK:2 * RANK], blank])
            self.g_out = jnp.concatenate([blank, blank, blank, table[2 * RANK:3 * RANK]])
            self.mg_out = jnp.concatenate([table[3 * RANK:4 * RANK], blank])
            self.mu_out = jnp.concatenate([blank, table[4 * RANK:5 * RANK]])
            self.out_in = table[5 * RANK:6 * RANK]
            self.down_in = table[6 * RANK:7 * RANK]
            self.attn_in = pick(adapt_attn_in, work_id).T
            self.out_back = pick(adapt_out_back, work_id)
            self.mlp_in = pick(adapt_mlp_in, work_id).T
            self.down_back = pick(adapt_down_back, work_id)

        def rotation(self):
            self.turn = rotation_tables(seq_length, HALF)
            return self.turn

        def norm(self, x):
            return norm_rows(x, gain_attn)

        def project(self, a, w_qk, w_v):
            return project(
                ids, chunks, a, self.attn_in, jnp.concatenate([self.qk_out, self.v_out], axis=1),
                (w_qk, w_v), self.turn
            )

        def mix(self, a, qk, v, low, w_g):
            gate, = project(ids, chunks, a, low, self.g_out, (w_g,), ())
            return (*retention(spots, rates, self.seg_col, self.seg_row, qk, v, gate), gate)

        def fold(self, o, w_o):
            return fold(ids, o, self.out_in, self.out_back, w_o)

        def join(self, x, parts):
            return join_rows(x, parts, gain_mlp)

        def mlp_begin(self, b, w_mg, w_mu):
            return mlp_begin(ids, b, self.mlp_in, w_mg, w_mu)

        def hidden_grad(self, dy, w_d):
            return hidden_grad(ids, dy, self.down_back, self.down_in, w_d)

    steps = Steps()
    ((w_v, w_qk, w_g, w_o, w_d, w_mg, w_mu), x, a, grad, dy, (qk, v, low_a),
     (o, nrm, inverse, gate), low_o, middle, b, (dhid, low_dy, begun, late_weights)) = links.forward(
        [weight_value, jnp.concatenate([weight_query, weight_key], axis=1), weight_gate,
         weight_out, weight_mlp_down, weight_mlp_gate, weight_mlp_up],
        tokens[0], cotangent[0], own_line, steps,
    )
    seg_row, seg_col, work_id = steps.seg_row, steps.seg_col, steps.work_id
    qk_out, v_out, g_out, mg_out, mu_out = (
        steps.qk_out, steps.v_out, steps.g_out, steps.mg_out, steps.mu_out
    )
    attn_in, out_in, out_back = steps.attn_in, steps.out_in, steps.out_back
    mlp_in, down_in, down_back = steps.mlp_in, steps.down_in, steps.down_back

    span = depth // nt
    halves = lambda y: jnp.concatenate([y[:, :wide // 2], y[:, wide // 2:]])

    class Back:
        early_height = 3 * RANK

        def mlp(self):
            (self.hid, self.dgate, self.dup, self.lows, self.grad_hidden,
             self.grad_down) = mlp(
                ids, begun, b, mg_out, mu_out, down_in, dhid, low_dy, *late_weights
            )

        def unfold_mlp(self, size, blocks, dup=None):
            dup = self.dup if dup is None else dup
            return unfold(ids, (self.dgate, dup), self.lows[RANK:], mlp_in, (w_mg, w_mu),
                          size, blocks)

        def dz(self, parts):
            self.dmid, = rms_back(middle, grad, parts, gain_mlp, (BF,))
            return self.dmid

        def fold_down(self, hid):
            return fold(ids, hid, down_in, down_back, w_d)[:4]

        def output(self, parts):
            return (middle.astype(F32) + (
                parts[0].astype(F32) + parts[1].astype(F32) + parts[2].astype(F32)
            )).astype(BF)

        def early_lows(self):
            return jnp.concatenate([self.lows, low_o])

        def early(self, lows):
            mark = jnp.full((RANK, span), work_id, F32).astype(BF)
            return jnp.concatenate(
                [share(lows[:3 * RANK], span, ((RANK, dy), (2 * RANK, b))),
                 halves(jnp.concatenate([self.grad_hidden, self.grad_down])), mark]
            )

        def gate_back(self, dz, half):
            if half == 0:
                self.grad_out_in = self.grad_gate = jnp.zeros((RANK, wide), F32)
                self.dpg, self.dret, self.low_parts = (), (), ()
            dpg, dret, _, dlow, self.grad_out_in, self.grad_gate = gate_back(
                ids, dz, out_back, out_in, gate, nrm, inverse, o, low_a, g_out, w_o, half,
                self.grad_out_in, self.grad_gate
            )
            self.dpg, self.dret = self.dpg + (dpg,), self.dret + (dret,)
            self.low_parts = self.low_parts + (dlow,)
            return dret

        def retention_back(self, *dret):
            (self.dpq, self.dpk, self.dpv, self.dlow, self.grad_q, self.grad_k,
             self.grad_v) = retention_back(
                spots, rates, seg_col, seg_row, *steps.turn, low_a,
                jnp.concatenate(self.low_parts, axis=1), qk_out, v_out, qk, v, *dret
            )
            return self.dpv

        def late_shares(self, lows):
            return share(lows, span, ((4 * RANK, a),))

        def late_rest(self, lows, dz):
            return jnp.concatenate(
                [share(lows[3 * RANK:], span, ((RANK, dz),)),
                 halves(jnp.concatenate(
                     [jnp.concatenate([self.grad_q, self.grad_k], axis=1), self.grad_v,
                      self.grad_gate.astype(BF), self.grad_out_in.astype(BF)]
                 ))]
            )

        def unfold_attn(self, size, blocks, dpv=None):
            dpv = self.dpv if dpv is None else dpv
            return unfold(ids, (self.dpq, self.dpk, dpv, self.dpg), self.dlow, attn_in,
                          (w_qk, w_v, w_g), size, blocks)

        def dx(self, parts):
            return rms_back(x, self.dmid, parts, gain_attn, (F32, BF))

        def place_early(self, arrays, at):
            sequences = sum(array.shape[0] for array in arrays)
            shares = nt * self.early_height
            marks = [array[:, shares + 6 * RANK, 0] for array in arrays]
            all_ids = jnp.concatenate(marks).astype(jnp.int32)[at]
            numbers = jnp.arange(adapters, dtype=jnp.int32)
            chosen = numbers[:, None] == all_ids[None, :]
            if sequences == adapters:
                self.order = jnp.sum(jnp.where(chosen, numbers[None, :], 0), axis=1)
                self.total = None
            else:
                self.order = numbers
                self.total = lambda y: jnp.einsum(
                    "es,sij->eij", chosen.astype(BF), y, preferred_element_type=F32
                )
                arrays, at = [self.total(arrays[0])], numbers
            pitch = self.early_height
            return place(
                at[self.order], arrays,
                ((0, RANK, "shares", pitch), (RANK, 2 * RANK, "shares", pitch),
                 (shares, 2 * RANK, "halves", 3 * RANK),
                 (shares + 2 * RANK, RANK, "halves", 3 * RANK)), nt
            )

        def place_late(self, arrays, at):
            if self.total is not None:
                arrays, at = [self.total(arrays[0])], self.order
            pitch = 4 * RANK
            first, rest = nt * pitch, nt * (pitch + RANK)
            return place(
                at[self.order], arrays,
                ((0, pitch, "shares", pitch), (first, RANK, "shares", RANK),
                 (rest, RANK, "two", 4 * RANK), (rest + RANK, 2 * RANK, "halves", 4 * RANK),
                 (rest + 3 * RANK, RANK, "halves", 4 * RANK)), nt
            )

    output, input_grad, early, late = links.backward(Back())
    down_back_out, mlp_out, hidden_out, down_out = early
    attn_out, out_back_out, qk_grads, vg_grads, out_out = late
    return (
        output[None],
        input_grad[None],
        jnp.swapaxes(attn_out, 1, 2),
        qk_grads,
        vg_grads.reshape(adapters, 2, RANK, wide),
        jnp.swapaxes(out_out, 1, 2),
        out_back_out,
        jnp.swapaxes(mlp_out, 1, 2),
        hidden_out.reshape(adapters, 2, RANK, wide),
        jnp.swapaxes(down_out, 1, 2),
        down_back_out,
    )


def solution(mesh):
    in_specs = (
        P("dp", "tensor", None),
        P("dp", "tensor", None),
        P("dp", None),
        P("dp", None),
        P(),
        P(),
        P("dp", "tensor"),
        P("dp", "tensor"),
        P("dp", "tensor"),
        P("dp", "tensor"),
        P("tensor", "dp"),
        P("dp", "tensor"),
        P("dp", "tensor"),
        P("tensor", "dp"),
        P(),
        P(None, None, None, "tensor"),
        P(None, None, None, "tensor"),
        P(None, "tensor", None),
        P(),
        P(),
        P(None, None, None, "tensor"),
        P(None, "tensor", None),
        P(),
    )
    out_specs = (
        P("dp", "tensor", None),
        P("dp", "tensor", None),
        P(),
        P(None, None, None, "tensor"),
        P(None, None, None, "tensor"),
        P(None, "tensor", None),
        P(),
        P(),
        P(None, None, None, "tensor"),
        P(None, "tensor", None),
        P(),
    )
    local = partial(shards, mesh.shape["dp"], mesh.shape["tensor"])
    return jax.shard_map(local, mesh=mesh, in_specs=in_specs, out_specs=out_specs, check_vma=False)
```

```python
from functools import partial

import jax
import jax.numpy as jnp
from jax import lax
from jax.experimental import pallas as pl
from jax.experimental.pallas import tpu as pltpu
from jax.sharding import PartitionSpec as P

KEY_DIM = 256
VALUE_DIM = 512
RANK = 16
HALF = KEY_DIM // 2

rms_epsilon = 1e-06
group_floor = 1.0
BF = jnp.bfloat16
F32 = jnp.float32


def dot(a, b):
    return jnp.dot(a, b, preferred_element_type=F32)


def dot_nt(a, b):
    return lax.dot_general(a, b, (((1,), (1,)), ((), ())), preferred_element_type=F32)


def dot_tn(a, b):
    return lax.dot_general(a, b, (((0,), (0,)), ((), ())), preferred_element_type=F32)


def aligned(start, size):
    return pl.ds(pl.multiple_of(start, size), size)


def params(mib):
    return pltpu.CompilerParams(
        vmem_limit_bytes=mib << 20, dimension_semantics=("arbitrary",)
    )


def estimate(flops, moved):
    return pl.CostEstimate(flops=1, bytes_accessed=1, transcendentals=0)


def full(shape):
    return pl.BlockSpec(shape, lambda *_: (0,) * len(shape))


def in_hbm(*arrays):
    return [pltpu.with_memory_space_constraint(array, pltpu.HBM) for array in arrays]


def far(shape, kind):
    return pltpu.HBM(shape, kind)


def smem():
    return pl.BlockSpec(memory_space=pltpu.SMEM)


def columns(refs, ids, begin=0, end=None):
    count = ids.shape[0]
    width = refs[0].shape[1] // count
    if count == 1:
        return all_rows(refs)
    chosen = range(begin, count if end is None else end)
    return jnp.concatenate(
        [
            jnp.concatenate([ref[:, aligned(ids[i] * width, width)] for i in chosen], axis=1)
            for ref in refs
        ],
        axis=0,
    )


def all_rows(refs):
    return refs[0][...] if len(refs) == 1 else jnp.concatenate([ref[...] for ref in refs], axis=0)


def low_rows(low_in, refs):
    return jnp.concatenate([dot_nt(low_in, ref[...]) for ref in refs], axis=1)


def whole(arrays):
    return [full(array.shape) for array in arrays]


def row_count(arrays):
    return sum(array.shape[0] for array in arrays)


def stacked(refs):
    return jnp.concatenate([w[s] for w in refs for s in range(w.shape[0])], axis=0)


def rotated(values, cosine, sine_table):
    first = values[:, :HALF]
    second = values[:, HALF:]
    return jnp.concatenate(
        [first * cosine - second * sine_table, second * cosine + first * sine_table], axis=1
    )


def unrotated(values, cosine, sine_table):
    first = values[:, :HALF]
    second = values[:, HALF:]
    return jnp.concatenate(
        [first * cosine + second * sine_table, second * cosine - first * sine_table], axis=1
    )


def norm_kernel(x, gain, out):
    rows = x[...].astype(F32)
    inverse = lax.rsqrt(jnp.mean(rows * rows, axis=1, keepdims=True) + rms_epsilon)
    out[...] = (rows * inverse * gain[...]).astype(BF)


def norm_rows(x, gain):
    return pl.pallas_call(
        norm_kernel,
        out_shape=far(x.shape, BF),
        compiler_params=pltpu.CompilerParams(vmem_limit_bytes=24 << 20),
        name="norm_rows",
    )(x, gain)


def piece_specs(pieces, width):
    return [
        pl.BlockSpec((w.shape[0], w.shape[1], width), lambda n: (0, 0, n)) for w in pieces
    ]


def project_kernel(layout, ids, chunks, low_in, low_out, *refs):
    parts, count, lengths, turn = layout
    if turn:
        (cosine, sine_table), refs = refs[:2], refs[2:]
    act, refs = refs[:parts], refs[parts:]
    groups = len(lengths)
    pieces, outs = refs[:groups * count], refs[groups * count:]
    if turn:
        low = outs[-1]

        @pl.when(pl.program_id(0) == 0)
        def _():
            low[...] = low_rows(low_in[...], act).astype(BF)
    else:
        low = low_in
    n = pl.program_id(0)
    begin = 0
    for i, length in enumerate(lengths):

        @pl.when((n >= begin) & (n < begin + length))
        def _(i=i, length=length):
            made = dot(columns(act, ids), stacked(pieces[i * count:(i + 1) * count]))
            made = made + dot_tn(low[...], low_out[...])
            if i > 0 or not turn:
                outs[i][...] = made.astype(BF)
                return
            scale = jnp.where(n >= length // 2, 1.0 / KEY_DIM**0.5, 1.0)
            size = made.shape[0] // chunks.shape[0]
            for j in range(chunks.shape[0]):
                at = aligned(chunks[j] * size, size)
                rows = slice(j * size, (j + 1) * size)
                turned = rotated(made[rows], cosine[at, :], sine_table[at, :])
                outs[i][rows, :] = (scale * turned).astype(BF)

        begin += length


def project(ids, chunks, act, low_in, low_out, weights, turn):
    rows, depth = row_count(act), act[0].shape[1]
    block = KEY_DIM
    lengths = tuple(w[0].shape[2] // block for w in weights)
    begins = [sum(lengths[:i]) for i in range(len(lengths))]

    def at(group):
        return lambda n: jnp.clip(n - begins[group], 0, lengths[group] - 1)

    pieces = [
        pl.BlockSpec((w.shape[0], w.shape[1], block), lambda n, at=at(i): (0, 0, at(n)))
        for i, weight in enumerate(weights) for w in weight
    ]
    outs = [pl.BlockSpec((rows, block), lambda n, at=at(i): (0, at(n))) for i in range(len(weights))]
    shapes = [far((rows, length * block), BF) for length in lengths]
    ranks = low_in.shape[0]
    if turn:
        outs.append(full((ranks, rows)))
        shapes.append(jax.ShapeDtypeStruct((ranks, rows), BF))
    return pl.pallas_call(
        partial(project_kernel, (len(act), len(weights[0]), lengths, bool(turn))),
        grid=(sum(lengths),),
        in_specs=[smem(), smem(), full(low_in.shape),
                  pl.BlockSpec((ranks, block), lambda n: (0, n))]
        + whole(turn) + whole(act) + pieces,
        out_specs=outs,
        out_shape=shapes,
        compiler_params=params(48),
        cost_estimate=estimate(0, 0),
        name="project",
    )(ids, chunks, low_in, low_out, *turn, *in_hbm(*act, *[w for x in weights for w in x]))


def decay_factors(rate, size):
    down = lax.broadcasted_iota(jnp.int32, (size, 1), 0).astype(F32)
    across = lax.broadcasted_iota(jnp.int32, (1, size), 1).astype(F32)
    return down, across


def retention_kernel(spots, rates, seg_col, seg_row, q, k, v, gate, out, nrm, inverse):
    rate = rates[pl.program_id(0)]
    count = spots.shape[0]
    size = q.shape[0] // count
    down, across = decay_factors(rate, size)
    row_factor = jnp.exp(rate * down)
    for i in range(count):
        here = aligned(spots[i] * size, size)
        query = q[here, :]
        seg_here = seg_col[i * size:(i + 1) * size, :]
        total = jnp.zeros((size, v.shape[1]), F32)
        for j in range(i + 1):
            there = aligned(spots[j] * size, size)
            column_factor = jnp.exp(rate * ((i - j) * size - across))
            alive = seg_here == seg_row[:, j * size:(j + 1) * size]
            if i == j:
                alive = alive & (down >= across)
            scores = dot_nt(query, k[there, :])
            mixed = jnp.where(alive, scores * row_factor * column_factor, 0.0).astype(BF)
            total = total + dot(mixed, v[there, :])
        centered = total - jnp.mean(total, axis=1, keepdims=True)
        scale = lax.rsqrt(jnp.mean(centered * centered, axis=1, keepdims=True) + group_floor)
        normed = centered * scale
        level = gate[here, :].astype(F32)
        out[here, :] = (level / (1.0 + jnp.exp(-level)) * normed).astype(BF)
        nrm[here, :] = normed.astype(nrm.dtype)
        inverse[0, here, :] = jnp.broadcast_to(scale, (size, 128))


def retention(spots, rates, seg_col, seg_row, qk, v, gate):
    rows = qk.shape[0]
    heads = v.shape[1] // VALUE_DIM
    return pl.pallas_call(
        retention_kernel,
        grid=(heads,),
        in_specs=[smem(), smem(), full(seg_col.shape), full(seg_row.shape),
                  pl.BlockSpec((rows, KEY_DIM), lambda h: (0, h)),
                  pl.BlockSpec((rows, KEY_DIM), lambda h: (0, h + heads)),
                  pl.BlockSpec((rows, VALUE_DIM), lambda h: (0, h)),
                  pl.BlockSpec((rows, VALUE_DIM), lambda h: (0, h))],
        out_specs=[pl.BlockSpec((rows, VALUE_DIM), lambda h: (0, h)),
                   pl.BlockSpec((rows, VALUE_DIM), lambda h: (0, h)),
                   pl.BlockSpec((1, rows, 128), lambda h: (h, 0, 0))],
        out_shape=[far(v.shape, BF), far(v.shape, BF),
                   far((heads, rows, 128), F32)],
        compiler_params=params(40),
        cost_estimate=estimate(2 * rows * rows * 768 * heads, 30 << 20),
        name="retention",
    )(spots, rates, seg_col, seg_row, qk, qk, *in_hbm(v, gate))


def fold_kernel(ids, act, low_in, low_out, *refs):
    pieces, (outs, low) = refs[:-5], (refs[-5:-1], refs[-1])
    step = pl.program_id(0)
    subs = pl.num_programs(0)
    width = pieces[0].shape[2]
    size = outs[0].shape[0]

    @pl.when(step == 0)
    def _():
        low[...] = dot_nt(low_in[...], act[...])

    extra = low[...].astype(BF)
    rows = act[...]
    for i, piece in enumerate(pieces):
        at = aligned(ids[i * subs + step] * width, width)
        product = (dot(rows, piece[0]) + dot_tn(extra, low_out[:, at])).astype(BF)
        for j, out in enumerate(outs):
            out[:, at] = product[j * size:(j + 1) * size]


def fold(ids, act, low_in, low_out, pieces):
    rows, depth = act.shape
    subs = pieces[0].shape[0]
    width = low_out.shape[1]
    return pl.pallas_call(
        fold_kernel,
        grid=(subs,),
        in_specs=[smem(), full(act.shape), full(low_in.shape), full(low_out.shape)]
        + [pl.BlockSpec((1,) + w.shape[1:], lambda s: (s, 0, 0)) for w in pieces],
        out_specs=[full((rows // 4, width))] * 4 + [full((low_in.shape[0], rows))],
        out_shape=[far((rows // 4, width), BF)] * 4
        + [jax.ShapeDtypeStruct((low_in.shape[0], rows), F32)],
        compiler_params=params(48),
        cost_estimate=estimate(2 * rows * depth * width, 2 * depth * width + 4 * rows * depth),
        name="fold",
    )(ids, act, low_in, low_out, *pieces)


def join_kernel(x, part0, part1, part2, gain, middle, normed):
    rows = x[...].astype(F32) + (
        part0[...].astype(F32) + part1[...].astype(F32) + part2[...].astype(F32)
    )
    inverse = lax.rsqrt(jnp.mean(rows * rows, axis=1, keepdims=True) + rms_epsilon)
    middle[...] = rows.astype(BF)
    normed[...] = (rows * inverse * gain[...]).astype(BF)


def join_rows(x, parts, gain):
    return pl.pallas_call(
        join_kernel,
        out_shape=[jax.ShapeDtypeStruct(x.shape, BF), jax.ShapeDtypeStruct(x.shape, BF)],
        compiler_params=pltpu.CompilerParams(vmem_limit_bytes=24 << 20),
        name="join_rows",
    )(x, *parts, gain)


def rms_back_kernel(rows_in, grad_in, part0, part1, part2, gain, *outs):
    rows = rows_in[...].astype(F32)
    inverse = lax.rsqrt(jnp.mean(rows * rows, axis=1, keepdims=True) + rms_epsilon)
    normed = rows * inverse
    scaled = gain[...] * (
        part0[...].astype(F32) + part1[...].astype(F32) + part2[...].astype(F32)
    )
    result = grad_in[...].astype(F32) + inverse * (
        scaled - normed * jnp.mean(scaled * normed, axis=1, keepdims=True)
    )
    for out in outs:
        out[...] = result.astype(out.dtype)


def rms_back(rows_in, grad_in, parts, gain, kinds):
    count, width = rows_in.shape
    block = pl.BlockSpec((count // 2, width), lambda i: (i, 0))
    return pl.pallas_call(
        rms_back_kernel,
        grid=(2,),
        in_specs=[block] * 5 + [full(gain.shape)],
        out_specs=[block] * len(kinds),
        out_shape=[far((count, width), kind) for kind in kinds],
        compiler_params=params(24),
        name="rms_back",
    )(rows_in, grad_in, *parts, gain)


def hidden_grad_kernel(parts, ids, low_back, low_in, *refs):
    act, pieces, (out, low) = refs[:parts], refs[parts:-2], refs[-2:]

    @pl.when(pl.program_id(0) == 0)
    def _():
        low[...] = low_rows(low_back[...], act).astype(BF)

    weights = jnp.concatenate([w[s] for w in pieces for s in range(w.shape[0])], axis=1)
    out[...] = (dot_nt(columns(act, ids), weights) + dot_tn(low[...], low_in[...])).astype(BF)


def hidden_grad(ids, act, low_back, low_in, pieces):
    rows, depth = row_count(act), act[0].shape[1]
    width = pieces[0].shape[1]
    block = 256
    return pl.pallas_call(
        partial(hidden_grad_kernel, len(act)),
        grid=(width // block,),
        in_specs=[smem(), full(low_back.shape),
                  pl.BlockSpec((low_in.shape[0], block), lambda n: (0, n))]
        + whole(act) + [pl.BlockSpec((w.shape[0], block, w.shape[2]), lambda n: (0, n, 0)) for w in pieces],
        out_specs=[pl.BlockSpec((rows, block), lambda n: (0, n)),
                   full((low_back.shape[0], rows))],
        out_shape=[far((rows, width), BF),
                   jax.ShapeDtypeStruct((low_back.shape[0], rows), BF)],
        compiler_params=params(40),
        cost_estimate=estimate(2 * rows * depth * width, 2 * depth * width + 8 * rows * depth),
        name="hidden_grad",
    )(ids, low_back, low_in, *act, *pieces)


def mlp_begin_kernel(parts, count, ids, low_in, *refs):
    act, refs = refs[:parts], refs[parts:]
    gate_pieces, up_pieces = refs[:count], refs[count:2 * count]
    gate, up, low = refs[2 * count:]

    @pl.when(pl.program_id(0) == 0)
    def _():
        low[...] = low_rows(low_in[...], act).astype(BF)

    rows = columns(act, ids, 0, sum(w.shape[0] for w in gate_pieces))
    gate[...] = dot(rows, stacked(gate_pieces))
    up[...] = dot(rows, stacked(up_pieces))


def mlp_begin(ids, act, low_in, gate_pieces, up_pieces):
    rows, depth = row_count(act), act[0].shape[1]
    width = gate_pieces[0].shape[2]
    block = 256
    ranks = low_in.shape[0]
    column = pl.BlockSpec((rows, block), lambda n: (0, n))
    return pl.pallas_call(
        partial(mlp_begin_kernel, len(act), len(gate_pieces)),
        grid=(width // block,),
        in_specs=[smem(), full(low_in.shape)] + whole(act) + piece_specs(gate_pieces, block)
        + piece_specs(up_pieces, block),
        out_specs=[column, column, full((ranks, rows))],
        out_shape=[far((rows, width), F32)] * 2 + [jax.ShapeDtypeStruct((ranks, rows), BF)],
        compiler_params=params(48),
        cost_estimate=estimate(0, 0),
        name="mlp_begin",
    )(ids, low_in, *act, *gate_pieces, *up_pieces)


def mlp_kernel(parts, count, ids, gate_in, up_in, low, gate_out, up_out, down_in, grad, grad_low,
               *refs):
    act, refs = refs[:parts], refs[parts:]
    gate_pieces, up_pieces = refs[:count], refs[count:2 * count]
    hid, dgate, dup, lows, grad_hidden, grad_down = refs[2 * count:]

    @pl.when(pl.program_id(0) == 0)
    def _():
        lows[...] = jnp.zeros(lows.shape, F32)

    extra = low[...]
    gate = gate_in[...] + dot_tn(extra, gate_out[...])
    up = up_in[...] + dot_tn(extra, up_out[...])
    if count:
        last = sum(w.shape[0] for w in gate_pieces)
        rows = columns(act, ids, ids.shape[0] - last)
        gate = gate + dot(rows, stacked(gate_pieces))
        up = up + dot(rows, stacked(up_pieces))
    chance = 0.5 * (1.0 + lax.erf(gate * (0.5**0.5)))
    active = gate * chance
    slope = chance + gate * (jnp.exp(-0.5 * gate * gate) * 0.3989422804014327)
    hidden = (active * up).astype(BF)
    back = grad[...].astype(F32)
    back_gate = (back * up * slope).astype(BF)
    back_up = (back * active).astype(BF)
    hid[...] = hidden
    dgate[...] = back_gate
    dup[...] = back_up
    lows[:RANK, :] += dot_nt(down_in[...], hidden)
    lows[RANK:, :] += dot_nt(gate_out[...], back_gate) + dot_nt(up_out[...], back_up)
    grad_hidden[:RANK, :] = dot(extra[:RANK], back_gate).astype(BF)
    grad_hidden[RANK:, :] = dot(extra[RANK:], back_up).astype(BF)
    grad_down[...] = dot(grad_low[...], hidden).astype(BF)


def mlp(ids, begun, act, gate_out, up_out, down_in, grad, grad_low, gate_pieces, up_pieces):
    gate_in, up_in, low = begun
    rows, width = gate_in.shape
    block = 256
    ranks = low.shape[0]
    column = lambda height: pl.BlockSpec((height, block), lambda n: (0, n))
    return pl.pallas_call(
        partial(mlp_kernel, len(act), len(gate_pieces)),
        grid=(width // block,),
        in_specs=[smem(), column(rows), column(rows), full(low.shape), column(ranks),
                  column(ranks), column(down_in.shape[0]), column(rows), full(grad_low.shape)]
        + whole(act) + piece_specs(gate_pieces, block) + piece_specs(up_pieces, block),
        out_specs=[column(rows), column(rows), column(rows), full((ranks + RANK, rows)),
                   column(ranks), column(grad_low.shape[0])],
        out_shape=[jax.ShapeDtypeStruct((rows, width), BF)] * 3
        + [jax.ShapeDtypeStruct((ranks + RANK, rows), F32),
           jax.ShapeDtypeStruct((ranks, width), BF),
           jax.ShapeDtypeStruct((grad_low.shape[0], width), BF)],
        compiler_params=params(48),
        cost_estimate=estimate(0, 0),
        name="mlp",
    )(ids, gate_in, up_in, low, gate_out, up_out, down_in, grad, grad_low, *act, *gate_pieces,
      *up_pieces)


def unfold_kernel(layout, ids, low_in, *refs):
    blocks, count, weights = layout
    lows, refs = refs[:blocks], refs[blocks:]
    acts, pieces, outs = refs[:blocks * count], refs[blocks * count:-blocks], refs[-blocks:]
    size = outs[0].shape[0]
    step = pl.program_id(0)
    subs = pl.num_programs(0)
    width = pieces[0].shape[1]
    extra = jnp.concatenate([low[...] for low in lows], axis=1).T.astype(BF)
    per = len(pieces) // weights
    rows = jnp.concatenate(
        [jnp.concatenate([act[...] for act in acts[i * count:(i + 1) * count]], axis=1)
         for i in range(blocks)], axis=0
    )
    for i in range(per):
        at = aligned(ids[i * subs + step] * width, width)
        weight = jnp.concatenate([pieces[k * per + i][0] for k in range(weights)], axis=1)
        product = (dot_nt(rows, weight) + dot(extra, low_in[:, at])).astype(BF)
        for j, out in enumerate(outs):
            out[:, at] = product[j * size:(j + 1) * size]


def unfold(ids, acts, low, low_in, weights, size, blocks):
    subs = weights[0][0].shape[0]
    width = low_in.shape[1]
    pieces = [piece for weight in weights for piece in weight]
    count = len(blocks)
    chosen = []
    for at in blocks:
        for act in acts:
            if isinstance(act, tuple):
                per = act[0].shape[0] // size
                chosen.append((act[at // per], at % per))
            else:
                chosen.append((act, at))
    depth = sum(act.shape[1] for act, _ in chosen) // count
    return pl.pallas_call(
        partial(unfold_kernel, (count, len(acts), len(weights))),
        grid=(subs,),
        in_specs=[smem(), full(low_in.shape)]
        + [pl.BlockSpec((low.shape[0], size), lambda s, at=at: (0, at)) for at in blocks]
        + [pl.BlockSpec((size, act.shape[1]), lambda s, at=at: (at, 0)) for act, at in chosen]
        + [pl.BlockSpec((1,) + w.shape[1:], lambda s: (s, 0, 0)) for w in pieces],
        out_specs=[full((size, width))] * count,
        out_shape=[jax.ShapeDtypeStruct((size, width), BF)] * count,
        compiler_params=params(48),
        cost_estimate=estimate(
            2 * count * size * depth * width, 2 * depth * width + 4 * count * size * depth
        ),
        name="unfold",
    )(ids, low_in, *[low] * count, *in_hbm(*[act for act, _ in chosen], *pieces))


def gate_back_kernel(parts, ids, low_back, low_in, gate, nrm, inverse, hold, low_gate, low_out,
                     begin_in, begin_gate, *refs):
    act, pieces = refs[:parts], refs[parts:-6]
    dgate, dret, low, dlow, grad_in, grad_gate = refs[-6:]

    @pl.when(pl.program_id(0) == 0)
    def _():
        low[...] = low_rows(low_back[...], act).astype(BF)
        dlow[...] = jnp.zeros(dlow.shape, F32)

    weights = jnp.concatenate([w[s] for w in pieces for s in range(w.shape[0])], axis=1)
    back = dot_nt(columns(act, ids), weights) + dot_tn(low[...], low_in[...])
    level = gate[...].astype(F32)
    normed = nrm[...].astype(F32)
    chance = 1.0 / (1.0 + jnp.exp(-level))
    slope = chance * (1.0 + level * (1.0 - chance))
    back_gate = (back * normed * slope).astype(BF)
    grad = back * (level * chance)
    mean = jnp.mean(grad, axis=1, keepdims=True)
    along = jnp.mean(grad * normed, axis=1, keepdims=True)
    dgate[...] = back_gate
    dret[...] = (inverse[0, :, :1] * (grad - mean - normed * along)).astype(BF)
    grad_in[...] = begin_in[...] + dot(low[...], hold[...])
    grad_gate[...] = begin_gate[...] + dot(low_gate[...], back_gate)
    dlow[...] += dot_nt(low_out[...], back_gate)


def gate_back(ids, act, low_back, low_in, gate, nrm, inverse, hold, low_gate, low_out, pieces,
              half, begin_in, begin_gate):
    if len(act) > 1:
        act = act[len(act) // 2 * half:len(act) // 2 * (half + 1)]
    rows, depth = gate.shape[0] // 2, act[0].shape[1]
    width = gate.shape[1]
    block = VALUE_DIM
    ranks = low_back.shape[0]
    if len(act) == 1:
        acts = [pl.BlockSpec((rows, depth), lambda n: (half, 0))]
    else:
        acts = whole(act)
    column = lambda height: pl.BlockSpec((height, block), lambda n: (0, n))
    place = pl.BlockSpec((rows, block), lambda n: (half, n))
    return pl.pallas_call(
        partial(gate_back_kernel, len(act)),
        grid=(width // block,),
        in_specs=[smem(), full(low_back.shape), column(ranks), place, place,
                  pl.BlockSpec((1, rows, 128), lambda n: (n, half, 0)), place,
                  pl.BlockSpec((ranks, rows), lambda n: (low_gate.shape[0] // ranks - 1, half)),
                  column(low_out.shape[0]), column(ranks), column(ranks)]
        + acts + [pl.BlockSpec((w.shape[0], block, w.shape[2]), lambda n: (0, n, 0))
                  for w in pieces],
        out_specs=[column(rows), column(rows), full((ranks, rows)),
                   full((low_out.shape[0], rows)), column(ranks), column(ranks)],
        out_shape=[jax.ShapeDtypeStruct((rows, width), BF)] * 2
        + [jax.ShapeDtypeStruct((ranks, rows), BF),
           jax.ShapeDtypeStruct((low_out.shape[0], rows), F32),
           jax.ShapeDtypeStruct((ranks, width), F32), jax.ShapeDtypeStruct((ranks, width), F32)],
        compiler_params=params(56),
        cost_estimate=estimate(2 * rows * depth * width, 2 * depth * width + 16 * rows * width),
        name="gate_back",
    )(ids, low_back, low_in, *in_hbm(gate, nrm, inverse, hold), low_gate, low_out, begin_in,
      begin_gate, *act, *pieces)


def retention_back_kernel(spots, rates, seg_col, seg_row, cosine, sine_table, low, begin, q_out,
                          k_out, v_out, q, k, v, dret0, dret1, dq, dk, dv, dlow, grad_q, grad_k,
                          grad_v, sums):
    head = pl.program_id(0)
    rate = rates[head]
    count = spots.shape[0]
    size = q.shape[0] // count
    down, across = decay_factors(rate, size)
    column_factor = jnp.exp(rate * across)
    key_scale = 1.0 / KEY_DIM**0.5

    @pl.when(head == 0)
    def _():
        dlow[...] = begin[...]

    sums[...] = jnp.zeros(sums.shape, F32)
    for j in range(count):
        there = aligned(spots[j] * size, size)
        place = slice(j * size, (j + 1) * size)
        key, value = k[there, :], v[there, :]
        seg_there = seg_col[place, :]
        key_sum = jnp.zeros((size, KEY_DIM), F32)
        value_sum = jnp.zeros((size, VALUE_DIM), F32)
        for i in range(j, count):
            here = aligned(spots[i] * size, size)
            query = q[here, :]
            within = aligned(spots[i] % (count // 2) * size, size)
            back = jnp.where(spots[i] < count // 2, dret0[within, :], dret1[within, :])
            row_factor = jnp.exp(rate * ((i - j) * size - down))
            alive = seg_there == seg_row[:, i * size:(i + 1) * size]
            if i == j:
                alive = alive & (across >= down)
            weight = jnp.where(alive, row_factor * column_factor, 0.0)
            mixed = (dot_nt(key, query) * weight).astype(BF)
            grad = (dot_nt(value, back) * weight).astype(BF)
            value_sum = value_sum + dot(mixed, back)
            key_sum = key_sum + dot(grad, query)
            sums[i * size:(i + 1) * size, :] += dot_tn(grad, key)
        dk[there, :] = (
            key_scale * unrotated(key_sum, cosine[place, :], sine_table[place, :])
        ).astype(BF)
        dv[there, :] = value_sum.astype(BF)
    for i in range(count):
        place = slice(i * size, (i + 1) * size)
        dq[aligned(spots[i] * size, size), :] = unrotated(
            sums[place, :], cosine[place, :], sine_table[place, :]
        ).astype(BF)
    back_q, back_k, back_v = dq[...], dk[...], dv[...]
    dlow[...] += (
        dot_nt(q_out[...], back_q) + dot_nt(k_out[...], back_k) + dot_nt(v_out[...], back_v)
    )
    grad_q[...] = dot(low[:RANK, :], back_q).astype(BF)
    grad_k[...] = dot(low[RANK:2 * RANK, :], back_k).astype(BF)
    grad_v[...] = dot(low[2 * RANK:3 * RANK, :], back_v).astype(BF)


def retention_back(spots, rates, seg_col, seg_row, cosine, sine_table, low, begin, qk_out, v_out,
                   qk, v, dret0, dret1):
    rows = qk.shape[0]
    heads = v.shape[1] // VALUE_DIM
    ranks = low.shape[0]
    key = lambda height: pl.BlockSpec((height, KEY_DIM), lambda h: (0, h))
    later = lambda height: pl.BlockSpec((height, KEY_DIM), lambda h: (0, h + heads))
    value = lambda height: pl.BlockSpec((height, VALUE_DIM), lambda h: (0, h))
    keys = heads * KEY_DIM
    return pl.pallas_call(
        retention_back_kernel,
        grid=(heads,),
        in_specs=[smem(), smem(), full(seg_col.shape), full(seg_row.shape), full(cosine.shape),
                  full(cosine.shape), full(low.shape), full(begin.shape), key(ranks),
                  later(ranks), value(ranks),
                  key(rows), later(rows), value(rows), value(rows // 2), value(rows // 2)],
        out_specs=[key(rows), key(rows), value(rows), full((ranks, rows)), key(RANK), key(RANK),
                   value(RANK)],
        out_shape=[jax.ShapeDtypeStruct((rows, keys), BF), jax.ShapeDtypeStruct((rows, keys), BF),
                   jax.ShapeDtypeStruct(v.shape, BF), jax.ShapeDtypeStruct((ranks, rows), F32),
                   jax.ShapeDtypeStruct((RANK, keys), BF), jax.ShapeDtypeStruct((RANK, keys), BF),
                   jax.ShapeDtypeStruct((RANK, v.shape[1]), BF)],
        scratch_shapes=[pltpu.VMEM((rows, KEY_DIM), F32)],
        compiler_params=params(48),
        cost_estimate=estimate(2 * rows * rows * 1792 * heads, 30 << 20),
        name="retention_back",
    )(spots, rates, seg_col, seg_row,
      cosine, sine_table, low, begin, qk_out, qk_out, v_out, qk, qk, v, dret0, dret1)


def share_kernel(heights, low, *refs):
    out = refs[-1]
    at, first = 0, 0
    for height, parts in heights:
        total = jnp.zeros((height, out.shape[2]), F32)
        begin = 0
        for ref in refs[first:first + parts]:
            end = begin + ref.shape[0]
            total = total + dot(low[at:at + height, begin:end], ref[...])
            begin = end
        out[0, at:at + height, :] = total.astype(BF)
        at, first = at + height, first + parts


def share(low, span, items):
    acts = [array for _, act in items for array in act]
    heights = tuple((height, len(act)) for height, act in items)
    count = acts[0].shape[1] // span
    made = pl.pallas_call(
        partial(share_kernel, heights),
        grid=(count,),
        in_specs=[full(low.shape)]
        + [pl.BlockSpec((act.shape[0], span), lambda i: (0, i)) for act in acts],
        out_specs=pl.BlockSpec((1, low.shape[0], span), lambda i: (i, 0, 0)),
        out_shape=jax.ShapeDtypeStruct((count, low.shape[0], span), BF),
        compiler_params=params(32),
        cost_estimate=estimate(0, 0),
        name="share",
    )(low, *in_hbm(*acts))
    return made.reshape(count * low.shape[0], span)


def place_kernel(layout, arrays, order, *refs):
    packs, outs = refs[:arrays], refs[arrays:]
    pack = packs[0][0]
    if arrays == 2:
        which = order[pl.program_id(0)] >= order[pl.num_programs(0)]
        pack = jnp.where(which, packs[1][0], pack)
    span = pack.shape[1]
    for (begin, height, kind, stride), out in zip(layout, outs):
        if kind == "shares":
            for j in range(out.shape[2] // span):
                rows = pack[begin + stride * j:begin + stride * j + height]
                out[0, :, j * span:(j + 1) * span] = rows.astype(F32)
            continue
        for j in range(2):
            rows = pack[begin + stride * j:begin + stride * j + height].astype(F32)
            if kind == "halves":
                out[0, :, j * span:(j + 1) * span] = rows
            else:
                out[0, j] = rows


def place(order, arrays, layout, shares):
    entries = order.shape[0]
    size, _, span = arrays[0].shape
    shapes = []
    for _, height, kind, _ in layout:
        shapes.append({"shares": (height, shares * span),
                       "halves": (height, 2 * span)}.get(kind, (2, height, span)))

    def spec(number):
        def index(e, o):
            return (jnp.clip(o[e] - number * size, 0, size - 1), 0, 0)
        return pl.BlockSpec((1,) + arrays[0].shape[1:], index)

    order = jnp.concatenate([order, jnp.full((1,), size, jnp.int32)])
    return pl.pallas_call(
        partial(place_kernel, layout, len(arrays)),
        grid_spec=pltpu.PrefetchScalarGridSpec(
            num_scalar_prefetch=1,
            grid=(entries,),
            in_specs=[spec(number) for number in range(len(arrays))],
            out_specs=[
                pl.BlockSpec((1,) + shape, lambda e, o, n=len(shape): (e,) + (0,) * n)
                for shape in shapes
            ],
        ),
        out_shape=[jax.ShapeDtypeStruct((entries,) + shape, F32) for shape in shapes],
        compiler_params=params(32),
        cost_estimate=estimate(0, 10 << 20),
        name="place",
    )(order, *in_hbm(*arrays))


def after(x, *others):
    return lax.optimization_barrier((x,) + others)[0]


class PlainLinks:
    def __init__(self, ndp, nt):
        self.ndp, self.nt = ndp, nt
        self.rank = lax.axis_index("tensor")
        self.chunks = jnp.arange(nt, dtype=jnp.int32)
        self.spots = self.chunks
        self.row_ids = jnp.zeros((1,), jnp.int32)

    def exchange(self, x):
        return x

    def mine(self, own, other):
        return own

    def gather(self, x):
        return [lax.all_gather(x, "tensor", axis=0, tiled=True)]

    def scatter(self, rows):
        total = lax.psum_scatter(
            jnp.concatenate(rows, axis=0), "tensor", scatter_dimension=0, tiled=True
        )
        zero = jnp.zeros_like(total)
        return (total, zero, zero)

    def forward(self, shards, tokens, cotangent, line, steps):
        steps.rotation()
        blocks = [
            [lax.all_gather(shard, "dp", axis=int(shard.shape[1] * self.ndp == tokens.shape[1]),
                            tiled=True)[None]]
            for shard in shards
        ]
        steps.ready(line, steps.tables(line, line)[0])
        a = self.gather(steps.norm(tokens))
        dy = self.gather(cotangent)
        projected = steps.project(a, blocks[1], blocks[0])
        mixed = steps.mix(a, *projected, blocks[2])
        *rows, low = steps.fold(mixed[0], blocks[3])
        middle, b = steps.join(tokens, self.scatter(rows))
        b = self.gather(b)
        begun = steps.mlp_begin(b, blocks[5], blocks[6])
        dhid = (*steps.hidden_grad(dy, blocks[4]), begun, ([], []))
        return blocks, tokens, a, cotangent, dy, projected, mixed, low, middle, b, dhid

    def group_sum(self, x):
        return lax.psum(x.astype(BF), "tensor")

    def backward(self, steps):
        steps.mlp()
        dz = self.gather(steps.dz(self.scatter(steps.unfold_mlp(256, (0, 1, 2, 3)))))
        output = steps.output(self.scatter(steps.fold_down(steps.hid)))
        lows = self.group_sum(steps.early_lows())
        early = lax.all_gather(steps.early(lows), "dp")
        early = steps.place_early([early], jnp.arange(self.ndp, dtype=jnp.int32))
        steps.gate_back(dz, 0)
        steps.gate_back(dz, 1)
        steps.retention_back(*steps.dret)
        late = jnp.concatenate(
            [steps.late_shares(self.group_sum(steps.dlow)), steps.late_rest(lows, dz)]
        )
        late = lax.all_gather(late, "dp")
        late = steps.place_late([late], jnp.arange(self.ndp, dtype=jnp.int32))
        parts = self.scatter(steps.unfold_attn(256, (0, 1, 2, 3)))
        dx, _ = steps.dx(parts)
        return output, dx, early, late


class PairedLinks:
    def __init__(self, ndp, nt):
        self.ndp, self.nt = ndp, nt
        d, t = lax.axis_index("dp"), lax.axis_index("tensor")
        c, p, m = d % 2, t // 2, t % 2
        self.home = c == p
        self.rank = 2 * c + m
        flips = jnp.array([0, 2, 1, 3], jnp.int32)
        self.chunks = self.rank ^ flips
        order = jnp.arange(4, dtype=jnp.int32) ^ self.rank
        self.spots = (order % 2) * 2 + order // 2
        g = d // 2
        self.row_ids = ((2 * (g ^ jnp.arange(4, dtype=jnp.int32))[:, None]
                         + jnp.arange(2, dtype=jnp.int32)[None, :]) ^ c).reshape(-1)
        self.last = {}
        self.last_round = ()
        self.slow = ()

    def pairs(self, place):
        listed = []
        for d in range(self.ndp):
            for t in range(self.nt):
                to = place(d, t)
                if to is not None:
                    listed.append((d * self.nt + t, to[0] * self.nt + to[1]))
        return listed

    def move(self, x, place, chain=None):
        if chain in self.last:
            x = after(x, *self.last[chain])
        moved = lax.ppermute(x, ("dp", "tensor"), self.pairs(place))
        if chain is not None:
            self.last[chain] = (moved,)
        return moved

    def send(self, moves):
        return [lax.ppermute(x, ("dp", "tensor"), self.pairs(place)) for x, place in moves]

    def round(self, moves, work=None, inputs=(), later=(), slow=(), feed=0):
        every = list(moves) + list(slow)
        values = [x for x, _ in every]
        flat, form = jax.tree.flatten((values, inputs))
        last, _ = jax.tree.flatten(self.last_round)
        if last:
            flat = lax.optimization_barrier((*flat, *last))[:len(flat)]
        values, inputs = jax.tree.unflatten(form, flat)
        moved = self.send([(x, place) for x, (_, place) in zip(values, every)])
        moved, slowly = moved[:len(moves)], moved[len(moves):]
        second = []
        if later:
            count, make = later
            moves = make(moved[:count])
            values = [x for x, _ in moves]
            values = lax.optimization_barrier((*values, *moved[:count]))[:len(values)]
            second = self.send([(x, place) for x, (_, place) in zip(values, moves)])
        made = work(*moved[:feed], *inputs) if work is not None else ()
        self.last_round = (moved, second, made, self.slow)
        self.slow = slowly
        return moved + slowly, second, made

    def core(self, x):
        return self.move(x, lambda d, t: (d ^ 1, t))

    def pair(self, x):
        return self.move(x, lambda d, t: (d, t ^ 1), "pair")

    def mine(self, own, other):
        return jnp.where(self.home, own, other)

    def exchange(self, x):
        moved = self.move(
            x, lambda d, t: (d ^ 1, t ^ 2) if d % 2 != t // 2 else None, "middle"
        )
        return jnp.where(self.home, x, moved)

    def gather(self, x):
        across = self.pair(x)
        return [x, self.core(x), across, self.core(across)]

    def forward(self, shards, tokens, cotangent, line, steps):
        by_one = lambda d, t: (d ^ 2, t)
        by_two = lambda d, t: (d ^ 4, t)
        core = lambda d, t: (d ^ 1, t)
        pair = lambda d, t: (d, t ^ 1)
        swap = lambda d, t: (d ^ 1, t ^ 2) if d % 2 != t // 2 else None
        seat = lambda d, t: (d, t ^ 2) if d % 2 == t // 2 else None
        blocks = [[None] * 4 for _ in shards]
        doubled = [jnp.stack([shards[0], self.core(shards[0])])]

        def over(i):
            return (doubled[i], seat)

        def arrived(i, moved):
            blocks[i][0] = self.mine(doubled[i], moved)

        hops = {
            "x": lambda i: (blocks[i][0], by_one),
            "y": lambda i: (blocks[i][0], by_two),
            "xy": lambda i: (blocks[i][1], by_two),
            "yx": lambda i: (blocks[i][2], by_one),
        }
        place_of = {"x": 1, "y": 2, "xy": 3, "yx": 3}

        def go(first, second, others, work=None, inputs=()):
            def later(moved):
                for (i, way), block in zip(first, moved):
                    blocks[i][place_of[way]] = block
                return [hops[way](i) for i, way in second]

            moved, seconds, made = self.round(
                [hops[way](i) for i, way in first] + list(others), work, inputs,
                (len(first), later)
            )
            for (i, way), block in zip(second, seconds):
                blocks[i][place_of[way]] = block
            return moved[len(first):], made

        def double(rest):
            return [jnp.stack([shard, self.core(shard)]) for shard in rest]

        other = self.core(line)
        def begin(rest):
            return double(rest), steps.rotation()

        (moved,), (made, turn) = go([], [], [over(0)], begin, (shards[1:],))
        steps.turn = turn
        doubled += made
        arrived(0, moved)
        (moved,), (home_table, sent_table) = go(
            [(0, "x"), (0, "y")], [], [over(1)], steps.tables, (line, other)
        )
        arrived(1, moved)
        (x, table, moved), _ = go([(1, "x"), (0, "xy")], [(1, "y")],
                                  [(tokens, swap), (sent_table, seat), over(2)])
        arrived(2, moved)
        x = self.mine(tokens, x)
        steps.ready(other, self.mine(home_table, table))
        a = steps.norm(x)
        (across, moved, grad), _ = go([(2, "x"), (2, "y")], [(1, "yx"), (2, "xy")],
                                      [(a, pair), over(3), (cotangent, swap)])
        arrived(3, moved)
        grad = self.mine(cotangent, grad)
        def attend(near, beyond, own, across, *weights):
            a = [own, near, across, beyond]
            return a, steps.project(a, *weights[::-1])

        moves = [(a, core), (across, core), hops["x"](3), hops["y"](3), over(4)]
        moved, _, (a, projected) = self.round(
            moves, attend, (a, across, *blocks[:2]), feed=2
        )
        _, _, blocks[3][1], blocks[3][2], moved = moved
        arrived(4, moved)
        half = grad.shape[0] // 2
        (moved, across0), mixed = go(
            [(4, "x"), (3, "xy")], [], [over(5), (grad[:half], pair)], steps.mix,
            (a, *projected, blocks[2])
        )
        arrived(5, moved)
        (moved, across1), folded = go(
            [(5, "x"), (4, "y")], [], [over(6), (grad[half:], pair)], steps.fold,
            (mixed[0], blocks[3])
        )
        across = jnp.concatenate([across0, across1])
        arrived(6, moved)
        own, near, far, beyond, low = folded
        moves = [(near, core), (beyond, core), hops["yx"](4), hops["y"](5)]
        moved, (far,), _ = self.round(
            moves, later=(2, lambda moved: [(self.add(far, moved[1]), pair)])
        )
        near, _, blocks[4][3], blocks[5][2] = moved
        middle, b = steps.join(x, (own, near, far))
        (far, near_grad, beyond_grad), _ = go([(6, "x"), (6, "y")], [],
                                              [(b, pair), (grad, core), (across, core)])
        dy = [grad, near_grad, across, beyond_grad]

        def beside(near, beyond, own, across, dy, w_d, *weights):
            rows = [own, near, across, beyond]
            return steps.hidden_grad(dy, w_d), rows, steps.mlp_begin(rows, *weights)

        moves = [(b, core), (far, core), hops["yx"](5), hops["xy"](6)]
        moved, _, (dhid, b, begun) = self.round(
            moves, beside, (b, far, dy, blocks[4], blocks[5][:3], blocks[6][:3]), feed=2
        )
        blocks[5][3], blocks[6][3] = moved[2:]
        dhid = (*dhid, begun, (blocks[5][3:], blocks[6][3:]))
        return blocks, x, a, grad, dy, projected, mixed, low, middle, b, dhid

    def add(self, one, two):
        return (one.astype(F32) + two.astype(F32)).astype(BF)

    def core_sum(self, x, other):
        size = x.shape[1] // 4
        other = other.astype(F32)
        return (x + jnp.concatenate(
            [other[:, i * size:(i + 1) * size] for i in (1, 0, 3, 2)], axis=1
        )).astype(BF)

    def pair_sum(self, x, other):
        size = x.shape[1] // 2
        other = jnp.concatenate([other[:, size:], other[:, :size]], axis=1)
        return (x.astype(F32) + other.astype(F32)).astype(BF)

    def both_halves(self, halves, one, two):
        return jnp.concatenate(
            [jnp.concatenate([halves[0], one]),
             jnp.concatenate([halves[1][:1], two[:1], halves[1][1:], two[1:]])], axis=1
        )

    def backward(self, steps):
        pair = lambda d, t: (d, t ^ 1)
        swap = lambda d, t: (d ^ 1, t ^ 2) if d % 2 != t // 2 else None
        by_one = lambda d, t: (d ^ 2, t)
        by_two = lambda d, t: (d ^ 4, t)
        core = lambda d, t: (d ^ 1, t)

        self.last_round = ()
        steps.mlp()
        (lows,), _, (near, far, beyond) = self.round(
            [(steps.early_lows().astype(BF), core)],
            lambda dup: steps.unfold_mlp(256, (1, 2, 3), dup), (steps.dup,)
        )
        lows = self.core_sum(steps.early_lows(), lows)
        (beyond, near, other), _, _ = self.round([(beyond, core), (near, core), (lows, pair)])
        far = self.add(far, beyond)
        half = far.shape[0] // 2
        lows = self.pair_sum(lows, other)
        (far,), _, ((own,), folded, early) = self.round(
            [(far, pair)],
            lambda dup, hid, lows: (steps.unfold_mlp(256, (0,), dup), steps.fold_down(hid),
                                    steps.early(lows)),
            (steps.dup, steps.hid, lows)
        )
        own_out, near_out, far_out, beyond_out = folded
        dz = steps.dz((own, near, far))


        def beside(beyond, dz_near, far, dz):
            return self.add(far, beyond), steps.gate_back([dz, dz_near, dz, dz], 0)

        (_, dz_near, across, near_out), _, (far_out, dret0) = self.round(
            [(beyond_out, core), (dz, core), (dz, pair), (near_out, core)],
            beside, (far_out, dz), feed=2
        )
        (dz_beyond,), _, _ = self.round([(across, core)])
        (moved, far_out), _, dret1 = self.round(
            [(early, swap)],
            lambda across, beyond: steps.gate_back([across, across, across, beyond], 1),
            (across, dz_beyond), slow=[(far_out, pair)]
        )
        early = self.mine(early, moved)
        size = early.shape[0] // 2
        early = [early[:size][None], early[size:][None]]
        (one, two), _, dpv = self.round(
            [(early[0], by_one), (early[1], by_two)], steps.retention_back, (dret0, dret1)
        )
        early = [jnp.concatenate([early[0], one]), jnp.concatenate([early[1], two])]
        dz = [dz, dz_near, across, dz_beyond]

        (dlow,), _, output = self.round(
            [(steps.dlow.astype(BF), core)], lambda *parts: steps.output(parts),
            (own_out, near_out, far_out)
        )
        dlow = self.core_sum(steps.dlow, dlow)
        (other, moved_out, one, two), _, ((own, near, far, beyond), rest) = self.round(
            [(dlow, pair), (output, swap), (early[0], by_two), (early[1], by_one)],
            lambda dpv, lows: (steps.unfold_attn(256, (0, 1, 2, 3), dpv),
                               steps.late_rest(lows, dz)),
            (dpv, lows)
        )
        (beyond, near, moved), _, shares = self.round(
            [(beyond, core), (near, core), (rest, swap)],
            lambda dlow, other: steps.late_shares(self.pair_sum(dlow, other)), (dlow, other)
        )
        rest = self.mine(rest, moved)
        (moved,), _, (far, early) = self.round(
            [(shares, swap)],
            lambda far, beyond, *early: (self.add(far, beyond), self.both_halves(*early)),
            (far, beyond, early, one, two)
        )
        late = [self.mine(shares, moved)[None], rest[None]]
        (one, two, far0), _, _ = self.round(
            [(late[0], by_one), (late[1], by_two), (far[:half], pair)]
        )
        late = [jnp.concatenate([late[0], one]), jnp.concatenate([late[1], two])]
        (one, two, far1), _, _ = self.round(
            [(late[0], by_two), (late[1], by_one), (far[half:], pair)]
        )
        dx, low = steps.dx((own, near, jnp.concatenate([far0, far1])))
        late = self.both_halves(late, one, two)
        apart = jnp.arange(self.ndp, dtype=jnp.int32) ^ lax.axis_index("dp")

        def put(early_other, other, early, late):
            at = apart // 2 + 4 * (apart % 2)
            early = steps.place_early([early, early_other], at)
            return early, steps.place_late([late, other], at)

        (_, _, moved), _, (early, late) = self.round(
            [(early, core), (late, core), (low, swap)], put, (early, late), feed=2
        )
        moved, early, late = lax.optimization_barrier((moved, early, late))
        return (self.mine(output, moved_out),
                self.mine(dx, moved.astype(F32)), early, late)


def rotation_tables(seq_length, half_dim):
    positions = jnp.arange(seq_length, dtype=jnp.float32)
    frequency = jnp.exp(-jnp.log(10000.0) * jnp.arange(half_dim, dtype=jnp.float32) / half_dim)
    angles = positions[:, None] * frequency[None, :]
    return (jnp.cos(angles), jnp.sin(angles))


def shards(
    ndp,
    nt,
    tokens,
    cotangent,
    adapter_ids,
    segments,
    norm_attn,
    norm_mlp,
    weight_query,
    weight_key,
    weight_value,
    weight_gate,
    weight_out,
    weight_mlp_gate,
    weight_mlp_up,
    weight_mlp_down,
    adapt_attn_in,
    adapt_query_key,
    adapt_value_gate,
    adapt_out_in,
    adapt_out_back,
    adapt_mlp_in,
    adapt_mlp_hidden,
    adapt_down_in,
    adapt_down_back,
):
    links = PairedLinks(ndp, nt) if (ndp, nt) == (8, 4) else PlainLinks(ndp, nt)
    rank, chunks, spots, ids = links.rank, links.chunks, links.spots, links.row_ids
    adapters = adapt_attn_in.shape[0]
    depth = tokens.shape[2]
    seq_length = segments.shape[1]
    gain_attn, gain_mlp = norm_attn[None], norm_mlp[None]

    def pick(table, which):
        return lax.dynamic_index_in_dim(table, which, 0, keepdims=False)

    def packed(which):
        qk, vg = pick(adapt_query_key, which), pick(adapt_value_gate, which)
        return jnp.concatenate(
            [jnp.concatenate([qk[0], qk[1]], axis=1), vg[0], vg[1],
             pick(adapt_mlp_hidden, which).reshape(2 * RANK, -1),
             pick(adapt_out_in, which).T, pick(adapt_down_in, which).T], axis=0
        )

    own_id = adapter_ids[0, 0]
    own_line = jnp.concatenate([segments, jnp.broadcast_to(adapter_ids, (1, 128))], axis=1)
    wide = weight_gate.shape[1]
    keys = adapt_query_key.shape[3]
    heads_local = wide // VALUE_DIM
    head_ids = (rank * heads_local + jnp.arange(heads_local, dtype=jnp.int32)).astype(F32)
    rates = jnp.log(1.0 - jnp.exp2(-5.0 - head_ids))
    class Steps:
        def tables(self, line, other):
            return packed(line[0, seq_length]), packed(other[0, seq_length])

        def ready(self, other, table):
            line = links.mine(own_line, other)
            self.work_id = work_id = line[0, seq_length]
            self.seg_row = line[:, :seq_length]
            self.seg_col = self.seg_row.reshape(seq_length, 1)
            blank = jnp.zeros((RANK, wide), BF)
            left = jnp.arange(wide)[None, :] < keys
            zero = jnp.zeros((), BF)
            self.qk_out = jnp.concatenate([jnp.where(left, table[:RANK], zero),
                                           jnp.where(left, zero, table[:RANK]), blank, blank])
            self.v_out = jnp.concatenate([blank, blank, table[RANK:2 * RANK], blank])
            self.g_out = jnp.concatenate([blank, blank, blank, table[2 * RANK:3 * RANK]])
            self.mg_out = jnp.concatenate([table[3 * RANK:4 * RANK], blank])
            self.mu_out = jnp.concatenate([blank, table[4 * RANK:5 * RANK]])
            self.out_in = table[5 * RANK:6 * RANK]
            self.down_in = table[6 * RANK:7 * RANK]
            self.attn_in = pick(adapt_attn_in, work_id).T
            self.out_back = pick(adapt_out_back, work_id)
            self.mlp_in = pick(adapt_mlp_in, work_id).T
            self.down_back = pick(adapt_down_back, work_id)

        def rotation(self):
            self.turn = rotation_tables(seq_length, HALF)
            return self.turn

        def norm(self, x):
            return norm_rows(x, gain_attn)

        def project(self, a, w_qk, w_v):
            return project(
                ids, chunks, a, self.attn_in, jnp.concatenate([self.qk_out, self.v_out], axis=1),
                (w_qk, w_v), self.turn
            )

        def mix(self, a, qk, v, low, w_g):
            gate, = project(ids, chunks, a, low, self.g_out, (w_g,), ())
            return (*retention(spots, rates, self.seg_col, self.seg_row, qk, v, gate), gate)

        def fold(self, o, w_o):
            return fold(ids, o, self.out_in, self.out_back, w_o)

        def join(self, x, parts):
            return join_rows(x, parts, gain_mlp)

        def mlp_begin(self, b, w_mg, w_mu):
            return mlp_begin(ids, b, self.mlp_in, w_mg, w_mu)

        def hidden_grad(self, dy, w_d):
            return hidden_grad(ids, dy, self.down_back, self.down_in, w_d)

    steps = Steps()
    ((w_v, w_qk, w_g, w_o, w_d, w_mg, w_mu), x, a, grad, dy, (qk, v, low_a),
     (o, nrm, inverse, gate), low_o, middle, b, (dhid, low_dy, begun, late_weights)) = links.forward(
        [weight_value, jnp.concatenate([weight_query, weight_key], axis=1), weight_gate,
         weight_out, weight_mlp_down, weight_mlp_gate, weight_mlp_up],
        tokens[0], cotangent[0], own_line, steps,
    )
    seg_row, seg_col, work_id = steps.seg_row, steps.seg_col, steps.work_id
    qk_out, v_out, g_out, mg_out, mu_out = (
        steps.qk_out, steps.v_out, steps.g_out, steps.mg_out, steps.mu_out
    )
    attn_in, out_in, out_back = steps.attn_in, steps.out_in, steps.out_back
    mlp_in, down_in, down_back = steps.mlp_in, steps.down_in, steps.down_back

    span = depth // nt
    halves = lambda y: jnp.concatenate([y[:, :wide // 2], y[:, wide // 2:]])

    class Back:
        early_height = 3 * RANK

        def mlp(self):
            (self.hid, self.dgate, self.dup, self.lows, self.grad_hidden,
             self.grad_down) = mlp(
                ids, begun, b, mg_out, mu_out, down_in, dhid, low_dy, *late_weights
            )

        def unfold_mlp(self, size, blocks, dup=None):
            dup = self.dup if dup is None else dup
            return unfold(ids, (self.dgate, dup), self.lows[RANK:], mlp_in, (w_mg, w_mu),
                          size, blocks)

        def dz(self, parts):
            self.dmid, = rms_back(middle, grad, parts, gain_mlp, (BF,))
            return self.dmid

        def fold_down(self, hid):
            return fold(ids, hid, down_in, down_back, w_d)[:4]

        def output(self, parts):
            return (middle.astype(F32) + (
                parts[0].astype(F32) + parts[1].astype(F32) + parts[2].astype(F32)
            )).astype(BF)

        def early_lows(self):
            return jnp.concatenate([self.lows, low_o])

        def early(self, lows):
            mark = jnp.full((RANK, span), work_id, F32).astype(BF)
            return jnp.concatenate(
                [share(lows[:3 * RANK], span, ((RANK, dy), (2 * RANK, b))),
                 halves(jnp.concatenate([self.grad_hidden, self.grad_down])), mark]
            )

        def gate_back(self, dz, half):
            if half == 0:
                self.grad_out_in = self.grad_gate = jnp.zeros((RANK, wide), F32)
                self.dpg, self.dret, self.low_parts = (), (), ()
            dpg, dret, _, dlow, self.grad_out_in, self.grad_gate = gate_back(
                ids, dz, out_back, out_in, gate, nrm, inverse, o, low_a, g_out, w_o, half,
                self.grad_out_in, self.grad_gate
            )
            self.dpg, self.dret = self.dpg + (dpg,), self.dret + (dret,)
            self.low_parts = self.low_parts + (dlow,)
            return dret

        def retention_back(self, *dret):
            (self.dpq, self.dpk, self.dpv, self.dlow, self.grad_q, self.grad_k,
             self.grad_v) = retention_back(
                spots, rates, seg_col, seg_row, *steps.turn, low_a,
                jnp.concatenate(self.low_parts, axis=1), qk_out, v_out, qk, v, *dret
            )
            return self.dpv

        def late_shares(self, lows):
            return share(lows, span, ((4 * RANK, a),))

        def late_rest(self, lows, dz):
            return jnp.concatenate(
                [share(lows[3 * RANK:], span, ((RANK, dz),)),
                 halves(jnp.concatenate(
                     [jnp.concatenate([self.grad_q, self.grad_k], axis=1), self.grad_v,
                      self.grad_gate.astype(BF), self.grad_out_in.astype(BF)]
                 ))]
            )

        def unfold_attn(self, size, blocks, dpv=None):
            dpv = self.dpv if dpv is None else dpv
            return unfold(ids, (self.dpq, self.dpk, dpv, self.dpg), self.dlow, attn_in,
                          (w_qk, w_v, w_g), size, blocks)

        def dx(self, parts):
            return rms_back(x, self.dmid, parts, gain_attn, (F32, BF))

        def place_early(self, arrays, at):
            sequences = sum(array.shape[0] for array in arrays)
            shares = nt * self.early_height
            marks = [array[:, shares + 6 * RANK, 0] for array in arrays]
            all_ids = jnp.concatenate(marks).astype(jnp.int32)[at]
            numbers = jnp.arange(adapters, dtype=jnp.int32)
            chosen = numbers[:, None] == all_ids[None, :]
            if sequences == adapters:
                self.order = jnp.sum(jnp.where(chosen, numbers[None, :], 0), axis=1)
                self.total = None
            else:
                self.order = numbers
                self.total = lambda y: jnp.einsum(
                    "es,sij->eij", chosen.astype(BF), y, preferred_element_type=F32
                )
                arrays, at = [self.total(arrays[0])], numbers
            pitch = self.early_height
            return place(
                at[self.order], arrays,
                ((0, RANK, "shares", pitch), (RANK, 2 * RANK, "shares", pitch),
                 (shares, 2 * RANK, "halves", 3 * RANK),
                 (shares + 2 * RANK, RANK, "halves", 3 * RANK)), nt
            )

        def place_late(self, arrays, at):
            if self.total is not None:
                arrays, at = [self.total(arrays[0])], self.order
            pitch = 4 * RANK
            first, rest = nt * pitch, nt * (pitch + RANK)
            return place(
                at[self.order], arrays,
                ((0, pitch, "shares", pitch), (first, RANK, "shares", RANK),
                 (rest, RANK, "two", 4 * RANK), (rest + RANK, 2 * RANK, "halves", 4 * RANK),
                 (rest + 3 * RANK, RANK, "halves", 4 * RANK)), nt
            )

    output, input_grad, early, late = links.backward(Back())
    down_back_out, mlp_out, hidden_out, down_out = early
    attn_out, out_back_out, qk_grads, vg_grads, out_out = late
    return (
        output[None],
        input_grad[None],
        jnp.swapaxes(attn_out, 1, 2),
        qk_grads,
        vg_grads.reshape(adapters, 2, RANK, wide),
        jnp.swapaxes(out_out, 1, 2),
        out_back_out,
        jnp.swapaxes(mlp_out, 1, 2),
        hidden_out.reshape(adapters, 2, RANK, wide),
        jnp.swapaxes(down_out, 1, 2),
        down_back_out,
    )


def solution(mesh):
    in_specs = (
        P("dp", "tensor", None),
        P("dp", "tensor", None),
        P("dp", None),
        P("dp", None),
        P(),
        P(),
        P("dp", "tensor"),
        P("dp", "tensor"),
        P("dp", "tensor"),
        P("dp", "tensor"),
        P("tensor", "dp"),
        P("dp", "tensor"),
        P("dp", "tensor"),
        P("tensor", "dp"),
        P(),
        P(None, None, None, "tensor"),
        P(None, None, None, "tensor"),
        P(None, "tensor", None),
        P(),
        P(),
        P(None, None, None, "tensor"),
        P(None, "tensor", None),
        P(),
    )
    out_specs = (
        P("dp", "tensor", None),
        P("dp", "tensor", None),
        P(),
        P(None, None, None, "tensor"),
        P(None, None, None, "tensor"),
        P(None, "tensor", None),
        P(),
        P(),
        P(None, None, None, "tensor"),
        P(None, "tensor", None),
        P(),
    )
    local = partial(shards, mesh.shape["dp"], mesh.shape["tensor"])
    return jax.shard_map(local, mesh=mesh, in_specs=in_specs, out_specs=out_specs, check_vma=False)
```

```python
from functools import partial

import jax
import jax.numpy as jnp
from jax import lax
from jax.experimental import pallas as pl
from jax.experimental.pallas import tpu as pltpu
from jax.sharding import PartitionSpec as P

KEY_DIM = 256
VALUE_DIM = 512
RANK = 16
HALF = KEY_DIM // 2

rms_epsilon = 1e-06
group_floor = 1.0
BF = jnp.bfloat16
F32 = jnp.float32


def dot(a, b):
    return jnp.dot(a, b, preferred_element_type=F32)


def dot_nt(a, b):
    return lax.dot_general(a, b, (((1,), (1,)), ((), ())), preferred_element_type=F32)


def dot_tn(a, b):
    return lax.dot_general(a, b, (((0,), (0,)), ((), ())), preferred_element_type=F32)


def aligned(start, size):
    return pl.ds(pl.multiple_of(start, size), size)


def params(mib):
    return pltpu.CompilerParams(
        vmem_limit_bytes=mib << 20, dimension_semantics=("arbitrary",)
    )


def estimate(flops, moved):
    return pl.CostEstimate(flops=1, bytes_accessed=1, transcendentals=0)


def full(shape):
    return pl.BlockSpec(shape, lambda *_: (0,) * len(shape))


def in_hbm(*arrays):
    return [pltpu.with_memory_space_constraint(array, pltpu.HBM) for array in arrays]


def far(shape, kind):
    return pltpu.HBM(shape, kind)


def smem():
    return pl.BlockSpec(memory_space=pltpu.SMEM)


def columns(refs, ids, begin=0, end=None):
    count = ids.shape[0]
    width = refs[0].shape[1] // count
    if count == 1:
        return all_rows(refs)
    chosen = range(begin, count if end is None else end)
    return jnp.concatenate(
        [
            jnp.concatenate([ref[:, aligned(ids[i] * width, width)] for i in chosen], axis=1)
            for ref in refs
        ],
        axis=0,
    )


def all_rows(refs):
    return refs[0][...] if len(refs) == 1 else jnp.concatenate([ref[...] for ref in refs], axis=0)


def low_rows(low_in, refs):
    return jnp.concatenate([dot_nt(low_in, ref[...]) for ref in refs], axis=1)


def whole(arrays):
    return [full(array.shape) for array in arrays]


def row_count(arrays):
    return sum(array.shape[0] for array in arrays)


def stacked(refs):
    return jnp.concatenate([w[s] for w in refs for s in range(w.shape[0])], axis=0)


def rotated(values, cosine, sine_table):
    first = values[:, :HALF]
    second = values[:, HALF:]
    return jnp.concatenate(
        [first * cosine - second * sine_table, second * cosine + first * sine_table], axis=1
    )


def unrotated(values, cosine, sine_table):
    first = values[:, :HALF]
    second = values[:, HALF:]
    return jnp.concatenate(
        [first * cosine + second * sine_table, second * cosine - first * sine_table], axis=1
    )


def norm_kernel(x, gain, out):
    rows = x[...].astype(F32)
    inverse = lax.rsqrt(jnp.mean(rows * rows, axis=1, keepdims=True) + rms_epsilon)
    out[...] = (rows * inverse * gain[...]).astype(BF)


def norm_rows(x, gain):
    return pl.pallas_call(
        norm_kernel,
        out_shape=far(x.shape, BF),
        compiler_params=pltpu.CompilerParams(vmem_limit_bytes=24 << 20),
        name="norm_rows",
    )(x, gain)


def piece_specs(pieces, width):
    return [
        pl.BlockSpec((w.shape[0], w.shape[1], width), lambda n: (0, 0, n)) for w in pieces
    ]


def project_kernel(layout, ids, chunks, low_in, low_out, *refs):
    parts, count, lengths, turn = layout
    if turn:
        (cosine, sine_table), refs = refs[:2], refs[2:]
    act, refs = refs[:parts], refs[parts:]
    groups = len(lengths)
    pieces, outs = refs[:groups * count], refs[groups * count:]
    if turn:
        low = outs[-1]

        @pl.when(pl.program_id(0) == 0)
        def _():
            low[...] = low_rows(low_in[...], act).astype(BF)
    else:
        low = low_in
    n = pl.program_id(0)
    begin = 0
    for i, length in enumerate(lengths):

        @pl.when((n >= begin) & (n < begin + length))
        def _(i=i, length=length):
            made = dot(columns(act, ids), stacked(pieces[i * count:(i + 1) * count]))
            made = made + dot_tn(low[...], low_out[...])
            if i > 0 or not turn:
                outs[i][...] = made.astype(BF)
                return
            scale = jnp.where(n >= length // 2, 1.0 / KEY_DIM**0.5, 1.0)
            size = made.shape[0] // chunks.shape[0]
            for j in range(chunks.shape[0]):
                at = aligned(chunks[j] * size, size)
                rows = slice(j * size, (j + 1) * size)
                turned = rotated(made[rows], cosine[at, :], sine_table[at, :])
                outs[i][rows, :] = (scale * turned).astype(BF)

        begin += length


def project(ids, chunks, act, low_in, low_out, weights, turn):
    rows, depth = row_count(act), act[0].shape[1]
    block = KEY_DIM
    lengths = tuple(w[0].shape[2] // block for w in weights)
    begins = [sum(lengths[:i]) for i in range(len(lengths))]

    def at(group):
        return lambda n: jnp.clip(n - begins[group], 0, lengths[group] - 1)

    pieces = [
        pl.BlockSpec((w.shape[0], w.shape[1], block), lambda n, at=at(i): (0, 0, at(n)))
        for i, weight in enumerate(weights) for w in weight
    ]
    outs = [pl.BlockSpec((rows, block), lambda n, at=at(i): (0, at(n))) for i in range(len(weights))]
    shapes = [far((rows, length * block), BF) for length in lengths]
    ranks = low_in.shape[0]
    if turn:
        outs.append(full((ranks, rows)))
        shapes.append(jax.ShapeDtypeStruct((ranks, rows), BF))
    return pl.pallas_call(
        partial(project_kernel, (len(act), len(weights[0]), lengths, bool(turn))),
        grid=(sum(lengths),),
        in_specs=[smem(), smem(), full(low_in.shape),
                  pl.BlockSpec((ranks, block), lambda n: (0, n))]
        + whole(turn) + whole(act) + pieces,
        out_specs=outs,
        out_shape=shapes,
        compiler_params=params(48),
        cost_estimate=estimate(0, 0),
        name="project",
    )(ids, chunks, low_in, low_out, *turn, *in_hbm(*act, *[w for x in weights for w in x]))


def decay_factors(rate, size):
    down = lax.broadcasted_iota(jnp.int32, (size, 1), 0).astype(F32)
    across = lax.broadcasted_iota(jnp.int32, (1, size), 1).astype(F32)
    return down, across


def retention_kernel(spots, rates, seg_col, seg_row, q, k, v, gate, out, nrm, inverse):
    rate = rates[pl.program_id(0)]
    count = spots.shape[0]
    size = q.shape[0] // count
    down, across = decay_factors(rate, size)
    row_factor = jnp.exp(rate * down)
    for i in range(count):
        here = aligned(spots[i] * size, size)
        query = q[here, :]
        seg_here = seg_col[i * size:(i + 1) * size, :]
        total = jnp.zeros((size, v.shape[1]), F32)
        for j in range(i + 1):
            there = aligned(spots[j] * size, size)
            column_factor = jnp.exp(rate * ((i - j) * size - across))
            alive = seg_here == seg_row[:, j * size:(j + 1) * size]
            if i == j:
                alive = alive & (down >= across)
            scores = dot_nt(query, k[there, :])
            mixed = jnp.where(alive, scores * row_factor * column_factor, 0.0).astype(BF)
            total = total + dot(mixed, v[there, :])
        centered = total - jnp.mean(total, axis=1, keepdims=True)
        scale = lax.rsqrt(jnp.mean(centered * centered, axis=1, keepdims=True) + group_floor)
        normed = centered * scale
        level = gate[here, :].astype(F32)
        out[here, :] = (level / (1.0 + jnp.exp(-level)) * normed).astype(BF)
        nrm[here, :] = normed.astype(nrm.dtype)
        inverse[0, here, :] = jnp.broadcast_to(scale, (size, 128))


def retention(spots, rates, seg_col, seg_row, qk, v, gate):
    rows = qk.shape[0]
    heads = v.shape[1] // VALUE_DIM
    return pl.pallas_call(
        retention_kernel,
        grid=(heads,),
        in_specs=[smem(), smem(), full(seg_col.shape), full(seg_row.shape),
                  pl.BlockSpec((rows, KEY_DIM), lambda h: (0, h)),
                  pl.BlockSpec((rows, KEY_DIM), lambda h: (0, h + heads)),
                  pl.BlockSpec((rows, VALUE_DIM), lambda h: (0, h)),
                  pl.BlockSpec((rows, VALUE_DIM), lambda h: (0, h))],
        out_specs=[pl.BlockSpec((rows, VALUE_DIM), lambda h: (0, h)),
                   pl.BlockSpec((rows, VALUE_DIM), lambda h: (0, h)),
                   pl.BlockSpec((1, rows, 128), lambda h: (h, 0, 0))],
        out_shape=[far(v.shape, BF), far(v.shape, BF),
                   far((heads, rows, 128), F32)],
        compiler_params=params(40),
        cost_estimate=estimate(2 * rows * rows * 768 * heads, 30 << 20),
        name="retention",
    )(spots, rates, seg_col, seg_row, qk, qk, *in_hbm(v, gate))


def fold_kernel(ids, act, low_in, low_out, *refs):
    pieces, (outs, low) = refs[:-5], (refs[-5:-1], refs[-1])
    step = pl.program_id(0)
    subs = pl.num_programs(0)
    width = pieces[0].shape[2]
    size = outs[0].shape[0]

    @pl.when(step == 0)
    def _():
        low[...] = dot_nt(low_in[...], act[...])

    extra = low[...].astype(BF)
    rows = act[...]
    for i, piece in enumerate(pieces):
        at = aligned(ids[i * subs + step] * width, width)
        product = (dot(rows, piece[0]) + dot_tn(extra, low_out[:, at])).astype(BF)
        for j, out in enumerate(outs):
            out[:, at] = product[j * size:(j + 1) * size]


def fold(ids, act, low_in, low_out, pieces):
    rows, depth = act.shape
    subs = pieces[0].shape[0]
    width = low_out.shape[1]
    return pl.pallas_call(
        fold_kernel,
        grid=(subs,),
        in_specs=[smem(), full(act.shape), full(low_in.shape), full(low_out.shape)]
        + [pl.BlockSpec((1,) + w.shape[1:], lambda s: (s, 0, 0)) for w in pieces],
        out_specs=[full((rows // 4, width))] * 4 + [full((low_in.shape[0], rows))],
        out_shape=[far((rows // 4, width), BF)] * 4
        + [jax.ShapeDtypeStruct((low_in.shape[0], rows), F32)],
        compiler_params=params(48),
        cost_estimate=estimate(2 * rows * depth * width, 2 * depth * width + 4 * rows * depth),
        name="fold",
    )(ids, act, low_in, low_out, *pieces)


def join_kernel(x, part0, part1, part2, gain, middle, normed):
    rows = x[...].astype(F32) + (
        part0[...].astype(F32) + part1[...].astype(F32) + part2[...].astype(F32)
    )
    inverse = lax.rsqrt(jnp.mean(rows * rows, axis=1, keepdims=True) + rms_epsilon)
    middle[...] = rows.astype(BF)
    normed[...] = (rows * inverse * gain[...]).astype(BF)


def join_rows(x, parts, gain):
    return pl.pallas_call(
        join_kernel,
        out_shape=[jax.ShapeDtypeStruct(x.shape, BF), jax.ShapeDtypeStruct(x.shape, BF)],
        compiler_params=pltpu.CompilerParams(vmem_limit_bytes=24 << 20),
        name="join_rows",
    )(x, *parts, gain)


def rms_back_kernel(rows_in, grad_in, part0, part1, part2, gain, *outs):
    rows = rows_in[...].astype(F32)
    inverse = lax.rsqrt(jnp.mean(rows * rows, axis=1, keepdims=True) + rms_epsilon)
    normed = rows * inverse
    scaled = gain[...] * (
        part0[...].astype(F32) + part1[...].astype(F32) + part2[...].astype(F32)
    )
    result = grad_in[...].astype(F32) + inverse * (
        scaled - normed * jnp.mean(scaled * normed, axis=1, keepdims=True)
    )
    for out in outs:
        out[...] = result.astype(out.dtype)


def rms_back(rows_in, grad_in, parts, gain, kinds):
    count, width = rows_in.shape
    block = pl.BlockSpec((count // 2, width), lambda i: (i, 0))
    return pl.pallas_call(
        rms_back_kernel,
        grid=(2,),
        in_specs=[block] * 5 + [full(gain.shape)],
        out_specs=[block] * len(kinds),
        out_shape=[far((count, width), kind) for kind in kinds],
        compiler_params=params(24),
        name="rms_back",
    )(rows_in, grad_in, *parts, gain)


def hidden_grad_kernel(parts, ids, low_back, low_in, *refs):
    act, pieces, (out, low) = refs[:parts], refs[parts:-2], refs[-2:]

    @pl.when(pl.program_id(0) == 0)
    def _():
        low[...] = low_rows(low_back[...], act).astype(BF)

    weights = jnp.concatenate([w[s] for w in pieces for s in range(w.shape[0])], axis=1)
    out[...] = (dot_nt(columns(act, ids), weights) + dot_tn(low[...], low_in[...])).astype(BF)


def hidden_grad(ids, act, low_back, low_in, pieces):
    rows, depth = row_count(act), act[0].shape[1]
    width = pieces[0].shape[1]
    block = 256
    return pl.pallas_call(
        partial(hidden_grad_kernel, len(act)),
        grid=(width // block,),
        in_specs=[smem(), full(low_back.shape),
                  pl.BlockSpec((low_in.shape[0], block), lambda n: (0, n))]
        + whole(act) + [pl.BlockSpec((w.shape[0], block, w.shape[2]), lambda n: (0, n, 0)) for w in pieces],
        out_specs=[pl.BlockSpec((rows, block), lambda n: (0, n)),
                   full((low_back.shape[0], rows))],
        out_shape=[far((rows, width), BF),
                   jax.ShapeDtypeStruct((low_back.shape[0], rows), BF)],
        compiler_params=params(40),
        cost_estimate=estimate(2 * rows * depth * width, 2 * depth * width + 8 * rows * depth),
        name="hidden_grad",
    )(ids, low_back, low_in, *act, *pieces)


def mlp_begin_kernel(parts, count, ids, low_in, *refs):
    act, refs = refs[:parts], refs[parts:]
    gate_pieces, up_pieces = refs[:count], refs[count:2 * count]
    gate, up, low = refs[2 * count:]

    @pl.when(pl.program_id(0) == 0)
    def _():
        low[...] = low_rows(low_in[...], act).astype(BF)

    rows = columns(act, ids, 0, sum(w.shape[0] for w in gate_pieces))
    gate[...] = dot(rows, stacked(gate_pieces))
    up[...] = dot(rows, stacked(up_pieces))


def mlp_begin(ids, act, low_in, gate_pieces, up_pieces):
    rows, depth = row_count(act), act[0].shape[1]
    width = gate_pieces[0].shape[2]
    block = 256
    ranks = low_in.shape[0]
    column = pl.BlockSpec((rows, block), lambda n: (0, n))
    return pl.pallas_call(
        partial(mlp_begin_kernel, len(act), len(gate_pieces)),
        grid=(width // block,),
        in_specs=[smem(), full(low_in.shape)] + whole(act) + piece_specs(gate_pieces, block)
        + piece_specs(up_pieces, block),
        out_specs=[column, column, full((ranks, rows))],
        out_shape=[far((rows, width), F32)] * 2 + [jax.ShapeDtypeStruct((ranks, rows), BF)],
        compiler_params=params(48),
        cost_estimate=estimate(0, 0),
        name="mlp_begin",
    )(ids, low_in, *act, *gate_pieces, *up_pieces)


def mlp_kernel(parts, count, ids, gate_in, up_in, low, gate_out, up_out, down_in, grad, grad_low,
               *refs):
    act, refs = refs[:parts], refs[parts:]
    gate_pieces, up_pieces = refs[:count], refs[count:2 * count]
    hid, dgate, dup, lows, grad_hidden, grad_down = refs[2 * count:]

    @pl.when(pl.program_id(0) == 0)
    def _():
        lows[...] = jnp.zeros(lows.shape, F32)

    extra = low[...]
    gate = gate_in[...] + dot_tn(extra, gate_out[...])
    up = up_in[...] + dot_tn(extra, up_out[...])
    if count:
        last = sum(w.shape[0] for w in gate_pieces)
        rows = columns(act, ids, ids.shape[0] - last)
        gate = gate + dot(rows, stacked(gate_pieces))
        up = up + dot(rows, stacked(up_pieces))
    chance = 0.5 * (1.0 + lax.erf(gate * (0.5**0.5)))
    active = gate * chance
    slope = chance + gate * (jnp.exp(-0.5 * gate * gate) * 0.3989422804014327)
    hidden = (active * up).astype(BF)
    back = grad[...].astype(F32)
    back_gate = (back * up * slope).astype(BF)
    back_up = (back * active).astype(BF)
    hid[...] = hidden
    dgate[...] = back_gate
    dup[...] = back_up
    lows[:RANK, :] += dot_nt(down_in[...], hidden)
    lows[RANK:, :] += dot_nt(gate_out[...], back_gate) + dot_nt(up_out[...], back_up)
    grad_hidden[:RANK, :] = dot(extra[:RANK], back_gate).astype(BF)
    grad_hidden[RANK:, :] = dot(extra[RANK:], back_up).astype(BF)
    grad_down[...] = dot(grad_low[...], hidden).astype(BF)


def mlp(ids, begun, act, gate_out, up_out, down_in, grad, grad_low, gate_pieces, up_pieces):
    gate_in, up_in, low = begun
    rows, width = gate_in.shape
    block = 256
    ranks = low.shape[0]
    column = lambda height: pl.BlockSpec((height, block), lambda n: (0, n))
    return pl.pallas_call(
        partial(mlp_kernel, len(act), len(gate_pieces)),
        grid=(width // block,),
        in_specs=[smem(), column(rows), column(rows), full(low.shape), column(ranks),
                  column(ranks), column(down_in.shape[0]), column(rows), full(grad_low.shape)]
        + whole(act) + piece_specs(gate_pieces, block) + piece_specs(up_pieces, block),
        out_specs=[column(rows), column(rows), column(rows), full((ranks + RANK, rows)),
                   column(ranks), column(grad_low.shape[0])],
        out_shape=[jax.ShapeDtypeStruct((rows, width), BF)] * 3
        + [jax.ShapeDtypeStruct((ranks + RANK, rows), F32),
           jax.ShapeDtypeStruct((ranks, width), BF),
           jax.ShapeDtypeStruct((grad_low.shape[0], width), BF)],
        compiler_params=params(48),
        cost_estimate=estimate(0, 0),
        name="mlp",
    )(ids, gate_in, up_in, low, gate_out, up_out, down_in, grad, grad_low, *act, *gate_pieces,
      *up_pieces)


def unfold_kernel(layout, ids, low_in, *refs):
    blocks, count, weights = layout
    lows, refs = refs[:blocks], refs[blocks:]
    acts, pieces, outs = refs[:blocks * count], refs[blocks * count:-blocks], refs[-blocks:]
    size = outs[0].shape[0]
    step = pl.program_id(0)
    subs = pl.num_programs(0)
    width = pieces[0].shape[1]
    extra = jnp.concatenate([low[...] for low in lows], axis=1).T.astype(BF)
    per = len(pieces) // weights
    rows = jnp.concatenate(
        [jnp.concatenate([act[...] for act in acts[i * count:(i + 1) * count]], axis=1)
         for i in range(blocks)], axis=0
    )
    for i in range(per):
        at = aligned(ids[i * subs + step] * width, width)
        weight = jnp.concatenate([pieces[k * per + i][0] for k in range(weights)], axis=1)
        product = (dot_nt(rows, weight) + dot(extra, low_in[:, at])).astype(BF)
        for j, out in enumerate(outs):
            out[:, at] = product[j * size:(j + 1) * size]


def unfold(ids, acts, low, low_in, weights, size, blocks):
    subs = weights[0][0].shape[0]
    width = low_in.shape[1]
    pieces = [piece for weight in weights for piece in weight]
    count = len(blocks)
    chosen = []
    for at in blocks:
        for act in acts:
            if isinstance(act, tuple):
                per = act[0].shape[0] // size
                chosen.append((act[at // per], at % per))
            else:
                chosen.append((act, at))
    depth = sum(act.shape[1] for act, _ in chosen) // count
    return pl.pallas_call(
        partial(unfold_kernel, (count, len(acts), len(weights))),
        grid=(subs,),
        in_specs=[smem(), full(low_in.shape)]
        + [pl.BlockSpec((low.shape[0], size), lambda s, at=at: (0, at)) for at in blocks]
        + [pl.BlockSpec((size, act.shape[1]), lambda s, at=at: (at, 0)) for act, at in chosen]
        + [pl.BlockSpec((1,) + w.shape[1:], lambda s: (s, 0, 0)) for w in pieces],
        out_specs=[full((size, width))] * count,
        out_shape=[jax.ShapeDtypeStruct((size, width), BF)] * count,
        compiler_params=params(48),
        cost_estimate=estimate(
            2 * count * size * depth * width, 2 * depth * width + 4 * count * size * depth
        ),
        name="unfold",
    )(ids, low_in, *[low] * count, *in_hbm(*[act for act, _ in chosen], *pieces))


def gate_back_kernel(parts, ids, low_back, low_in, gate, nrm, inverse, hold, low_gate, low_out,
                     begin_in, begin_gate, *refs):
    act, pieces = refs[:parts], refs[parts:-6]
    dgate, dret, low, dlow, grad_in, grad_gate = refs[-6:]

    @pl.when(pl.program_id(0) == 0)
    def _():
        low[...] = low_rows(low_back[...], act).astype(BF)
        dlow[...] = jnp.zeros(dlow.shape, F32)

    weights = jnp.concatenate([w[s] for w in pieces for s in range(w.shape[0])], axis=1)
    back = dot_nt(columns(act, ids), weights) + dot_tn(low[...], low_in[...])
    level = gate[...].astype(F32)
    normed = nrm[...].astype(F32)
    chance = 1.0 / (1.0 + jnp.exp(-level))
    slope = chance * (1.0 + level * (1.0 - chance))
    back_gate = (back * normed * slope).astype(BF)
    grad = back * (level * chance)
    mean = jnp.mean(grad, axis=1, keepdims=True)
    along = jnp.mean(grad * normed, axis=1, keepdims=True)
    dgate[...] = back_gate
    dret[...] = (inverse[0, :, :1] * (grad - mean - normed * along)).astype(BF)
    grad_in[...] = begin_in[...] + dot(low[...], hold[...])
    grad_gate[...] = begin_gate[...] + dot(low_gate[...], back_gate)
    dlow[...] += dot_nt(low_out[...], back_gate)


def gate_back(ids, act, low_back, low_in, gate, nrm, inverse, hold, low_gate, low_out, pieces,
              half, begin_in, begin_gate):
    if len(act) > 1:
        act = act[len(act) // 2 * half:len(act) // 2 * (half + 1)]
    rows, depth = gate.shape[0] // 2, act[0].shape[1]
    width = gate.shape[1]
    block = VALUE_DIM
    ranks = low_back.shape[0]
    if len(act) == 1:
        acts = [pl.BlockSpec((rows, depth), lambda n: (half, 0))]
    else:
        acts = whole(act)
    column = lambda height: pl.BlockSpec((height, block), lambda n: (0, n))
    place = pl.BlockSpec((rows, block), lambda n: (half, n))
    return pl.pallas_call(
        partial(gate_back_kernel, len(act)),
        grid=(width // block,),
        in_specs=[smem(), full(low_back.shape), column(ranks), place, place,
                  pl.BlockSpec((1, rows, 128), lambda n: (n, half, 0)), place,
                  pl.BlockSpec((ranks, rows), lambda n: (low_gate.shape[0] // ranks - 1, half)),
                  column(low_out.shape[0]), column(ranks), column(ranks)]
        + acts + [pl.BlockSpec((w.shape[0], block, w.shape[2]), lambda n: (0, n, 0))
                  for w in pieces],
        out_specs=[column(rows), column(rows), full((ranks, rows)),
                   full((low_out.shape[0], rows)), column(ranks), column(ranks)],
        out_shape=[jax.ShapeDtypeStruct((rows, width), BF)] * 2
        + [jax.ShapeDtypeStruct((ranks, rows), BF),
           jax.ShapeDtypeStruct((low_out.shape[0], rows), F32),
           jax.ShapeDtypeStruct((ranks, width), F32), jax.ShapeDtypeStruct((ranks, width), F32)],
        compiler_params=params(56),
        cost_estimate=estimate(2 * rows * depth * width, 2 * depth * width + 16 * rows * width),
        name="gate_back",
    )(ids, low_back, low_in, *in_hbm(gate, nrm, inverse, hold), low_gate, low_out, begin_in,
      begin_gate, *act, *pieces)


def retention_back_kernel(spots, rates, seg_col, seg_row, cosine, sine_table, low, begin, q_out,
                          k_out, v_out, q, k, v, dret0, dret1, dq, dk, dv, dlow, grad_q, grad_k,
                          grad_v, sums):
    head = pl.program_id(0)
    rate = rates[head]
    count = spots.shape[0]
    size = q.shape[0] // count
    down, across = decay_factors(rate, size)
    column_factor = jnp.exp(rate * across)
    key_scale = 1.0 / KEY_DIM**0.5

    @pl.when(head == 0)
    def _():
        dlow[...] = begin[...]

    sums[...] = jnp.zeros(sums.shape, F32)
    for j in range(count):
        there = aligned(spots[j] * size, size)
        place = slice(j * size, (j + 1) * size)
        key, value = k[there, :], v[there, :]
        seg_there = seg_col[place, :]
        key_sum = jnp.zeros((size, KEY_DIM), F32)
        value_sum = jnp.zeros((size, VALUE_DIM), F32)
        for i in range(j, count):
            here = aligned(spots[i] * size, size)
            query = q[here, :]
            within = aligned(spots[i] % (count // 2) * size, size)
            back = jnp.where(spots[i] < count // 2, dret0[within, :], dret1[within, :])
            row_factor = jnp.exp(rate * ((i - j) * size - down))
            alive = seg_there == seg_row[:, i * size:(i + 1) * size]
            if i == j:
                alive = alive & (across >= down)
            weight = jnp.where(alive, row_factor * column_factor, 0.0)
            mixed = (dot_nt(key, query) * weight).astype(BF)
            grad = (dot_nt(value, back) * weight).astype(BF)
            value_sum = value_sum + dot(mixed, back)
            key_sum = key_sum + dot(grad, query)
            sums[i * size:(i + 1) * size, :] += dot_tn(grad, key)
        dk[there, :] = (
            key_scale * unrotated(key_sum, cosine[place, :], sine_table[place, :])
        ).astype(BF)
        dv[there, :] = value_sum.astype(BF)
    for i in range(count):
        place = slice(i * size, (i + 1) * size)
        dq[aligned(spots[i] * size, size), :] = unrotated(
            sums[place, :], cosine[place, :], sine_table[place, :]
        ).astype(BF)
    back_q, back_k, back_v = dq[...], dk[...], dv[...]
    dlow[...] += (
        dot_nt(q_out[...], back_q) + dot_nt(k_out[...], back_k) + dot_nt(v_out[...], back_v)
    )
    grad_q[...] = dot(low[:RANK, :], back_q).astype(BF)
    grad_k[...] = dot(low[RANK:2 * RANK, :], back_k).astype(BF)
    grad_v[...] = dot(low[2 * RANK:3 * RANK, :], back_v).astype(BF)


def retention_back(spots, rates, seg_col, seg_row, cosine, sine_table, low, begin, qk_out, v_out,
                   qk, v, dret0, dret1):
    rows = qk.shape[0]
    heads = v.shape[1] // VALUE_DIM
    ranks = low.shape[0]
    key = lambda height: pl.BlockSpec((height, KEY_DIM), lambda h: (0, h))
    later = lambda height: pl.BlockSpec((height, KEY_DIM), lambda h: (0, h + heads))
    value = lambda height: pl.BlockSpec((height, VALUE_DIM), lambda h: (0, h))
    keys = heads * KEY_DIM
    return pl.pallas_call(
        retention_back_kernel,
        grid=(heads,),
        in_specs=[smem(), smem(), full(seg_col.shape), full(seg_row.shape), full(cosine.shape),
                  full(cosine.shape), full(low.shape), full(begin.shape), key(ranks),
                  later(ranks), value(ranks),
                  key(rows), later(rows), value(rows), value(rows // 2), value(rows // 2)],
        out_specs=[key(rows), key(rows), value(rows), full((ranks, rows)), key(RANK), key(RANK),
                   value(RANK)],
        out_shape=[jax.ShapeDtypeStruct((rows, keys), BF), jax.ShapeDtypeStruct((rows, keys), BF),
                   jax.ShapeDtypeStruct(v.shape, BF), jax.ShapeDtypeStruct((ranks, rows), F32),
                   jax.ShapeDtypeStruct((RANK, keys), BF), jax.ShapeDtypeStruct((RANK, keys), BF),
                   jax.ShapeDtypeStruct((RANK, v.shape[1]), BF)],
        scratch_shapes=[pltpu.VMEM((rows, KEY_DIM), F32)],
        compiler_params=params(48),
        cost_estimate=estimate(2 * rows * rows * 1792 * heads, 30 << 20),
        name="retention_back",
    )(spots, rates, seg_col, seg_row,
      cosine, sine_table, low, begin, qk_out, qk_out, v_out, qk, qk, v, dret0, dret1)


def share_kernel(heights, low, *refs):
    out = refs[-1]
    at, first = 0, 0
    for height, parts in heights:
        total = jnp.zeros((height, out.shape[2]), F32)
        begin = 0
        for ref in refs[first:first + parts]:
            end = begin + ref.shape[0]
            total = total + dot(low[at:at + height, begin:end], ref[...])
            begin = end
        out[0, at:at + height, :] = total.astype(BF)
        at, first = at + height, first + parts


def share(low, span, items):
    acts = [array for _, act in items for array in act]
    heights = tuple((height, len(act)) for height, act in items)
    count = acts[0].shape[1] // span
    made = pl.pallas_call(
        partial(share_kernel, heights),
        grid=(count,),
        in_specs=[full(low.shape)]
        + [pl.BlockSpec((act.shape[0], span), lambda i: (0, i)) for act in acts],
        out_specs=pl.BlockSpec((1, low.shape[0], span), lambda i: (i, 0, 0)),
        out_shape=jax.ShapeDtypeStruct((count, low.shape[0], span), BF),
        compiler_params=params(32),
        cost_estimate=estimate(0, 0),
        name="share",
    )(low, *in_hbm(*acts))
    return made.reshape(count * low.shape[0], span)


def place_kernel(layout, arrays, order, *refs):
    packs, outs = refs[:arrays], refs[arrays:]
    pack = packs[0][0]
    if arrays == 2:
        which = order[pl.program_id(0)] >= order[pl.num_programs(0)]
        pack = jnp.where(which, packs[1][0], pack)
    span = pack.shape[1]
    for (begin, height, kind, stride), out in zip(layout, outs):
        if kind == "shares":
            for j in range(out.shape[2] // span):
                rows = pack[begin + stride * j:begin + stride * j + height]
                out[0, :, j * span:(j + 1) * span] = rows.astype(F32)
            continue
        for j in range(2):
            rows = pack[begin + stride * j:begin + stride * j + height].astype(F32)
            if kind == "halves":
                out[0, :, j * span:(j + 1) * span] = rows
            else:
                out[0, j] = rows


def place(order, arrays, layout, shares):
    entries = order.shape[0]
    size, _, span = arrays[0].shape
    shapes = []
    for _, height, kind, _ in layout:
        shapes.append({"shares": (height, shares * span),
                       "halves": (height, 2 * span)}.get(kind, (2, height, span)))

    def spec(number):
        def index(e, o):
            return (jnp.clip(o[e] - number * size, 0, size - 1), 0, 0)
        return pl.BlockSpec((1,) + arrays[0].shape[1:], index)

    order = jnp.concatenate([order, jnp.full((1,), size, jnp.int32)])
    return pl.pallas_call(
        partial(place_kernel, layout, len(arrays)),
        grid_spec=pltpu.PrefetchScalarGridSpec(
            num_scalar_prefetch=1,
            grid=(entries,),
            in_specs=[spec(number) for number in range(len(arrays))],
            out_specs=[
                pl.BlockSpec((1,) + shape, lambda e, o, n=len(shape): (e,) + (0,) * n)
                for shape in shapes
            ],
        ),
        out_shape=[jax.ShapeDtypeStruct((entries,) + shape, F32) for shape in shapes],
        compiler_params=params(32),
        cost_estimate=estimate(0, 10 << 20),
        name="place",
    )(order, *in_hbm(*arrays))


def after(x, *others):
    return lax.optimization_barrier((x,) + others)[0]


class PlainLinks:
    def __init__(self, ndp, nt):
        self.ndp, self.nt = ndp, nt
        self.rank = lax.axis_index("tensor")
        self.chunks = jnp.arange(nt, dtype=jnp.int32)
        self.spots = self.chunks
        self.row_ids = jnp.zeros((1,), jnp.int32)

    def exchange(self, x):
        return x

    def mine(self, own, other):
        return own

    def gather(self, x):
        return [lax.all_gather(x, "tensor", axis=0, tiled=True)]

    def scatter(self, rows):
        total = lax.psum_scatter(
            jnp.concatenate(rows, axis=0), "tensor", scatter_dimension=0, tiled=True
        )
        zero = jnp.zeros_like(total)
        return (total, zero, zero)

    def forward(self, shards, tokens, cotangent, line, steps):
        steps.rotation()
        blocks = [
            [lax.all_gather(shard, "dp", axis=int(shard.shape[1] * self.ndp == tokens.shape[1]),
                            tiled=True)[None]]
            for shard in shards
        ]
        steps.ready(line, steps.tables(line, line)[0])
        a = self.gather(steps.norm(tokens))
        dy = self.gather(cotangent)
        projected = steps.project(a, blocks[1], blocks[0])
        mixed = steps.mix(a, *projected, blocks[2])
        *rows, low = steps.fold(mixed[0], blocks[3])
        middle, b = steps.join(tokens, self.scatter(rows))
        b = self.gather(b)
        begun = steps.mlp_begin(b, blocks[5], blocks[6])
        dhid = (*steps.hidden_grad(dy, blocks[4]), begun, ([], []))
        return blocks, tokens, a, cotangent, dy, projected, mixed, low, middle, b, dhid

    def group_sum(self, x):
        return lax.psum(x.astype(BF), "tensor")

    def backward(self, steps):
        steps.mlp()
        dz = self.gather(steps.dz(self.scatter(steps.unfold_mlp(256, (0, 1, 2, 3)))))
        output = steps.output(self.scatter(steps.fold_down(steps.hid)))
        early = lax.all_gather(steps.early(self.group_sum(steps.lows)), "dp")
        early = steps.place_early([early], jnp.arange(self.ndp, dtype=jnp.int32))
        steps.gate_back(dz, 0)
        steps.gate_back(dz, 1)
        steps.retention_back(*steps.dret)
        late = lax.all_gather(steps.late(self.group_sum(steps.late_lows()), dz), "dp")
        late = steps.place_late([late], jnp.arange(self.ndp, dtype=jnp.int32))
        parts = self.scatter(steps.unfold_attn(256, (0, 1, 2, 3)))
        dx, _ = steps.dx(parts)
        return output, dx, early, late


class PairedLinks:
    def __init__(self, ndp, nt):
        self.ndp, self.nt = ndp, nt
        d, t = lax.axis_index("dp"), lax.axis_index("tensor")
        c, p, m = d % 2, t // 2, t % 2
        self.home = c == p
        self.rank = 2 * c + m
        flips = jnp.array([0, 2, 1, 3], jnp.int32)
        self.chunks = self.rank ^ flips
        order = jnp.arange(4, dtype=jnp.int32) ^ self.rank
        self.spots = (order % 2) * 2 + order // 2
        g = d // 2
        self.row_ids = ((2 * (g ^ jnp.arange(4, dtype=jnp.int32))[:, None]
                         + jnp.arange(2, dtype=jnp.int32)[None, :]) ^ c).reshape(-1)
        self.last = {}
        self.last_round = ()
        self.slow = ()

    def pairs(self, place):
        listed = []
        for d in range(self.ndp):
            for t in range(self.nt):
                to = place(d, t)
                if to is not None:
                    listed.append((d * self.nt + t, to[0] * self.nt + to[1]))
        return listed

    def move(self, x, place, chain=None):
        if chain in self.last:
            x = after(x, *self.last[chain])
        moved = lax.ppermute(x, ("dp", "tensor"), self.pairs(place))
        if chain is not None:
            self.last[chain] = (moved,)
        return moved

    def send(self, moves):
        return [lax.ppermute(x, ("dp", "tensor"), self.pairs(place)) for x, place in moves]

    def round(self, moves, work=None, inputs=(), later=(), slow=(), feed=0):
        every = list(moves) + list(slow)
        values = [x for x, _ in every]
        flat, form = jax.tree.flatten((values, inputs))
        last, _ = jax.tree.flatten(self.last_round)
        if last:
            flat = lax.optimization_barrier((*flat, *last))[:len(flat)]
        values, inputs = jax.tree.unflatten(form, flat)
        moved = self.send([(x, place) for x, (_, place) in zip(values, every)])
        moved, slowly = moved[:len(moves)], moved[len(moves):]
        second = []
        if later:
            count, make = later
            moves = make(moved[:count])
            values = [x for x, _ in moves]
            values = lax.optimization_barrier((*values, *moved[:count]))[:len(values)]
            second = self.send([(x, place) for x, (_, place) in zip(values, moves)])
        made = work(*moved[:feed], *inputs) if work is not None else ()
        self.last_round = (moved, second, made, self.slow)
        self.slow = slowly
        return moved + slowly, second, made

    def core(self, x):
        return self.move(x, lambda d, t: (d ^ 1, t))

    def pair(self, x):
        return self.move(x, lambda d, t: (d, t ^ 1), "pair")

    def mine(self, own, other):
        return jnp.where(self.home, own, other)

    def exchange(self, x):
        moved = self.move(
            x, lambda d, t: (d ^ 1, t ^ 2) if d % 2 != t // 2 else None, "middle"
        )
        return jnp.where(self.home, x, moved)

    def gather(self, x):
        across = self.pair(x)
        return [x, self.core(x), across, self.core(across)]

    def forward(self, shards, tokens, cotangent, line, steps):
        by_one = lambda d, t: (d ^ 2, t)
        by_two = lambda d, t: (d ^ 4, t)
        core = lambda d, t: (d ^ 1, t)
        pair = lambda d, t: (d, t ^ 1)
        swap = lambda d, t: (d ^ 1, t ^ 2) if d % 2 != t // 2 else None
        seat = lambda d, t: (d, t ^ 2) if d % 2 == t // 2 else None
        blocks = [[None] * 4 for _ in shards]
        doubled = [jnp.stack([shards[0], self.core(shards[0])])]

        def over(i):
            return (doubled[i], seat)

        def arrived(i, moved):
            blocks[i][0] = self.mine(doubled[i], moved)

        hops = {
            "x": lambda i: (blocks[i][0], by_one),
            "y": lambda i: (blocks[i][0], by_two),
            "xy": lambda i: (blocks[i][1], by_two),
            "yx": lambda i: (blocks[i][2], by_one),
        }
        place_of = {"x": 1, "y": 2, "xy": 3, "yx": 3}

        def go(first, second, others, work=None, inputs=()):
            def later(moved):
                for (i, way), block in zip(first, moved):
                    blocks[i][place_of[way]] = block
                return [hops[way](i) for i, way in second]

            moved, seconds, made = self.round(
                [hops[way](i) for i, way in first] + list(others), work, inputs,
                (len(first), later)
            )
            for (i, way), block in zip(second, seconds):
                blocks[i][place_of[way]] = block
            return moved[len(first):], made

        def double(rest):
            return [jnp.stack([shard, self.core(shard)]) for shard in rest]

        other = self.core(line)
        def begin(rest):
            return double(rest), steps.rotation()

        (moved,), (made, turn) = go([], [], [over(0)], begin, (shards[1:],))
        steps.turn = turn
        doubled += made
        arrived(0, moved)
        (moved,), (home_table, sent_table) = go(
            [(0, "x"), (0, "y")], [], [over(1)], steps.tables, (line, other)
        )
        arrived(1, moved)
        (x, table, moved), _ = go([(1, "x"), (0, "xy")], [(1, "y")],
                                  [(tokens, swap), (sent_table, seat), over(2)])
        arrived(2, moved)
        x = self.mine(tokens, x)
        steps.ready(other, self.mine(home_table, table))
        a = steps.norm(x)
        (across, moved, grad), _ = go([(2, "x"), (2, "y")], [(1, "yx"), (2, "xy")],
                                      [(a, pair), over(3), (cotangent, swap)])
        arrived(3, moved)
        grad = self.mine(cotangent, grad)
        def attend(near, beyond, own, across, *weights):
            a = [own, near, across, beyond]
            return a, steps.project(a, *weights[::-1])

        moves = [(a, core), (across, core), hops["x"](3), hops["y"](3), over(4)]
        moved, _, (a, projected) = self.round(
            moves, attend, (a, across, *blocks[:2]), feed=2
        )
        _, _, blocks[3][1], blocks[3][2], moved = moved
        arrived(4, moved)
        half = grad.shape[0] // 2
        (moved, across0), mixed = go(
            [(4, "x"), (3, "xy")], [], [over(5), (grad[:half], pair)], steps.mix,
            (a, *projected, blocks[2])
        )
        arrived(5, moved)
        (moved, across1), folded = go(
            [(5, "x"), (4, "y")], [], [over(6), (grad[half:], pair)], steps.fold,
            (mixed[0], blocks[3])
        )
        across = jnp.concatenate([across0, across1])
        arrived(6, moved)
        own, near, far, beyond, low = folded
        moves = [(near, core), (beyond, core), hops["yx"](4), hops["y"](5)]
        moved, (far,), _ = self.round(
            moves, later=(2, lambda moved: [(self.add(far, moved[1]), pair)])
        )
        near, _, blocks[4][3], blocks[5][2] = moved
        middle, b = steps.join(x, (own, near, far))
        (far, near_grad, beyond_grad), _ = go([(6, "x"), (6, "y")], [],
                                              [(b, pair), (grad, core), (across, core)])
        dy = [grad, near_grad, across, beyond_grad]

        def beside(near, beyond, own, across, dy, w_d, *weights):
            rows = [own, near, across, beyond]
            return steps.hidden_grad(dy, w_d), rows, steps.mlp_begin(rows, *weights)

        moves = [(b, core), (far, core), hops["yx"](5), hops["xy"](6)]
        moved, _, (dhid, b, begun) = self.round(
            moves, beside, (b, far, dy, blocks[4], blocks[5][:3], blocks[6][:3]), feed=2
        )
        blocks[5][3], blocks[6][3] = moved[2:]
        dhid = (*dhid, begun, (blocks[5][3:], blocks[6][3:]))
        return blocks, x, a, grad, dy, projected, mixed, low, middle, b, dhid

    def add(self, one, two):
        return (one.astype(F32) + two.astype(F32)).astype(BF)

    def core_sum(self, x, other):
        size = x.shape[1] // 4
        other = other.astype(F32)
        return (x + jnp.concatenate(
            [other[:, i * size:(i + 1) * size] for i in (1, 0, 3, 2)], axis=1
        )).astype(BF)

    def pair_sum(self, x, other):
        size = x.shape[1] // 2
        other = jnp.concatenate([other[:, size:], other[:, :size]], axis=1)
        return (x.astype(F32) + other.astype(F32)).astype(BF)

    def both_halves(self, halves, one, two):
        return jnp.concatenate(
            [jnp.concatenate([halves[0], one]),
             jnp.concatenate([halves[1][:1], two[:1], halves[1][1:], two[1:]])], axis=1
        )

    def backward(self, steps):
        pair = lambda d, t: (d, t ^ 1)
        swap = lambda d, t: (d ^ 1, t ^ 2) if d % 2 != t // 2 else None
        by_one = lambda d, t: (d ^ 2, t)
        by_two = lambda d, t: (d ^ 4, t)
        core = lambda d, t: (d ^ 1, t)

        self.last_round = ()
        steps.mlp()
        (lows,), _, (near, far, beyond) = self.round(
            [(steps.lows.astype(BF), core)],
            lambda dup: steps.unfold_mlp(256, (1, 2, 3), dup), (steps.dup,)
        )
        lows = self.core_sum(steps.lows, lows)
        (beyond, near), _, _ = self.round([(beyond, core), (near, core)])
        far = self.add(far, beyond)
        half = far.shape[0] // 2
        (far, other), _, ((own,), folded) = self.round(
            [(far, pair), (lows, pair)],
            lambda dup, hid: (steps.unfold_mlp(256, (0,), dup), steps.fold_down(hid)),
            (steps.dup, steps.hid)
        )
        own_out, near_out, far_out, beyond_out = folded
        dz = steps.dz((own, near, far))


        def beside(beyond, dz_near, far, dz, lows, other):
            return (self.add(far, beyond), steps.gate_back([dz, dz_near, dz, dz], 0),
                    steps.early(self.pair_sum(lows, other)))

        (_, dz_near, across, near_out), _, (far_out, dret0, early) = self.round(
            [(beyond_out, core), (dz, core), (dz, pair), (near_out, core)],
            beside, (far_out, dz, lows, other), feed=2
        )
        (dz_beyond,), _, _ = self.round([(across, core)])
        (moved, far_out), _, dret1 = self.round(
            [(early, swap)],
            lambda across, beyond: steps.gate_back([across, across, across, beyond], 1),
            (across, dz_beyond), slow=[(far_out, pair)]
        )
        early = self.mine(early, moved)
        size = early.shape[0] // 2
        early = [early[:size][None], early[size:][None]]
        (one, two), _, dpv = self.round(
            [(early[0], by_one), (early[1], by_two)], steps.retention_back, (dret0, dret1)
        )
        early = [jnp.concatenate([early[0], one]), jnp.concatenate([early[1], two])]
        dz = [dz, dz_near, across, dz_beyond]

        (dlow,), _, output = self.round(
            [(steps.late_lows().astype(BF), core)], lambda *parts: steps.output(parts),
            (own_out, near_out, far_out)
        )
        dlow = self.core_sum(steps.late_lows(), dlow)
        (other, moved_out, one, two), _, (own, near, far, beyond) = self.round(
            [(dlow, pair), (output, swap), (early[0], by_two), (early[1], by_one)],
            lambda dpv: steps.unfold_attn(256, (0, 1, 2, 3), dpv), (dpv,)
        )
        (beyond, near), _, late = self.round(
            [(beyond, core), (near, core)],
            lambda dlow, other: steps.late(self.pair_sum(dlow, other), dz), (dlow, other)
        )
        (moved,), _, (far, early) = self.round(
            [(late, swap)],
            lambda far, beyond, *early: (self.add(far, beyond), self.both_halves(*early)),
            (far, beyond, early, one, two)
        )
        late = self.mine(late, moved)
        size = late.shape[0] // 2
        late = [late[:size][None], late[size:][None]]
        (one, two, far0), _, _ = self.round(
            [(late[0], by_one), (late[1], by_two), (far[:half], pair)]
        )
        late = [jnp.concatenate([late[0], one]), jnp.concatenate([late[1], two])]
        (one, two, far1), _, _ = self.round(
            [(late[0], by_two), (late[1], by_one), (far[half:], pair)]
        )
        dx, low = steps.dx((own, near, jnp.concatenate([far0, far1])))
        late = self.both_halves(late, one, two)
        apart = jnp.arange(self.ndp, dtype=jnp.int32) ^ lax.axis_index("dp")

        def put(early_other, other, early, late):
            at = apart // 2 + 4 * (apart % 2)
            early = steps.place_early([early, early_other], at)
            return early, steps.place_late([late, other], at)

        (_, _, moved), _, (early, late) = self.round(
            [(early, core), (late, core), (low, swap)], put, (early, late), feed=2
        )
        moved, early, late = lax.optimization_barrier((moved, early, late))
        return (self.mine(output, moved_out),
                self.mine(dx, moved.astype(F32)), early, late)


def rotation_tables(seq_length, half_dim):
    positions = jnp.arange(seq_length, dtype=jnp.float32)
    frequency = jnp.exp(-jnp.log(10000.0) * jnp.arange(half_dim, dtype=jnp.float32) / half_dim)
    angles = positions[:, None] * frequency[None, :]
    return (jnp.cos(angles), jnp.sin(angles))


def shards(
    ndp,
    nt,
    tokens,
    cotangent,
    adapter_ids,
    segments,
    norm_attn,
    norm_mlp,
    weight_query,
    weight_key,
    weight_value,
    weight_gate,
    weight_out,
    weight_mlp_gate,
    weight_mlp_up,
    weight_mlp_down,
    adapt_attn_in,
    adapt_query_key,
    adapt_value_gate,
    adapt_out_in,
    adapt_out_back,
    adapt_mlp_in,
    adapt_mlp_hidden,
    adapt_down_in,
    adapt_down_back,
):
    links = PairedLinks(ndp, nt) if (ndp, nt) == (8, 4) else PlainLinks(ndp, nt)
    rank, chunks, spots, ids = links.rank, links.chunks, links.spots, links.row_ids
    adapters = adapt_attn_in.shape[0]
    depth = tokens.shape[2]
    seq_length = segments.shape[1]
    gain_attn, gain_mlp = norm_attn[None], norm_mlp[None]

    def pick(table, which):
        return lax.dynamic_index_in_dim(table, which, 0, keepdims=False)

    def packed(which):
        qk, vg = pick(adapt_query_key, which), pick(adapt_value_gate, which)
        return jnp.concatenate(
            [jnp.concatenate([qk[0], qk[1]], axis=1), vg[0], vg[1],
             pick(adapt_mlp_hidden, which).reshape(2 * RANK, -1),
             pick(adapt_out_in, which).T, pick(adapt_down_in, which).T], axis=0
        )

    own_id = adapter_ids[0, 0]
    own_line = jnp.concatenate([segments, jnp.broadcast_to(adapter_ids, (1, 128))], axis=1)
    wide = weight_gate.shape[1]
    keys = adapt_query_key.shape[3]
    heads_local = wide // VALUE_DIM
    head_ids = (rank * heads_local + jnp.arange(heads_local, dtype=jnp.int32)).astype(F32)
    rates = jnp.log(1.0 - jnp.exp2(-5.0 - head_ids))
    class Steps:
        def tables(self, line, other):
            return packed(line[0, seq_length]), packed(other[0, seq_length])

        def ready(self, other, table):
            line = links.mine(own_line, other)
            self.work_id = work_id = line[0, seq_length]
            self.seg_row = line[:, :seq_length]
            self.seg_col = self.seg_row.reshape(seq_length, 1)
            blank = jnp.zeros((RANK, wide), BF)
            left = jnp.arange(wide)[None, :] < keys
            zero = jnp.zeros((), BF)
            self.qk_out = jnp.concatenate([jnp.where(left, table[:RANK], zero),
                                           jnp.where(left, zero, table[:RANK]), blank, blank])
            self.v_out = jnp.concatenate([blank, blank, table[RANK:2 * RANK], blank])
            self.g_out = jnp.concatenate([blank, blank, blank, table[2 * RANK:3 * RANK]])
            self.mg_out = jnp.concatenate([table[3 * RANK:4 * RANK], blank])
            self.mu_out = jnp.concatenate([blank, table[4 * RANK:5 * RANK]])
            self.out_in = table[5 * RANK:6 * RANK]
            self.down_in = table[6 * RANK:7 * RANK]
            self.attn_in = pick(adapt_attn_in, work_id).T
            self.out_back = pick(adapt_out_back, work_id)
            self.mlp_in = pick(adapt_mlp_in, work_id).T
            self.down_back = pick(adapt_down_back, work_id)

        def rotation(self):
            self.turn = rotation_tables(seq_length, HALF)
            return self.turn

        def norm(self, x):
            return norm_rows(x, gain_attn)

        def project(self, a, w_qk, w_v):
            return project(
                ids, chunks, a, self.attn_in, jnp.concatenate([self.qk_out, self.v_out], axis=1),
                (w_qk, w_v), self.turn
            )

        def mix(self, a, qk, v, low, w_g):
            gate, = project(ids, chunks, a, low, self.g_out, (w_g,), ())
            return (*retention(spots, rates, self.seg_col, self.seg_row, qk, v, gate), gate)

        def fold(self, o, w_o):
            return fold(ids, o, self.out_in, self.out_back, w_o)

        def join(self, x, parts):
            return join_rows(x, parts, gain_mlp)

        def mlp_begin(self, b, w_mg, w_mu):
            return mlp_begin(ids, b, self.mlp_in, w_mg, w_mu)

        def hidden_grad(self, dy, w_d):
            return hidden_grad(ids, dy, self.down_back, self.down_in, w_d)

    steps = Steps()
    ((w_v, w_qk, w_g, w_o, w_d, w_mg, w_mu), x, a, grad, dy, (qk, v, low_a),
     (o, nrm, inverse, gate), low_o, middle, b, (dhid, low_dy, begun, late_weights)) = links.forward(
        [weight_value, jnp.concatenate([weight_query, weight_key], axis=1), weight_gate,
         weight_out, weight_mlp_down, weight_mlp_gate, weight_mlp_up],
        tokens[0], cotangent[0], own_line, steps,
    )
    seg_row, seg_col, work_id = steps.seg_row, steps.seg_col, steps.work_id
    qk_out, v_out, g_out, mg_out, mu_out = (
        steps.qk_out, steps.v_out, steps.g_out, steps.mg_out, steps.mu_out
    )
    attn_in, out_in, out_back = steps.attn_in, steps.out_in, steps.out_back
    mlp_in, down_in, down_back = steps.mlp_in, steps.down_in, steps.down_back

    span = depth // nt
    halves = lambda y: jnp.concatenate([y[:, :wide // 2], y[:, wide // 2:]])

    class Back:
        early_height = 3 * RANK
        late_height = 5 * RANK

        def mlp(self):
            (self.hid, self.dgate, self.dup, self.lows, self.grad_hidden,
             self.grad_down) = mlp(
                ids, begun, b, mg_out, mu_out, down_in, dhid, low_dy, *late_weights
            )

        def unfold_mlp(self, size, blocks, dup=None):
            dup = self.dup if dup is None else dup
            return unfold(ids, (self.dgate, dup), self.lows[RANK:], mlp_in, (w_mg, w_mu),
                          size, blocks)

        def dz(self, parts):
            self.dmid, = rms_back(middle, grad, parts, gain_mlp, (BF,))
            return self.dmid

        def fold_down(self, hid):
            return fold(ids, hid, down_in, down_back, w_d)[:4]

        def output(self, parts):
            return (middle.astype(F32) + (
                parts[0].astype(F32) + parts[1].astype(F32) + parts[2].astype(F32)
            )).astype(BF)

        def early(self, lows):
            mark = jnp.full((RANK, span), work_id, F32).astype(BF)
            return jnp.concatenate(
                [share(lows, span, ((RANK, dy), (2 * RANK, b))),
                 halves(jnp.concatenate([self.grad_hidden, self.grad_down])), mark]
            )

        def gate_back(self, dz, half):
            if half == 0:
                self.grad_out_in = self.grad_gate = jnp.zeros((RANK, wide), F32)
                self.dpg, self.dret, self.low_parts = (), (), ()
            dpg, dret, _, dlow, self.grad_out_in, self.grad_gate = gate_back(
                ids, dz, out_back, out_in, gate, nrm, inverse, o, low_a, g_out, w_o, half,
                self.grad_out_in, self.grad_gate
            )
            self.dpg, self.dret = self.dpg + (dpg,), self.dret + (dret,)
            self.low_parts = self.low_parts + (dlow,)
            return dret

        def late_lows(self):
            return jnp.concatenate([self.dlow, low_o])

        def retention_back(self, *dret):
            (self.dpq, self.dpk, self.dpv, self.dlow, self.grad_q, self.grad_k,
             self.grad_v) = retention_back(
                spots, rates, seg_col, seg_row, *steps.turn, low_a,
                jnp.concatenate(self.low_parts, axis=1), qk_out, v_out, qk, v, *dret
            )
            return self.dpv

        def late(self, lows, dz):
            return jnp.concatenate(
                [share(lows, span, ((4 * RANK, a), (RANK, dz))),
                 halves(jnp.concatenate(
                     [jnp.concatenate([self.grad_q, self.grad_k], axis=1), self.grad_v,
                      self.grad_gate.astype(BF), self.grad_out_in.astype(BF)]
                 ))]
            )

        def unfold_attn(self, size, blocks, dpv=None):
            dpv = self.dpv if dpv is None else dpv
            return unfold(ids, (self.dpq, self.dpk, dpv, self.dpg), self.dlow, attn_in,
                          (w_qk, w_v, w_g), size, blocks)

        def dx(self, parts):
            return rms_back(x, self.dmid, parts, gain_attn, (F32, BF))

        def place_early(self, arrays, at):
            sequences = sum(array.shape[0] for array in arrays)
            shares = nt * self.early_height
            marks = [array[:, shares + 6 * RANK, 0] for array in arrays]
            all_ids = jnp.concatenate(marks).astype(jnp.int32)[at]
            numbers = jnp.arange(adapters, dtype=jnp.int32)
            chosen = numbers[:, None] == all_ids[None, :]
            if sequences == adapters:
                self.order = jnp.sum(jnp.where(chosen, numbers[None, :], 0), axis=1)
                self.total = None
            else:
                self.order = numbers
                self.total = lambda y: jnp.einsum(
                    "es,sij->eij", chosen.astype(BF), y, preferred_element_type=F32
                )
                arrays, at = [self.total(arrays[0])], numbers
            pitch = self.early_height
            return place(
                at[self.order], arrays,
                ((0, RANK, "shares", pitch), (RANK, 2 * RANK, "shares", pitch),
                 (shares, 2 * RANK, "halves", 3 * RANK),
                 (shares + 2 * RANK, RANK, "halves", 3 * RANK)), nt
            )

        def place_late(self, arrays, at):
            if self.total is not None:
                arrays, at = [self.total(arrays[0])], self.order
            pitch = self.late_height
            shares = nt * pitch
            return place(
                at[self.order], arrays,
                ((0, 4 * RANK, "shares", pitch), (4 * RANK, RANK, "shares", pitch),
                 (shares, RANK, "two", 4 * RANK), (shares + RANK, 2 * RANK, "halves", 4 * RANK),
                 (shares + 3 * RANK, RANK, "halves", 4 * RANK)), nt
            )

    output, input_grad, early, late = links.backward(Back())
    down_back_out, mlp_out, hidden_out, down_out = early
    attn_out, out_back_out, qk_grads, vg_grads, out_out = late
    return (
        output[None],
        input_grad[None],
        jnp.swapaxes(attn_out, 1, 2),
        qk_grads,
        vg_grads.reshape(adapters, 2, RANK, wide),
        jnp.swapaxes(out_out, 1, 2),
        out_back_out,
        jnp.swapaxes(mlp_out, 1, 2),
        hidden_out.reshape(adapters, 2, RANK, wide),
        jnp.swapaxes(down_out, 1, 2),
        down_back_out,
    )


def solution(mesh):
    in_specs = (
        P("dp", "tensor", None),
        P("dp", "tensor", None),
        P("dp", None),
        P("dp", None),
        P(),
        P(),
        P("dp", "tensor"),
        P("dp", "tensor"),
        P("dp", "tensor"),
        P("dp", "tensor"),
        P("tensor", "dp"),
        P("dp", "tensor"),
        P("dp", "tensor"),
        P("tensor", "dp"),
        P(),
        P(None, None, None, "tensor"),
        P(None, None, None, "tensor"),
        P(None, "tensor", None),
        P(),
        P(),
        P(None, None, None, "tensor"),
        P(None, "tensor", None),
        P(),
    )
    out_specs = (
        P("dp", "tensor", None),
        P("dp", "tensor", None),
        P(),
        P(None, None, None, "tensor"),
        P(None, None, None, "tensor"),
        P(None, "tensor", None),
        P(),
        P(),
        P(None, None, None, "tensor"),
        P(None, "tensor", None),
        P(),
    )
    local = partial(shards, mesh.shape["dp"], mesh.shape["tensor"])
    return jax.shard_map(local, mesh=mesh, in_specs=in_specs, out_specs=out_specs, check_vma=False)
```
